32 devices in a mesh: dp: 4 (over x, core), fsdp: 8 (over z, y).
Axes of the slice: x: 2, y: 2, z: 4, core: 2. Of those that a mesh axis runs over, the one named last changes fastest.
Arguments:
- slot_states: bfloat16 [64, 288, 768], P(('dp', 'fsdp')), may hold values from -6 to 6
- answer_tags: int32 [64, 288], P(('dp', 'fsdp')), may hold values 0 or 1
- slot_mask: int32 [8, 8], replicated, may hold values from 0 to 1, as said below
- retrieval: float32 [8, 8], replicated, may hold values from -4 to 4
- query_emb: bfloat16 [8, 768], P(None, ('dp', 'fsdp')), may hold values from -0.21875 to 0.21875
- qkv_weight: bfloat16 [768, 2304], P(('dp', 'fsdp')), may hold values from -0.21875 to 0.21875
- qkv_bias: bfloat16 [1536], P(('dp', 'fsdp')), may hold values from -1.5 to 1.5
- out_weight: bfloat16 [768, 768], P(('dp', 'fsdp')), may hold values from -0.875 to 0.875
- out_bias: bfloat16 [768], P(('dp', 'fsdp')), may hold values from -1.5 to 1.5
- attn_gain: bfloat16 [768], P(('dp', 'fsdp')), may hold values from 0.5 to 1.5
- attn_shift: bfloat16 [768], P(('dp', 'fsdp')), may hold values from -1.5 to 1.5
- up_weight: bfloat16 [768, 3072], P(('dp', 'fsdp')), may hold values from -0.21875 to 0.21875
- up_bias: bfloat16 [3072], P(('dp', 'fsdp')), may hold values from -1.5 to 1.5
- down_weight: bfloat16 [3072, 768], P(('dp', 'fsdp')), may hold values from -0.109375 to 0.109375
- down_bias: bfloat16 [768], P(('dp', 'fsdp')), may hold values from -1.5 to 1.5
- ffn_gain: bfloat16 [768], P(('dp', 'fsdp')), may hold values from 0.5 to 1.5
- ffn_shift: bfloat16 [768], P(('dp', 'fsdp')), may hold values from -1.5 to 1.5
Outputs:
- mixed_out: bfloat16 [64, 288, 768], P(('dp', 'fsdp'))
- loss: float32 [], replicated
- states_grad: bfloat16 [64, 288, 768], P(('dp', 'fsdp'))
- query_grad: float32 [8, 768], P(None, ('dp', 'fsdp'))
- qkv_weight_grad: float32 [768, 2304], P(('dp', 'fsdp'))
- qkv_bias_grad: float32 [1536], P(('dp', 'fsdp'))
- out_weight_grad: float32 [768, 768], P(('dp', 'fsdp'))
- out_bias_grad: float32 [768], P(('dp', 'fsdp'))
- attn_gain_grad: float32 [768], P(('dp', 'fsdp'))
- attn_shift_grad: float32 [768], P(('dp', 'fsdp'))
- up_weight_grad: float32 [768, 3072], P(('dp', 'fsdp'))
- up_bias_grad: float32 [3072], P(('dp', 'fsdp'))
- down_weight_grad: float32 [3072, 768], P(('dp', 'fsdp'))
- down_bias_grad: float32 [768], P(('dp', 'fsdp'))
- ffn_gain_grad: float32 [768], P(('dp', 'fsdp'))
- ffn_shift_grad: float32 [768], P(('dp', 'fsdp'))
The draws below stay inside these ranges and needn't reach their ends.
Inputs may be any that keep to these rules, and one draw needn't show every extreme that they name: `slot_mask`: each row holds 4 to 8 ones and 48 ones lie in the whole array; some row has 8 and some row has 4.
All inputs are finite; a program needn't handle non-finite values. No bound on the sum of `answer_tags` on one device may be relied on, other than what follows from the above.
Results may differ from the reference program's by a relative error of at most 0.01.
Values may be sent and summed in bfloat16 or wider, within the bound.
No kernel may reach another device: no remote copies, remote signals or barrier semaphores. Data moves between devices by JAX's collectives and lax.ppermute only.
A program may use at most 192 MiB of HBM per device.

```python
import math
import jax
import jax.numpy as jnp
from jax import lax

D = 768
HEADS = 12
HEAD = 64
FF = 3072
SLOT_LEN = 288
SLOTS = 8
SLOT_DEV = 2
BUFFERS = 64
VALID = 48
QUERIES = 8
DEVICES = 32


def draw_slot_mask(key, part):
    key = jax.random.fold_in(key, 11)
    key_pair, key_ticket, key_place = jax.random.split(key, 3)
    query_ids = jnp.arange(QUERIES, dtype=jnp.int32)
    query_order = jax.random.permutation(key_pair, QUERIES)
    fullest = query_order[0]
    sparsest = query_order[1]
    special = (query_ids == fullest) | (query_ids == sparsest)
    ticket_owner = jnp.arange(QUERIES * 4, dtype=jnp.int32) // 4
    ticket_rank = jax.random.permutation(key_ticket, QUERIES * 4).astype(jnp.int32)
    ticket_rank = jnp.where(special[ticket_owner], ticket_rank + QUERIES * 4, ticket_rank)
    ticket_order = jnp.argsort(jnp.argsort(ticket_rank, stable=True), stable=True)
    chosen = (ticket_order < VALID - 4 * QUERIES - 4).astype(jnp.int32)
    counts = 4 + jnp.sum(chosen.reshape(QUERIES, 4), axis=1) + 4 * (query_ids == fullest).astype(jnp.int32)
    slot_noise = jax.random.randint(key_place, (QUERIES, SLOTS), 0, 1 << 20) * SLOTS + jnp.arange(SLOTS, dtype=jnp.int32)[None, :]
    slot_order = jnp.argsort(jnp.argsort(slot_noise, axis=1, stable=True), axis=1, stable=True)
    return (slot_order < counts[:, None]).astype(jnp.int32)


def place_ends(drawn, key, smallest, high):
    extent = drawn.shape
    place = [jax.random.randint(jax.random.fold_in(key, axis), (), 0, extent[axis]) for axis in range(len(extent))]
    drawn = drawn.at[tuple(place)].set(smallest)
    longest = extent.index(max(extent))
    place[longest] = (place[longest] + 1) % extent[longest]
    return drawn.at[tuple(place)].set(high)


def level_of(key, shape, shards, least, top_value):
    loudness, own = 1.0, jax.random.fold_in(key, 6)
    for dim, parts in shards:
        steps = jnp.exp(jax.random.uniform(jax.random.fold_in(own, dim), (parts,), jnp.float32, least / len(shards), top_value / len(shards)))
        loudness = loudness * jnp.repeat(steps, shape[dim] // parts).reshape([-1 if axis == dim else 1 for axis in range(len(shape))])
    return loudness


def noise(stream_key, shape, scale, limit, cuts=(), kind=jnp.bfloat16):
    values = scale * jax.random.normal(stream_key, shape, jnp.float32)
    if cuts:
        values = values * level_of(stream_key, shape, cuts, -0.22, 0.18)
    return jnp.clip(values, -limit, limit).astype(kind)


def setup_inputs(seed: int = 0) -> dict:
    key_of = jax.random.split(jax.random.key(seed), 18)
    slot_states = noise(key_of[0], (BUFFERS, SLOT_LEN, D), 1.0, 6.0, ((0, 32),))
    answer_tags = place_ends((jax.random.randint(key_of[1], (BUFFERS, SLOT_LEN), 0, 4) < 1).astype(jnp.int32), jax.random.fold_in(key_of[1], 1), 0, 1)
    slot_mask = draw_slot_mask(jax.random.fold_in(key_of[17], 71), 0)
    retrieval = noise(key_of[3], (QUERIES, SLOTS), 1.0, 4.0, (), jnp.float32)
    query_emb = noise(key_of[4], (QUERIES, D), D ** -0.5, 0.21875, ((1, 32),))
    qkv_weight = noise(key_of[5], (D, 3 * D), D ** -0.5, 0.21875, ((0, 32),))
    qkv_bias = noise(key_of[6], (2 * D,), 0.3, 1.5, ((0, 32),))
    out_weight = noise(key_of[7], (D, D), (D // 16) ** -0.5, 0.875, ((0, 32),))
    out_bias = noise(key_of[8], (D,), 0.3, 1.5, ((0, 32),))
    attn_gain = jnp.clip(1.0 + 0.1 * jax.random.normal(key_of[9], (D,), jnp.float32), 0.5, 1.5).astype(jnp.bfloat16)
    attn_shift = noise(key_of[10], (D,), 0.3, 1.5, ((0, 32),))
    up_weight = noise(key_of[11], (D, FF), D ** -0.5, 0.21875, ((0, 32),))
    up_bias = noise(key_of[12], (FF,), 0.3, 1.5, ((0, 32),))
    down_weight = noise(key_of[13], (FF, D), FF ** -0.5, 0.109375, ((0, 32),))
    down_bias = noise(key_of[14], (D,), 0.3, 1.5, ((0, 32),))
    ffn_gain = jnp.clip(1.0 + 0.1 * jax.random.normal(key_of[15], (D,), jnp.float32), 0.5, 1.5).astype(jnp.bfloat16)
    ffn_shift = noise(key_of[16], (D,), 0.3, 1.5, ((0, 32),))
    return dict(slot_states=slot_states, answer_tags=answer_tags, slot_mask=slot_mask, retrieval=retrieval, query_emb=query_emb, qkv_weight=qkv_weight, qkv_bias=qkv_bias, out_weight=out_weight, out_bias=out_bias, attn_gain=attn_gain, attn_shift=attn_shift, up_weight=up_weight, up_bias=up_bias, down_weight=down_weight, down_bias=down_bias, ffn_gain=ffn_gain, ffn_shift=ffn_shift)


@jax.custom_vjp
def low(v):
    return lax.optimization_barrier(v.astype(jnp.bfloat16)).astype(jnp.float32)

@jax.custom_vjp
def low_back(v):
    return v

def low_keep(v):
    return (low(v), None)

def low_pass(kept, grad):
    return (grad,)

def back_keep(v):
    return (v, None)

def back_low(kept, grad):
    return (low(grad),)
low.defvjp(low_keep, low_pass)
low_back.defvjp(back_keep, back_low)
eps_norm = 1e-12
loss_scale = 65536.0
highest = lax.Precision.HIGHEST

def norm_rows(residual, norm_gain, norm_shift):
    center = residual - lax.optimization_barrier(jnp.mean(residual, axis=-1, keepdims=True))
    spread = lax.optimization_barrier(jnp.mean(center * center, axis=-1, keepdims=True))
    return center * lax.rsqrt(spread + eps_norm) * norm_gain + norm_shift

def buffer_places(slot_mask):
    running = jnp.cumsum(slot_mask.reshape(-1), dtype=jnp.int32)
    buffer_ids = jnp.arange(BUFFERS, dtype=jnp.int32)
    slot_ranks = buffer_ids % SLOT_DEV * DEVICES + buffer_ids // SLOT_DEV
    return lax.optimization_barrier(jnp.sum((running[None, :] <= slot_ranks[:, None]).astype(jnp.int32), axis=1, dtype=jnp.int32))

def block_forward(weights, states, labels, chosen):
    qkv_weight, qkv_bias, out_weight, out_bias, attn_gain, attn_shift, up_weight, up_bias, down_weight, down_bias, ffn_gain, ffn_shift = weights
    model_width = states.shape[-1]
    bias_full = jnp.concatenate([qkv_bias[:model_width], jnp.zeros((model_width,), jnp.float32), qkv_bias[model_width:]])
    pre_proj = low_back(jnp.einsum('bld,de->ble', states, qkv_weight, precision=highest) + bias_full)
    qkv_low = low(pre_proj)
    head_shape = states.shape[:2] + (HEADS, HEAD)
    query_heads = qkv_low[..., :model_width].reshape(head_shape)
    key_heads = qkv_low[..., model_width:2 * model_width].reshape(head_shape)
    value_heads = qkv_low[..., 2 * model_width:].reshape(head_shape)
    score_scale = 1.0 / math.sqrt(HEAD)
    raw_scores = low_back(jnp.einsum('bqhd,bkhd->bhqk', query_heads, key_heads, precision=highest) * score_scale)
    attn_soft = low(jax.nn.softmax(raw_scores, axis=-1))
    context = low(low_back(jnp.einsum('bhqk,bkhd->bqhd', attn_soft, value_heads, precision=highest))).reshape(states.shape)
    attn_out = low_back(jnp.einsum('bld,de->ble', context, out_weight, precision=highest) + out_bias)
    hidden = low(norm_rows(states + attn_out, attn_gain, attn_shift))
    up_proj = low_back(jnp.einsum('bld,df->blf', hidden, up_weight, precision=highest) + up_bias)
    act_low = low(jax.nn.gelu(up_proj, approximate=False))
    down_proj = low_back(jnp.einsum('blf,fd->bld', act_low, down_weight, precision=highest) + down_bias)
    out_low = low(norm_rows(hidden + down_proj, ffn_gain, ffn_shift))
    logits = jnp.einsum('bld,bd->bl', out_low, chosen, precision=highest)
    likelihood = lax.optimization_barrier(jnp.mean(labels * jax.nn.log_sigmoid(logits) + (1.0 - labels) * jax.nn.log_sigmoid(-logits), axis=-1))
    return (out_low, likelihood)

def reference(slot_states, answer_tags, slot_mask, retrieval, query_emb, qkv_weight, qkv_bias, out_weight, out_bias, attn_gain, attn_shift, up_weight, up_bias, down_weight, down_bias, ffn_gain, ffn_shift):
    places = buffer_places(slot_mask)
    slot_pick = places[:, None] == jnp.arange(QUERIES * SLOTS, dtype=jnp.int32)[None, :]
    owner_mask = (places // SLOTS)[:, None] == jnp.arange(QUERIES, dtype=jnp.int32)[None, :]
    owner_float = owner_mask.astype(jnp.float32)
    prior_score = lax.optimization_barrier(jnp.sum(jnp.where(slot_pick, retrieval.reshape(-1)[None, :], 0.0), axis=1))
    labels = answer_tags.astype(jnp.float32)
    group_size = math.gcd(BUFFERS, 8)
    params = tuple((tensor.astype(jnp.float32) for tensor in (qkv_weight, qkv_bias, out_weight, out_bias, attn_gain, attn_shift, up_weight, up_bias, down_weight, down_bias, ffn_gain, ffn_shift)))

    def objective(states, query_table, weights):
        chosen = jnp.dot(owner_float, query_table, precision=highest)

        def run_group(group_data):
            return block_forward(weights, group_data[0], group_data[1], group_data[2])
        outputs, likelihood = lax.map(jax.checkpoint(run_group), (states.reshape(-1, group_size, SLOT_LEN, D), labels.reshape(-1, group_size, SLOT_LEN), chosen.reshape(-1, group_size, D)))
        scores = likelihood.reshape(-1) + prior_score
        totals = jax.nn.logsumexp(jnp.where(owner_mask, scores[:, None], -1e+30), axis=0, where=owner_mask)
        return (outputs.reshape(states.shape), -loss_scale * jnp.sum(totals))
    (mixed_out, scaled), pullback = jax.vjp(objective, slot_states.astype(jnp.float32), query_emb.astype(jnp.float32), params)
    grad_states, grad_query, grad_weights = pullback((jnp.zeros_like(mixed_out), jnp.ones_like(scaled)))
    return (mixed_out.astype(jnp.bfloat16), (scaled / loss_scale).astype(jnp.float32), grad_states.astype(jnp.bfloat16), grad_query.astype(jnp.float32), grad_weights[0].astype(jnp.float32), grad_weights[1].astype(jnp.float32), grad_weights[2].astype(jnp.float32), grad_weights[3].astype(jnp.float32), grad_weights[4].astype(jnp.float32), grad_weights[5].astype(jnp.float32), grad_weights[6].astype(jnp.float32), grad_weights[7].astype(jnp.float32), grad_weights[8].astype(jnp.float32), grad_weights[9].astype(jnp.float32), grad_weights[10].astype(jnp.float32), grad_weights[11].astype(jnp.float32))
```

```python
import functools
import math

import jax
import jax.numpy as jnp
import numpy as np
from jax import lax
from jax.experimental import pallas as pl
from jax.experimental.pallas import tpu as pltpu
from jax.sharding import PartitionSpec as P

HEAD = 64


eps_norm = 1e-12
loss_scale = 65536.0
neg_fill = -1e30
highest = lax.Precision.HIGHEST


def norm_forward(residual, norm_gain, norm_shift):
    center = residual - jnp.mean(residual, axis=-1, keepdims=True)
    spread = jnp.mean(center * center, axis=-1, keepdims=True)
    inverse = lax.rsqrt(spread + eps_norm)
    normed = center * inverse
    return (normed * norm_gain + norm_shift, normed, inverse)


def norm_backward(grad_out, normed, inverse):
    mean_grad = jnp.mean(grad_out, axis=-1, keepdims=True)
    mean_cross = jnp.mean(grad_out * normed, axis=-1, keepdims=True)
    return inverse * (grad_out - mean_grad - normed * mean_cross)


def merge_parts(first, second):
    peak = jnp.maximum(first[0], second[0])
    return (peak, first[1] * jnp.exp(first[0] - peak) + second[1] * jnp.exp(second[0] - peak))


def gelu_exact(values):
    return jax.nn.gelu(values, approximate=False)


def layer_forward(params, slot_states):
    (
        qkv_weight,
        qkv_bias,
        out_weight,
        out_bias,
        attn_gain,
        attn_shift,
        up_weight,
        up_bias,
        down_weight,
        down_bias,
        ffn_gain,
        ffn_shift,
    ) = params
    model_width = slot_states.shape[-1]
    bias_float = qkv_bias.astype(jnp.float32)
    bias_full = jnp.concatenate(
        [bias_float[:model_width], jnp.zeros((model_width,), jnp.float32), bias_float[model_width:]]
    )
    pre_proj = (
        jnp.einsum("bld,de->ble", slot_states, qkv_weight, preferred_element_type=jnp.float32)
        + bias_full
    )
    qkv_low = pre_proj.astype(jnp.bfloat16)
    head_shape = slot_states.shape[:2] + (model_width // HEAD, HEAD)
    query_heads = qkv_low[..., :model_width].reshape(head_shape)
    key_heads = qkv_low[..., model_width : 2 * model_width].reshape(head_shape)
    value_heads = qkv_low[..., 2 * model_width :].reshape(head_shape)
    score_scale = 1.0 / math.sqrt(HEAD)
    raw_scores = (
        jnp.einsum("bqhd,bkhd->bhqk", query_heads, key_heads, preferred_element_type=jnp.float32)
        * score_scale
    )
    row_peak = jnp.max(raw_scores, axis=-1, keepdims=True)
    exp_scores = jnp.exp(raw_scores - row_peak)
    attn_soft = exp_scores / jnp.sum(exp_scores, axis=-1, keepdims=True)
    soft_low = attn_soft.astype(jnp.bfloat16)
    context = (
        jnp.einsum("bhqk,bkhd->bqhd", soft_low, value_heads, preferred_element_type=jnp.float32)
        .astype(jnp.bfloat16)
        .reshape(slot_states.shape)
    )
    attn_out = jnp.einsum(
        "bld,de->ble", context, out_weight, preferred_element_type=jnp.float32
    ) + out_bias.astype(jnp.float32)
    hidden, normed_attn, inverse_attn = norm_forward(
        slot_states.astype(jnp.float32) + attn_out,
        attn_gain.astype(jnp.float32),
        attn_shift.astype(jnp.float32),
    )
    hidden_low = hidden.astype(jnp.bfloat16)
    up_proj = jnp.einsum(
        "bld,df->blf", hidden_low, up_weight, preferred_element_type=jnp.float32
    ) + up_bias.astype(jnp.float32)
    act_low = gelu_exact(up_proj).astype(jnp.bfloat16)
    down_proj = jnp.einsum(
        "blf,fd->bld", act_low, down_weight, preferred_element_type=jnp.float32
    ) + down_bias.astype(jnp.float32)
    mixed, normed_ffn, inverse_ffn = norm_forward(
        hidden_low.astype(jnp.float32) + down_proj,
        ffn_gain.astype(jnp.float32),
        ffn_shift.astype(jnp.float32),
    )
    return (
        query_heads,
        key_heads,
        value_heads,
        attn_soft,
        soft_low,
        context,
        hidden_low,
        normed_attn,
        inverse_attn,
        up_proj,
        act_low,
        normed_ffn,
        inverse_ffn,
        mixed.astype(jnp.bfloat16),
    )

AXES = ("dp", "fsdp")
X_BIT, CORE_BIT, Z_FAR, Z_NEAR, Y_BIT = 16, 8, 4, 2, 1
LINE = 128
SMALL = 20


def device_offsets(first, second):
    masks = (Z_FAR, Z_NEAR, first, second)
    return np.array(
        [sum(m for k, m in enumerate(masks) if p >> k & 1) for p in range(16)], np.int32
    )


def position_table(device_index):
    even = device_offsets(X_BIT, Y_BIT)
    odd = device_offsets(Y_BIT, X_BIT)
    table_even = jnp.asarray(np.concatenate([even, odd ^ CORE_BIT]))
    table_odd = jnp.asarray(np.concatenate([odd, even ^ CORE_BIT]))
    core = (device_index // CORE_BIT) % 2
    return jnp.where(core == 0, table_even, table_odd) ^ device_index


def exchange(value, even_mask, odd_mask):
    pairs = [(i, i ^ (odd_mask if i & CORE_BIT else even_mask)) for i in range(32)]
    return lax.ppermute(value, AXES, pairs)


def gather_blocks(shard):
    held = shard[None]
    for even_mask, odd_mask in ((Z_FAR, Z_FAR), (Z_NEAR, Z_NEAR), (X_BIT, Y_BIT)):
        held = jnp.concatenate([held, exchange(held, even_mask, odd_mask)])
    last = exchange(held, Y_BIT, X_BIT)
    return (held, last, exchange(held, CORE_BIT, CORE_BIT), exchange(last, CORE_BIT, CORE_BIT))


def add_low(first, second):
    return (first.astype(jnp.float32) + second.astype(jnp.float32)).astype(jnp.bfloat16)


def scatter_blocks(keep, send):
    held = add_low(keep, exchange(send, CORE_BIT, CORE_BIT))
    for even_mask, odd_mask in ((Y_BIT, X_BIT), (X_BIT, Y_BIT), (Z_NEAR, Z_NEAR), (Z_FAR, Z_FAR)):
        half = held.shape[0] // 2
        got = exchange(held[half:], even_mask, odd_mask)
        held = add_low(held[:half], got)
    return held[0]


def place_kernel(widths, table_ref, *refs):
    pieces, outs, sems = refs[:4], refs[4:-1], refs[-1]
    copies = []
    for spot in range(32):
        start = 0
        for out, width in zip(outs, widths):
            copies.append(
                pltpu.make_async_copy(
                    pieces[spot // 8].at[spot % 8, :, pl.ds(start, width)],
                    out.at[table_ref[spot]],
                    sems.at[len(copies)],
                )
            )
            start += width
    for copy in copies:
        copy.start()
    for copy in copies:
        copy.wait()


def place_blocks(table, pieces, widths):
    rows = pieces[0].shape[1]
    return pl.pallas_call(
        functools.partial(place_kernel, widths),
        out_shape=[jax.ShapeDtypeStruct((32, rows, width), jnp.bfloat16) for width in widths],
        in_specs=[pl.BlockSpec(memory_space=pltpu.SMEM)] + [pl.BlockSpec(memory_space=pl.ANY)] * 4,
        out_specs=[pl.BlockSpec(memory_space=pl.ANY)] * len(widths),
        scratch_shapes=[pltpu.SemaphoreType.DMA((32 * len(widths),))],
        name="place_blocks",
    )(table, *pieces)


def pick_kernel(widths, table_ref, *refs):
    count = len(widths)
    sources, outs, sems = refs[:count], refs[count:-1], refs[-1]
    copies = []
    for spot in range(32):
        start = 0
        for source, width in zip(sources, widths):
            copies.append(
                pltpu.make_async_copy(
                    source.at[table_ref[spot]],
                    outs[spot // 16].at[spot % 16, :, pl.ds(start, width)],
                    sems.at[len(copies)],
                )
            )
            start += width
    for copy in copies:
        copy.start()
    for copy in copies:
        copy.wait()


def pick_blocks(table, sources):
    widths = tuple(source.shape[2] for source in sources)
    rows = sources[0].shape[1]
    return pl.pallas_call(
        functools.partial(pick_kernel, widths),
        out_shape=[jax.ShapeDtypeStruct((16, rows, sum(widths)), jnp.bfloat16)] * 2,
        in_specs=[pl.BlockSpec(memory_space=pltpu.SMEM)]
        + [pl.BlockSpec(memory_space=pl.ANY)] * len(widths),
        out_specs=[pl.BlockSpec(memory_space=pl.ANY)] * 2,
        scratch_shapes=[pltpu.SemaphoreType.DMA((32 * len(widths),))],
        name="pick_blocks",
    )(table, *sources)


def merge_all(pair, device_count):
    if device_count == 32:
        for mask in (CORE_BIT, X_BIT, Y_BIT, Z_NEAR, Z_FAR):
            both = jnp.stack(pair)
            got = exchange(both, mask, mask)
            pair = merge_parts(pair, (got[0], got[1]))
        return pair
    peak = lax.pmax(pair[0], AXES)
    return (peak, lax.psum(pair[1] * jnp.exp(pair[0] - peak), AXES))


def gather_all(arrays, table):
    (qkv_weight, qkv_bias, out_weight, out_bias, attn_gain, attn_shift, up_weight, up_bias, down_weight, down_bias, ffn_gain, ffn_shift, query_emb) = arrays
    if table is None:
        return tuple(
            lax.all_gather(part, AXES, axis=0, tiled=True) for part in arrays[:-1]
        ) + (lax.all_gather(query_emb, AXES, axis=1, tiled=True),)
    rows = qkv_weight.shape[0]
    small = jnp.concatenate(
        [
            jnp.stack([out_bias, attn_gain, attn_shift, down_bias, ffn_gain, ffn_shift], axis=1),
            qkv_bias.reshape(rows, 2),
            up_bias.reshape(rows, 4),
            query_emb.T,
        ],
        axis=1,
    )
    small = jnp.pad(small, ((0, 0), (0, LINE - small.shape[1])))
    first = gather_blocks(jnp.concatenate([qkv_weight, out_weight, small], axis=1))
    second = gather_blocks(up_weight)
    third = gather_blocks(down_weight)
    widths = (qkv_weight.shape[1], out_weight.shape[1], LINE)
    qkv_all, out_all, small_all = place_blocks(table, first, widths)
    (up_all,) = place_blocks(table, second, (up_weight.shape[1],))
    (down_all,) = place_blocks(table, third, (down_weight.shape[1],))
    flat = lambda part: part.reshape(-1, part.shape[2])
    small_all = flat(small_all)
    rows6 = small_all[:, :6].T
    return (
        flat(qkv_all),
        small_all[:, 6:8].reshape(-1),
        flat(out_all),
        rows6[0],
        rows6[1],
        rows6[2],
        flat(up_all),
        small_all[:, 8:12].reshape(-1),
        flat(down_all),
        rows6[3],
        rows6[4],
        rows6[5],
        small_all[:, 12:20].T,
    )


def scatter_all(grads, table):
    if table is None:
        return tuple(
            lax.psum_scatter(part, AXES, scatter_dimension=0, tiled=True) for part in grads[:-1]
        ) + (lax.psum_scatter(grads[-1], AXES, scatter_dimension=1, tiled=True),)
    (qkv_weight, qkv_bias, out_weight, out_bias, attn_gain, attn_shift, up_weight, up_bias, down_weight, down_bias, ffn_gain, ffn_shift, query_emb) = grads
    blocks = lambda part: part.astype(jnp.bfloat16).reshape(32, -1, part.shape[1])
    small = jnp.concatenate(
        [
            jnp.stack([out_bias, attn_gain, attn_shift, down_bias, ffn_gain, ffn_shift], axis=1),
            qkv_bias.reshape(-1, 2),
            up_bias.reshape(-1, 4),
            query_emb.T,
        ],
        axis=1,
    )
    small = jnp.pad(small, ((0, 0), (0, LINE - small.shape[1])))
    down_part = scatter_blocks(*pick_blocks(table, [blocks(down_weight)]))
    up_part = scatter_blocks(*pick_blocks(table, [blocks(up_weight)]))
    first = scatter_blocks(
        *pick_blocks(table, [blocks(qkv_weight), blocks(out_weight), blocks(small)])
    )
    first = first.astype(jnp.float32)
    qkv_width, out_width = qkv_weight.shape[1], out_weight.shape[1]
    small = first[:, qkv_width + out_width :]
    return (
        first[:, :qkv_width],
        small[:, 6:8].reshape(-1),
        first[:, qkv_width : qkv_width + out_width],
        small[:, 0],
        small[:, 1],
        small[:, 2],
        up_part.astype(jnp.float32),
        small[:, 8:12].reshape(-1),
        down_part.astype(jnp.float32),
        small[:, 3],
        small[:, 4],
        small[:, 5],
        small[:, 12:20].T,
    )


def body(
    slot_states,
    answer_tags,
    slot_mask,
    retrieval,
    query_emb,
    qkv_weight,
    qkv_bias,
    out_weight,
    out_bias,
    attn_gain,
    attn_shift,
    up_weight,
    up_bias,
    down_weight,
    down_bias,
    ffn_gain,
    ffn_shift,
):
    group_count = lax.axis_size(AXES)
    device_index = lax.axis_index(AXES)
    table = position_table(device_index) if group_count == 32 else None
    gathered = gather_all(
        (
            qkv_weight,
            qkv_bias,
            out_weight,
            out_bias,
            attn_gain,
            attn_shift,
            up_weight,
            up_bias,
            down_weight,
            down_bias,
            ffn_gain,
            ffn_shift,
            query_emb,
        ),
        table,
    )
    params = tuple(gathered[:12])
    query_table = gathered[12]
    local_count = slot_states.shape[0]
    token_count = slot_states.shape[1]
    query_count, slot_count = slot_mask.shape
    running = jnp.cumsum(slot_mask.reshape(-1), dtype=jnp.int32)
    slot_ranks = jnp.arange(local_count, dtype=jnp.int32) * group_count + device_index
    places = jnp.sum(
        (running[None, :] <= slot_ranks[:, None]).astype(jnp.int32), axis=1, dtype=jnp.int32
    )
    slot_pick = (
        places[:, None] == jnp.arange(query_count * slot_count, dtype=jnp.int32)[None, :]
    ).astype(jnp.float32)
    owner_mask = (places // slot_count)[:, None] == jnp.arange(query_count, dtype=jnp.int32)[
        None, :
    ]
    owner_float = owner_mask.astype(jnp.float32)
    prior_score = jnp.dot(slot_pick, retrieval.reshape(-1), precision=highest)
    chosen_low = jnp.dot(
        owner_mask.astype(jnp.bfloat16), query_table, preferred_element_type=jnp.float32
    ).astype(jnp.bfloat16)
    labels = answer_tags.astype(jnp.float32)
    first_pass = layer_forward(params, slot_states)
    mixed_low = first_pass[13]
    logits = jnp.einsum("bld,bd->bl", mixed_low, chosen_low, preferred_element_type=jnp.float32)
    likelihood = jnp.mean(
        labels * jax.nn.log_sigmoid(logits) + (1.0 - labels) * jax.nn.log_sigmoid(-logits), axis=-1
    )
    scores = likelihood + prior_score
    masked = jnp.where(owner_mask, scores[:, None], neg_fill)
    local_peak = jnp.max(masked, axis=0)
    local_total = jnp.sum(jnp.where(owner_mask, jnp.exp(masked - local_peak[None, :]), 0.0), axis=0)
    merged = merge_all((local_peak, local_total), group_count)
    totals = merged[0] + jnp.log(merged[1])
    loss = -jnp.sum(totals)
    doc_weight = jnp.sum(
        jnp.where(owner_mask, jnp.exp(scores[:, None] - totals[None, :]), 0.0), axis=1
    )
    grad_score = -loss_scale * doc_weight
    grad_logit = grad_score[:, None] * (labels - jax.nn.sigmoid(logits)) / token_count
    grad_mixed = grad_logit[..., None] * chosen_low.astype(jnp.float32)[:, None, :]
    grad_chosen = jnp.einsum(
        "bl,bld->bd", grad_logit, mixed_low.astype(jnp.float32), precision=highest
    )
    grad_query = jnp.dot(owner_float.T, grad_chosen, precision=highest)
    params_back = params
    (
        qkv_full,
        qkv_bias_full,
        out_full,
        out_bias_full,
        attn_gain_full,
        attn_shift_full,
        up_full,
        up_bias_full,
        down_full,
        down_bias_full,
        ffn_gain_full,
        ffn_shift_full,
    ) = params_back
    (
        query_heads,
        key_heads,
        value_heads,
        attn_soft,
        soft_low,
        context,
        hidden_low,
        normed_attn,
        inverse_attn,
        up_proj,
        act_low,
        normed_ffn,
        inverse_ffn,
        mixed_again,
    ) = first_pass
    grad_ffn_gain = jnp.sum(grad_mixed * normed_ffn, axis=(0, 1))
    grad_ffn_shift = jnp.sum(grad_mixed, axis=(0, 1))
    grad_res_ffn = norm_backward(
        grad_mixed * ffn_gain_full.astype(jnp.float32), normed_ffn, inverse_ffn
    )
    grad_down_low = grad_res_ffn.astype(jnp.bfloat16)
    grad_down_bias = jnp.sum(grad_down_low, axis=(0, 1), dtype=jnp.float32)
    grad_down_weight = jnp.einsum(
        "blf,bld->fd", act_low, grad_down_low, preferred_element_type=jnp.float32
    )
    grad_act = jnp.einsum(
        "bld,fd->blf", grad_down_low, down_full, preferred_element_type=jnp.float32
    )
    gelu_value, gelu_pull = jax.vjp(gelu_exact, up_proj)
    grad_up_low = gelu_pull(grad_act)[0].astype(jnp.bfloat16)
    grad_up_bias = jnp.sum(grad_up_low, axis=(0, 1), dtype=jnp.float32)
    grad_up_weight = jnp.einsum(
        "bld,blf->df", hidden_low, grad_up_low, preferred_element_type=jnp.float32
    )
    grad_hidden = grad_res_ffn + jnp.einsum(
        "blf,df->bld", grad_up_low, up_full, preferred_element_type=jnp.float32
    )
    grad_attn_gain = jnp.sum(grad_hidden * normed_attn, axis=(0, 1))
    grad_attn_shift = jnp.sum(grad_hidden, axis=(0, 1))
    grad_res_attn = norm_backward(
        grad_hidden * attn_gain_full.astype(jnp.float32), normed_attn, inverse_attn
    )
    grad_attn_low = grad_res_attn.astype(jnp.bfloat16)
    grad_out_bias = jnp.sum(grad_attn_low, axis=(0, 1), dtype=jnp.float32)
    grad_out_weight = jnp.einsum(
        "bld,ble->de", context, grad_attn_low, preferred_element_type=jnp.float32
    )
    grad_context = (
        jnp.einsum("ble,de->bld", grad_attn_low, out_full, preferred_element_type=jnp.float32)
        .astype(jnp.bfloat16)
        .reshape(query_heads.shape)
    )
    grad_soft = jnp.einsum(
        "bqhd,bkhd->bhqk", grad_context, value_heads, preferred_element_type=jnp.float32
    )
    grad_value = jnp.einsum(
        "bhqk,bqhd->bkhd", soft_low, grad_context, preferred_element_type=jnp.float32
    )
    row_cross = jnp.sum(grad_soft * attn_soft, axis=-1, keepdims=True)
    grad_scores_low = (attn_soft * (grad_soft - row_cross)).astype(jnp.bfloat16)
    score_scale = 1.0 / math.sqrt(HEAD)
    grad_qheads = (
        jnp.einsum(
            "bhqk,bkhd->bqhd", grad_scores_low, key_heads, preferred_element_type=jnp.float32
        )
        * score_scale
    )
    grad_kheads = (
        jnp.einsum(
            "bhqk,bqhd->bkhd", grad_scores_low, query_heads, preferred_element_type=jnp.float32
        )
        * score_scale
    )
    flat_shape = slot_states.shape
    grad_pre_low = jnp.concatenate(
        [
            grad_qheads.reshape(flat_shape),
            grad_kheads.reshape(flat_shape),
            grad_value.reshape(flat_shape),
        ],
        axis=-1,
    ).astype(jnp.bfloat16)
    model_width = flat_shape[-1]
    grad_qkv_bias = jnp.concatenate(
        [
            jnp.sum(grad_pre_low[..., :model_width], axis=(0, 1), dtype=jnp.float32),
            jnp.sum(grad_pre_low[..., 2 * model_width :], axis=(0, 1), dtype=jnp.float32),
        ]
    )
    grad_qkv_weight = jnp.einsum(
        "bld,ble->de", slot_states, grad_pre_low, preferred_element_type=jnp.float32
    )
    states_grad = (
        grad_res_attn
        + jnp.einsum("ble,de->bld", grad_pre_low, qkv_full, preferred_element_type=jnp.float32)
    ).astype(jnp.bfloat16)
    all_sums = scatter_all(
        (
            grad_qkv_weight,
            grad_qkv_bias,
            grad_out_weight,
            grad_out_bias,
            grad_attn_gain,
            grad_attn_shift,
            grad_up_weight,
            grad_up_bias,
            grad_down_weight,
            grad_down_bias,
            grad_ffn_gain,
            grad_ffn_shift,
            grad_query,
        ),
        table,
    )
    summed = tuple(all_sums[:12])
    query_part = all_sums[12]
    return (
        mixed_low,
        loss,
        states_grad,
        query_part,
        summed[0],
        summed[1],
        summed[2],
        summed[3],
        summed[4],
        summed[5],
        summed[6],
        summed[7],
        summed[8],
        summed[9],
        summed[10],
        summed[11],
    )


def solution(mesh):
    in_specs = (
        P(("dp", "fsdp"), None, None),
        P(("dp", "fsdp"), None),
        P(),
        P(),
        P(None, ("dp", "fsdp")),
        P(("dp", "fsdp"), None),
        P(("dp", "fsdp")),
        P(("dp", "fsdp"), None),
        P(("dp", "fsdp")),
        P(("dp", "fsdp")),
        P(("dp", "fsdp")),
        P(("dp", "fsdp"), None),
        P(("dp", "fsdp")),
        P(("dp", "fsdp"), None),
        P(("dp", "fsdp")),
        P(("dp", "fsdp")),
        P(("dp", "fsdp")),
    )
    out_specs = (
        P(("dp", "fsdp"), None, None),
        P(),
        P(("dp", "fsdp"), None, None),
        P(None, ("dp", "fsdp")),
        P(("dp", "fsdp"), None),
        P(("dp", "fsdp")),
        P(("dp", "fsdp"), None),
        P(("dp", "fsdp")),
        P(("dp", "fsdp")),
        P(("dp", "fsdp")),
        P(("dp", "fsdp"), None),
        P(("dp", "fsdp")),
        P(("dp", "fsdp"), None),
        P(("dp", "fsdp")),
        P(("dp", "fsdp")),
        P(("dp", "fsdp")),
    )
    return jax.shard_map(body, mesh=mesh, in_specs=in_specs, out_specs=out_specs, check_vma=False)
```

```python
import functools
import math

import jax
import jax.numpy as jnp
import numpy as np
from jax import lax
from jax.experimental import pallas as pl
from jax.experimental.pallas import tpu as pltpu
from jax.sharding import PartitionSpec as P

HEAD = 64
PAIR = 2 * HEAD
LINE = 128
AXES = ("dp", "fsdp")
X_BIT, CORE_BIT, Z_FAR, Z_NEAR, Y_BIT = 16, 8, 4, 2, 1
BLOCKS = 32
HALF = BLOCKS // 2

eps_norm = 1e-12
loss_scale = 65536.0
neg_fill = -1e30
f32 = jnp.float32
bf16 = jnp.bfloat16
VMEM = pl.BlockSpec(memory_space=pltpu.VMEM)
SMEM = pl.BlockSpec(memory_space=pltpu.SMEM)
ANYWHERE = pl.BlockSpec(memory_space=pl.ANY)


def device_offsets(first, second):
    masks = (Z_FAR, Z_NEAR, first, second)
    return np.array(
        [sum(m for k, m in enumerate(masks) if p >> k & 1) for p in range(HALF)], np.int32
    )


def position_table(device_index):
    even = device_offsets(X_BIT, Y_BIT)
    odd = device_offsets(Y_BIT, X_BIT)
    table_even = jnp.asarray(np.concatenate([even, odd ^ CORE_BIT]))
    table_odd = jnp.asarray(np.concatenate([odd, even ^ CORE_BIT]))
    core = (device_index // CORE_BIT) % 2
    return jnp.where(core == 0, table_even, table_odd) ^ device_index


def exchange(value, even_mask, odd_mask):
    pairs = [(i, i ^ (odd_mask if i & CORE_BIT else even_mask)) for i in range(BLOCKS)]
    return lax.ppermute(value, AXES, pairs)


def gather_blocks(shard):
    held = shard[None]
    for even_mask, odd_mask in ((Z_FAR, Z_FAR), (Z_NEAR, Z_NEAR), (X_BIT, Y_BIT)):
        held = jnp.concatenate([held, exchange(held, even_mask, odd_mask)])
    last = exchange(held, Y_BIT, X_BIT)
    return (held, last, exchange(held, CORE_BIT, CORE_BIT), exchange(last, CORE_BIT, CORE_BIT))


def gather_plain(part):
    whole = lax.all_gather(part, AXES, axis=0, tiled=True)
    blocks = whole.reshape(BLOCKS, -1, whole.shape[1])
    return tuple(blocks[8 * k : 8 * k + 8] for k in range(4))


def add_low(first, second):
    return (first.astype(f32) + second.astype(f32)).astype(bf16)


def scatter_blocks(keep, send):
    held = add_low(keep, exchange(send, CORE_BIT, CORE_BIT))
    for even_mask, odd_mask in ((Y_BIT, X_BIT), (X_BIT, Y_BIT), (Z_NEAR, Z_NEAR), (Z_FAR, Z_FAR)):
        half = held.shape[0] // 2
        got = exchange(held[half:], even_mask, odd_mask)
        held = add_low(held[:half], got)
    return held[0].astype(f32)


def scatter_plain(keep, send):
    blocks = jnp.concatenate([keep, send])
    whole = blocks.reshape(-1, blocks.shape[2])
    return lax.psum_scatter(whole, AXES, scatter_dimension=0, tiled=True).astype(f32)


def merge_parts(first, second):
    peak = jnp.maximum(first[0], second[0])
    return (peak, first[1] * jnp.exp(first[0] - peak) + second[1] * jnp.exp(second[0] - peak))


def merge_all(pair, tuned):
    if tuned:
        for mask in (CORE_BIT, X_BIT, Y_BIT, Z_NEAR, Z_FAR):
            both = jnp.stack(pair)
            got = exchange(both, mask, mask)
            pair = merge_parts(pair, (got[0], got[1]))
        return pair
    peak = lax.pmax(pair[0], AXES)
    return (peak, lax.psum(pair[1] * jnp.exp(pair[0] - peak), AXES))


def call(kernel, name, outs, in_specs, out_specs, args, flops, moved, scratch=(), exps=0):
    return pl.pallas_call(
        kernel,
        out_shape=[jax.ShapeDtypeStruct(shape, dtype) for shape, dtype in outs],
        in_specs=in_specs,
        out_specs=out_specs,
        scratch_shapes=list(scratch),
        compiler_params=pltpu.CompilerParams(vmem_limit_bytes=44 * 2**20),
        cost_estimate=pl.CostEstimate(
            flops=int(flops), bytes_accessed=int(moved), transcendentals=int(exps)
        ),
        name=name,
    )(*args)


def mm(first, second):
    return jnp.dot(first, second, preferred_element_type=f32)


def mm_nt(first, second):
    return lax.dot_general(first, second, (((1,), (1,)), ((), ())), preferred_element_type=f32)


def mm_tn(first, second):
    return lax.dot_general(first, second, (((0,), (0,)), ((), ())), preferred_element_type=f32)


def row_mean(value):
    return jnp.mean(value, axis=-1, keepdims=True)


def block_copies(table_ref, pieces, start, width, target, sems):
    copies = [
        pltpu.make_async_copy(
            pieces[spot // 8].at[spot % 8, :, pl.ds(start, width)],
            target.at[table_ref[spot]],
            sems.at[spot],
        )
        for spot in range(BLOCKS)
    ]
    for copy in copies:
        copy.start()
    return copies


def wait_all(copies):
    for copy in copies:
        copy.wait()


def flat(value):
    return value.reshape(-1, value.shape[-1])


def small_kernel(start, table_ref, p0, p1, p2, p3, columns_ref, rows_ref, held_ref, sems):
    wait_all(block_copies(table_ref, (p0, p1, p2, p3), start, LINE, held_ref, sems))
    columns = flat(held_ref[...]).astype(f32)
    columns_ref[...] = columns
    rows_ref[...] = columns.T


def unpack_small(table, pieces, start):
    rows = pieces[0].shape[1]
    width = BLOCKS * rows
    return call(
        functools.partial(small_kernel, start),
        "unpack_small",
        [((width, LINE), f32), ((LINE, width), f32)],
        [SMEM] + [ANYWHERE] * 4,
        [VMEM, VMEM],
        (table, *pieces),
        0,
        width * LINE * 8,
        [pltpu.VMEM((BLOCKS, rows, LINE), bf16), pltpu.SemaphoreType.DMA((BLOCKS,))],
    )


def head_masks(shape):
    lane = lax.broadcasted_iota(jnp.int32, shape, 1)
    return lane < HEAD


def stacked(pair, low):
    zero = jnp.zeros_like(pair)
    return jnp.concatenate([jnp.where(low, pair, zero), jnp.where(low, zero, pair)])


def unstacked(value, low, length):
    return jnp.where(low, value[:length], value[length:])


def attention_kernel(
    buffers, table_ref, x_ref, bias_ref, p0, p1, p2, p3,
    qkv_ref, context_ref, lse_ref, wqkv_ref, wout_ref, sems, sems_out,
):
    pieces = (p0, p1, p2, p3)
    tokens, width = x_ref.shape
    length, pairs = tokens // buffers, width // PAIR
    copies = block_copies(table_ref, pieces, 0, 3 * width, wqkv_ref, sems)
    later = block_copies(table_ref, pieces, 3 * width, width, wout_ref, sems_out)
    wait_all(copies)
    x = x_ref[...]
    for part in range(3):
        span = slice(part * width, (part + 1) * width)
        weight = flat(wqkv_ref[:, :, span])
        qkv_ref[:, span] = (mm(x, weight) + bias_ref[:, span]).astype(bf16)
    scale = 1.0 / math.sqrt(HEAD)

    def step(index, carry):
        rows = pl.ds(pl.multiple_of(index // pairs * length, length), length)
        lane = pl.multiple_of(index % pairs * PAIR, PAIR)
        query = qkv_ref[rows, pl.ds(lane, PAIR)]
        key = qkv_ref[rows, pl.ds(lane + width, PAIR)]
        value = qkv_ref[rows, pl.ds(lane + 2 * width, PAIR)]
        low = head_masks(query.shape)
        scores = mm_nt(key, stacked(query, low)) * scale
        peak = jnp.max(scores, axis=0, keepdims=True)
        powers = jnp.exp(scores - peak)
        total = jnp.sum(powers, axis=0, keepdims=True)
        probs = (powers * (1.0 / total)).astype(bf16)
        mixed = mm_tn(value, probs).T
        context_ref[rows, pl.ds(lane, PAIR)] = unstacked(mixed, low, length).astype(bf16)
        lse_ref[index] = peak + jnp.log(total)
        return carry

    lax.fori_loop(0, buffers * pairs, step, 0)
    wait_all(later)


def attention_forward(table, x, buffers, bias, pieces):
    tokens, width = x.shape
    rows = pieces[0].shape[1]
    steps = buffers * (width // PAIR)
    length = tokens // buffers
    return call(
        functools.partial(attention_kernel, buffers),
        "attention_forward",
        [
            ((tokens, 3 * width), bf16),
            ((tokens, width), bf16),
            ((steps, 1, 2 * length), f32),
            ((BLOCKS, rows, 3 * width), bf16),
            ((BLOCKS, rows, width), bf16),
        ],
        [SMEM, VMEM, VMEM] + [ANYWHERE] * 4,
        [VMEM] * 5,
        (table, x, bias, *pieces),
        2 * tokens * width * (3 * width + 2 * length),
        20e6,
        [pltpu.SemaphoreType.DMA((BLOCKS,)), pltpu.SemaphoreType.DMA((BLOCKS,))],
        exps=tokens * length * width // HEAD,
    )


def normed_rows(residual):
    center = residual - row_mean(residual)
    inverse = lax.rsqrt(row_mean(center * center) + eps_norm)
    return center * inverse, inverse


def up_kernel(
    table_ref, x_ref, context_ref, wout_ref, vectors_ref, bias_ref, p0, p1, p2, p3,
    hidden_ref, normed_ref, inverse_ref, act_ref, slope_ref, wup_ref, sems,
):
    copies = block_copies(table_ref, (p0, p1, p2, p3), 0, wup_ref.shape[2], wup_ref, sems)
    out = mm(context_ref[...], flat(wout_ref[...])) + vectors_ref[0:1]
    normed, inverse = normed_rows(x_ref[...].astype(f32) + out)
    normed_ref[...] = normed
    inverse_ref[...] = inverse
    hidden = (normed * vectors_ref[1:2] + vectors_ref[2:3]).astype(bf16)
    hidden_ref[...] = hidden
    wait_all(copies)
    wide = 512

    def step(index, carry):
        span = pl.ds(pl.multiple_of(index * wide, wide), wide)
        up = mm(hidden_ref[...], flat(wup_ref[:, :, span])) + bias_ref[:, span]
        chance = 0.5 + 0.5 * lax.erf(up * math.sqrt(0.5))
        act_ref[:, span] = (up * chance).astype(bf16)
        density = jnp.exp(up * up * -0.5) * (1.0 / math.sqrt(2.0 * math.pi))
        slope_ref[:, span] = (chance + up * density).astype(bf16)
        return carry

    lax.fori_loop(0, wup_ref.shape[2] // wide, step, 0)


def up_forward(table, x, context, wout, vectors, bias, pieces):
    tokens, width = x.shape
    rows, hidden_units = pieces[0].shape[1:]
    return call(
        up_kernel,
        "up_forward",
        [
            ((tokens, width), bf16),
            ((tokens, width), f32),
            ((tokens, 1), f32),
            ((tokens, hidden_units), bf16),
            ((tokens, hidden_units), bf16),
            ((BLOCKS, rows, hidden_units), bf16),
        ],
        [SMEM] + [VMEM] * 5 + [ANYWHERE] * 4,
        [VMEM] * 6,
        (table, x, context, wout, vectors, bias, *pieces),
        2 * tokens * width * (width + hidden_units),
        20e6,
        [pltpu.SemaphoreType.DMA((BLOCKS,))],
        exps=2 * tokens * hidden_units,
    )


def down_kernel(
    buffers, table_ref, hidden_ref, act_ref, vectors_ref, chosen_ref, tags_ref, p0, p1, p2, p3,
    mixed_ref, like_ref, res_ref, low_ref, gain_ref, query_ref, bias_ref, wdown_ref, sems,
):
    tokens = hidden_ref.shape[0]
    length = tokens // buffers
    wait_all(block_copies(table_ref, (p0, p1, p2, p3), 0, wdown_ref.shape[2], wdown_ref, sems))
    weight = flat(wdown_ref[...])
    for buffer in range(buffers):
        rows = slice(buffer * length, (buffer + 1) * length)
        down = mm(act_ref[rows], weight) + vectors_ref[3:4]
        normed, inverse = normed_rows(hidden_ref[rows].astype(f32) + down)
        mixed = (normed * vectors_ref[4:5] + vectors_ref[5:6]).astype(bf16)
        mixed_ref[rows] = mixed
        mixed = mixed.astype(f32)
        chosen = chosen_ref[buffer : buffer + 1]
        logits = jnp.sum(mixed * chosen, axis=-1, keepdims=True)
        tags = tags_ref[rows].astype(f32)
        tail = jnp.log(1.0 + jnp.exp(-jnp.abs(logits)))
        log_yes = jnp.minimum(logits, 0.0) - tail
        log_no = jnp.minimum(-logits, 0.0) - tail
        like = jnp.sum(tags * log_yes + (1.0 - tags) * log_no, axis=0, keepdims=True) / length
        like_ref[buffer : buffer + 1] = jnp.broadcast_to(like, (1, LINE))
        pull = (tags - 1.0 / (1.0 + jnp.exp(-logits))) * (-loss_scale / length)
        gain_ref[buffer : buffer + 1] = jnp.sum(pull * normed, axis=0, keepdims=True) * chosen
        gain_ref[buffers + buffer : buffers + buffer + 1] = (
            jnp.sum(pull, axis=0, keepdims=True) * chosen
        )
        query_ref[buffer : buffer + 1] = jnp.sum(pull * mixed, axis=0, keepdims=True)
        slope = chosen * vectors_ref[4:5]
        grad = (inverse * pull) * (
            slope - row_mean(slope) - normed * row_mean(slope * normed)
        )
        res_ref[rows] = grad
        grad = grad.astype(bf16)
        low_ref[rows] = grad
        bias_ref[buffer : buffer + 1] = jnp.sum(grad.astype(f32), axis=0, keepdims=True)


def down_forward(table, hidden, act, vectors, chosen, tags, pieces, buffers):
    tokens, width = hidden.shape
    rows = pieces[0].shape[1]
    return call(
        functools.partial(down_kernel, buffers),
        "down_forward",
        [
            ((tokens, width), bf16),
            ((buffers, LINE), f32),
            ((tokens, width), f32),
            ((tokens, width), bf16),
            ((2 * buffers, width), f32),
            ((buffers, width), f32),
            ((buffers, width), f32),
            ((BLOCKS, rows, width), bf16),
        ],
        [SMEM] + [VMEM] * 5 + [ANYWHERE] * 4,
        [VMEM] * 8,
        (table, hidden, act, vectors, chosen, tags, *pieces),
        2 * tokens * width * BLOCKS * rows,
        20e6,
        [pltpu.SemaphoreType.DMA((BLOCKS,))],
    )


def up_back_kernel(buffers, low_ref, wdown_ref, slope_ref, grad_ref, bias_ref):
    tokens, units = slope_ref.shape
    length = tokens // buffers
    rows_of = wdown_ref.shape[1]
    part = 8

    def step(index, carry):
        blocks = pl.ds(index * part, part)
        wide = part * rows_of
        span = pl.ds(pl.multiple_of(index * wide, wide), wide)
        grad = mm_nt(low_ref[...], flat(wdown_ref[blocks])) * slope_ref[:, span].astype(f32)
        grad = grad.astype(bf16)
        grad_ref[:, span] = grad
        for buffer in range(buffers):
            piece = grad[buffer * length : (buffer + 1) * length].astype(f32)
            bias_ref[buffer : buffer + 1, span] = jnp.sum(piece, axis=0, keepdims=True)
        return carry

    lax.fori_loop(0, BLOCKS // part, step, 0)


def up_backward(low, wdown, slope, buffers):
    tokens, units = slope.shape
    return call(
        functools.partial(up_back_kernel, buffers),
        "up_backward",
        [((tokens, units), bf16), ((buffers, units), f32)],
        [VMEM] * 3,
        [VMEM] * 2,
        (low, wdown, slope),
        2 * tokens * units * low.shape[1],
        13e6,
    )


def hidden_back_kernel(
    buffers, res_ref, grad_up_ref, wup_ref, normed_ref, inverse_ref, vectors_ref, wout_ref,
    res_out_ref, low_ref, context_ref, gain_ref, bias_ref,
):
    tokens = res_ref.shape[0]
    length = tokens // buffers
    weight, weight_out = flat(wup_ref[...]), flat(wout_ref[...])
    for buffer in range(buffers):
        rows = slice(buffer * length, (buffer + 1) * length)
        normed = normed_ref[rows]
        grad = res_ref[rows] + mm_nt(grad_up_ref[rows], weight)
        gain_ref[buffer : buffer + 1] = jnp.sum(grad * normed, axis=0, keepdims=True)
        gain_ref[buffers + buffer : buffers + buffer + 1] = jnp.sum(grad, axis=0, keepdims=True)
        grad = grad * vectors_ref[1:2]
        grad = inverse_ref[rows] * (
            grad - row_mean(grad) - normed * row_mean(grad * normed)
        )
        res_out_ref[rows] = grad
        grad = grad.astype(bf16)
        low_ref[rows] = grad
        bias_ref[buffer : buffer + 1] = jnp.sum(grad.astype(f32), axis=0, keepdims=True)
        context_ref[rows] = mm_nt(grad, weight_out).astype(bf16)


def hidden_backward(res, grad_up, wup, normed, inverse, vectors, wout, buffers):
    tokens, width = res.shape
    return call(
        functools.partial(hidden_back_kernel, buffers),
        "hidden_backward",
        [
            ((tokens, width), f32),
            ((tokens, width), bf16),
            ((tokens, width), bf16),
            ((2 * buffers, width), f32),
            ((buffers, width), f32),
        ],
        [VMEM] * 7,
        [VMEM] * 5,
        (res, grad_up, wup, normed, inverse, vectors, wout),
        2 * tokens * width * (width + grad_up.shape[1]),
        18e6,
    )


def attention_back_kernel(buffers, qkv_ref, lse_ref, grad_ref, pre_ref, bias_ref):
    tokens, width = grad_ref.shape
    length, pairs = tokens // buffers, width // PAIR
    scale = 1.0 / math.sqrt(HEAD)

    def step(index, carry):
        rows = pl.ds(pl.multiple_of(index // pairs * length, length), length)
        lane = pl.multiple_of(index % pairs * PAIR, PAIR)
        query = qkv_ref[rows, pl.ds(lane, PAIR)]
        key = qkv_ref[rows, pl.ds(lane + width, PAIR)]
        value = qkv_ref[rows, pl.ds(lane + 2 * width, PAIR)]
        low = head_masks(query.shape)
        query = stacked(query, low)
        grad = stacked(grad_ref[rows, pl.ds(lane, PAIR)], low)
        probs = jnp.exp(mm_nt(key, query) * scale - lse_ref[index])
        grad_probs = mm_nt(value, grad)
        cross = jnp.sum(grad_probs * probs, axis=0, keepdims=True)
        grad_scores = (probs * (grad_probs - cross)).astype(bf16)
        grad_value = mm(probs.astype(bf16), grad)
        grad_key = mm(grad_scores, query) * scale
        grad_query = unstacked(mm_tn(key, grad_scores).T, low, length) * scale
        pre_ref[rows, pl.ds(lane, PAIR)] = grad_query.astype(bf16)
        pre_ref[rows, pl.ds(lane + width, PAIR)] = grad_key.astype(bf16)
        pre_ref[rows, pl.ds(lane + 2 * width, PAIR)] = grad_value.astype(bf16)
        return carry

    lax.fori_loop(0, buffers * pairs, step, 0)
    for buffer in range(buffers):
        rows = slice(buffer * length, (buffer + 1) * length)
        for start, source in ((0, 0), (width, 2 * width)):
            piece = pre_ref[rows, source : source + width].astype(f32)
            bias_ref[buffer : buffer + 1, start : start + width] = jnp.sum(
                piece, axis=0, keepdims=True
            )


def attention_backward(qkv, lse, grad, buffers):
    tokens, width = grad.shape
    length = tokens // buffers
    return call(
        functools.partial(attention_back_kernel, buffers),
        "attention_backward",
        [((tokens, 3 * width), bf16), ((buffers, 2 * width), f32)],
        [VMEM] * 3,
        [VMEM] * 2,
        (qkv, lse, grad),
        10 * tokens * length * width,
        7e6,
        exps=tokens * length * width // HEAD,
    )


def weight_kernel(buffers, tile, table_ref, scale_ref, left_ref, right_ref, *refs):
    extra, (keep_ref, send_ref, right_scaled, sums) = refs[:-4], refs[-4:]
    tokens, columns = right_ref.shape
    length = tokens // buffers
    rows = keep_ref.shape[1]
    for buffer in range(buffers):
        span = slice(buffer * length, (buffer + 1) * length)
        right_scaled[span] = (right_ref[span].astype(f32) * scale_ref[buffer]).astype(bf16)

    def place(value_of, start, count):
        for spot in range(BLOCKS):
            target = keep_ref if spot < HALF else send_ref
            target[spot % HALF, :, start : start + count] = value_of(table_ref[spot]).astype(bf16)

    def rows_at(block):
        return pl.ds(pl.multiple_of(block * rows, 8), rows)

    for start in range(0, columns, tile):
        sums[...] = mm_tn(left_ref[...], right_scaled[:, start : start + tile])
        place(lambda block: sums[rows_at(block)], start, tile)
    start = columns
    for ref in extra:
        place(lambda block, ref=ref: ref[rows_at(block)], start, ref.shape[1])
        start += ref.shape[1]


def weight_gradient(name, table, scale, left, right, buffers, tile, extra=()):
    tokens, height = left.shape
    columns = right.shape[1]
    rows = height // BLOCKS
    total = columns + sum(part.shape[1] for part in extra)
    return call(
        functools.partial(weight_kernel, buffers, tile),
        name,
        [((HALF, rows, total), bf16)] * 2,
        [SMEM, SMEM] + [VMEM] * (2 + len(extra)),
        [VMEM] * 2,
        (table, scale, left, right, *extra),
        2 * tokens * height * columns,
        10e6,
        [pltpu.VMEM((tokens, columns), bf16), pltpu.VMEM((height, tile), f32)],
    )


def out_weight_kernel(buffers, scale_ref, left_ref, right_ref, small_ref, out_ref, columns_ref):
    tokens = right_ref.shape[0]
    length = tokens // buffers
    scaled = jnp.concatenate(
        [
            (
                right_ref[buffer * length : (buffer + 1) * length].astype(f32)
                * scale_ref[buffer]
            ).astype(bf16)
            for buffer in range(buffers)
        ]
    )
    out_ref[...] = mm_tn(left_ref[...], scaled)
    columns_ref[...] = small_ref[...].T


def out_weight_gradient(scale, left, right, small, buffers):
    tokens, width = left.shape
    return call(
        functools.partial(out_weight_kernel, buffers),
        "out_weight_gradient",
        [((width, width), f32), ((width, LINE), f32)],
        [SMEM] + [VMEM] * 3,
        [VMEM] * 2,
        (scale, left, right, small),
        2 * tokens * width * width,
        6e6,
    )


def states_kernel(buffers, scale_ref, res_ref, pre_ref, weight_ref, out_ref):
    tokens = res_ref.shape[0]
    length = tokens // buffers
    weight = flat(weight_ref[...])
    for buffer in range(buffers):
        rows = slice(buffer * length, (buffer + 1) * length)
        grad = res_ref[rows] + mm_nt(pre_ref[rows], weight)
        out_ref[rows] = (grad * scale_ref[buffer]).astype(bf16)


def states_gradient(scale, res, pre, weight, buffers):
    tokens, width = res.shape
    return call(
        functools.partial(states_kernel, buffers),
        "states_gradient",
        [((tokens, width), bf16)],
        [SMEM] + [VMEM] * 3,
        [VMEM],
        (scale, res, pre, weight),
        6 * tokens * width * width,
        8e6,
    )[0]


def body(
    slot_states, answer_tags, slot_mask, retrieval, query_emb, qkv_weight, qkv_bias, out_weight,
    out_bias, attn_gain, attn_shift, up_weight, up_bias, down_weight, down_bias, ffn_gain, ffn_shift,
):
    group_count = lax.axis_size(AXES)
    device_index = lax.axis_index(AXES)
    tuned = group_count == BLOCKS
    buffers, length, width = slot_states.shape
    query_count, slot_count = slot_mask.shape
    tokens = buffers * length
    x = slot_states.reshape(tokens, width)

    running = jnp.cumsum(slot_mask.reshape(-1), dtype=jnp.int32)
    slot_ranks = jnp.arange(buffers, dtype=jnp.int32) * group_count + device_index
    places = jnp.sum(
        (running[None, :] <= slot_ranks[:, None]).astype(jnp.int32), axis=1, dtype=jnp.int32
    )
    slot_pick = places[:, None] == jnp.arange(query_count * slot_count, dtype=jnp.int32)[None, :]
    owner_mask = (places // slot_count)[:, None] == jnp.arange(query_count, dtype=jnp.int32)[None]
    prior_score = jnp.sum(jnp.where(slot_pick, retrieval.reshape(-1)[None, :], 0.0), axis=1)
    tags = answer_tags.reshape(tokens, 1)

    if tuned:
        table = position_table(device_index)
        rows = qkv_weight.shape[0]
        small = jnp.concatenate(
            [
                jnp.stack([out_bias, attn_gain, attn_shift, down_bias, ffn_gain, ffn_shift], axis=1),
                qkv_bias.reshape(rows, 2),
                up_bias.reshape(rows, 4),
                query_emb.T,
            ],
            axis=1,
        )
        small = jnp.pad(small, ((0, 0), (0, LINE - small.shape[1])))
        first = gather_blocks(jnp.concatenate([qkv_weight, out_weight, small], axis=1))
        second = gather_blocks(up_weight)
        third = gather_blocks(down_weight)
        columns, small_rows = unpack_small(table, first, 4 * width)
        vectors = small_rows[:6]
        qkv_bias_all = columns[:, 6:8].reshape(-1)
        up_bias_all = columns[:, 8:12].reshape(1, -1)
        query_table = small_rows[12 : 12 + query_count]
    else:
        table = jnp.arange(BLOCKS, dtype=jnp.int32)
        everything = lambda part: lax.all_gather(part, AXES, axis=0, tiled=True).astype(f32)
        first = gather_plain(jnp.concatenate([qkv_weight, out_weight], axis=1))
        second = gather_plain(up_weight)
        third = gather_plain(down_weight)
        vectors = jnp.stack(
            [
                everything(part)
                for part in (out_bias, attn_gain, attn_shift, down_bias, ffn_gain, ffn_shift)
            ]
        )
        qkv_bias_all = everything(qkv_bias)
        up_bias_all = everything(up_bias).reshape(1, -1)
        query_table = lax.all_gather(query_emb, AXES, axis=1, tiled=True).astype(f32)
    bias = jnp.concatenate(
        [qkv_bias_all[:width], jnp.zeros((width,), f32), qkv_bias_all[width:]]
    ).reshape(1, -1)
    chosen = jnp.sum(jnp.where(owner_mask[:, :, None], query_table[None], 0.0), axis=1)

    qkv, context, lse, wqkv, wout = attention_forward(table, x, buffers, bias, first)
    hidden, normed, inverse, act, slope, wup = up_forward(
        table, x, context, wout, vectors, up_bias_all, second
    )
    mixed, like, grad_res, grad_low, gain_sums, query_sums, down_sums, wdown = down_forward(
        table, hidden, act, vectors, chosen, tags, third, buffers
    )

    scores = like[:, 0] + prior_score
    masked = jnp.where(owner_mask, scores[:, None], neg_fill)
    local_peak = jnp.max(masked, axis=0)
    local_total = jnp.sum(jnp.where(owner_mask, jnp.exp(masked - local_peak[None, :]), 0.0), axis=0)
    merged = merge_all((local_peak, local_total), tuned)
    totals = merged[0] + jnp.log(merged[1])
    loss = -jnp.sum(totals)
    scale = jnp.sum(
        jnp.where(owner_mask, jnp.exp(scores[:, None] - totals[None, :]), 0.0), axis=1
    )

    grad_up, up_sums = up_backward(grad_low, wdown, slope, buffers)
    grad_hidden, grad_attn, grad_context, attn_sums, out_sums = hidden_backward(
        grad_res, grad_up, wup, normed, inverse, vectors, wout, buffers
    )
    grad_pre, pre_sums = attention_backward(qkv, lse, grad_context, buffers)

    scatter = scatter_blocks if tuned else scatter_plain
    down_part = scatter(
        *weight_gradient("down_gradient", table, scale, act, grad_low, buffers, width)
    )
    up_part = scatter(
        *weight_gradient("up_gradient", table, scale, hidden, grad_up, buffers, width)
    )
    weigh = lambda sums: jnp.sum(scale[:, None] * sums, axis=0)
    six = [
        weigh(out_sums),
        weigh(attn_sums[:buffers]),
        weigh(attn_sums[buffers:]),
        weigh(down_sums),
        weigh(gain_sums[:buffers]),
        weigh(gain_sums[buffers:]),
    ]
    qkv_bias_sum = weigh(pre_sums)
    up_bias_sum = weigh(up_sums)
    weighed = jnp.where(owner_mask, scale[:, None], 0.0)
    query_sum = jnp.sum(weighed[:, :, None] * query_sums[:, None, :], axis=0)
    if tuned:
        small = jnp.concatenate(
            [
                jnp.stack(six),
                qkv_bias_sum.reshape(width, 2).T,
                up_bias_sum.reshape(width, 4).T,
                query_sum,
            ]
        )
        small = jnp.pad(small, ((0, LINE - small.shape[0]), (0, 0)))
    else:
        small = jnp.zeros((LINE, width), f32)
    grad_out, small = out_weight_gradient(scale, context, grad_attn, small, buffers)
    first = scatter(
        *weight_gradient(
            "qkv_gradient", table, scale, x, grad_pre, buffers, width, (grad_out, small)
        )
    )
    states = states_gradient(scale, grad_hidden, grad_pre, wqkv, buffers)
    if tuned:
        small = first[:, 4 * width :]
        six = [small[:, k] for k in range(6)]
        qkv_bias_sum = small[:, 6:8].reshape(-1)
        up_bias_sum = small[:, 8:12].reshape(-1)
        query_sum = small[:, 12 : 12 + query_count].T
    else:
        mine = lambda part: lax.psum_scatter(part, AXES, scatter_dimension=0, tiled=True)
        six = [mine(part) for part in six]
        qkv_bias_sum = mine(qkv_bias_sum)
        up_bias_sum = mine(up_bias_sum)
        query_sum = lax.psum_scatter(query_sum, AXES, scatter_dimension=1, tiled=True)
    return (
        mixed.reshape(slot_states.shape),
        loss,
        states.reshape(slot_states.shape),
        query_sum,
        first[:, : 3 * width],
        qkv_bias_sum,
        first[:, 3 * width : 4 * width],
        six[0],
        six[1],
        six[2],
        up_part,
        up_bias_sum,
        down_part,
        six[3],
        six[4],
        six[5],
    )


def solution(mesh):
    split = P(AXES)
    in_specs = (split, split, P(), P(), P(None, AXES)) + (split,) * 12
    out_specs = (split, P(), split, P(None, AXES)) + (split,) * 12
    return jax.shard_map(body, mesh=mesh, in_specs=in_specs, out_specs=out_specs, check_vma=False)
```

```python
import functools
import math

import jax
import jax.numpy as jnp
import numpy as np
from jax import lax
from jax.experimental import pallas as pl
from jax.experimental.pallas import tpu as pltpu
from jax.sharding import PartitionSpec as P

HEAD = 64
PAIR = 2 * HEAD
LINE = 128
AXES = ("dp", "fsdp")
X_BIT, CORE_BIT, Z_FAR, Z_NEAR, Y_BIT = 16, 8, 4, 2, 1
BLOCKS = 32
HALF = BLOCKS // 2
SHARE = 0.02
LIMIT = 12

eps_norm = 1e-12
loss_scale = 65536.0
neg_fill = -1e30
f32 = jnp.float32
bf16 = jnp.bfloat16
VMEM = pl.BlockSpec(memory_space=pltpu.VMEM)
SMEM = pl.BlockSpec(memory_space=pltpu.SMEM)
HBM = pl.BlockSpec(memory_space=pltpu.HBM)


def device_offsets(first, second):
    masks = (Z_FAR, Z_NEAR, first, second)
    return np.array(
        [sum(m for k, m in enumerate(masks) if p >> k & 1) for p in range(HALF)], np.int32
    )


def position_table(device_index):
    even = device_offsets(X_BIT, Y_BIT)
    odd = device_offsets(Y_BIT, X_BIT)
    table_even = jnp.asarray(np.concatenate([even, odd ^ CORE_BIT]))
    table_odd = jnp.asarray(np.concatenate([odd, even ^ CORE_BIT]))
    core = (device_index // CORE_BIT) % 2
    return jnp.where(core == 0, table_even, table_odd) ^ device_index


def exchange(value, even_mask, odd_mask):
    pairs = [(i, i ^ (odd_mask if i & CORE_BIT else even_mask)) for i in range(BLOCKS)]
    return lax.ppermute(value, AXES, pairs)


def after(value, *earlier):
    return lax.optimization_barrier((value, *earlier))[0]


SIDE, OTHER, CORES = (X_BIT, Y_BIT), (Y_BIT, X_BIT), (CORE_BIT, CORE_BIT)
LINE_MASKS = (Z_FAR, Z_NEAR, Z_FAR | Z_NEAR)


class Order:
    def __init__(self, tuned):
        self.tuned, self.last = tuned, None

    def place(self, value):
        if self.tuned and self.last is not None:
            return after(value, self.last)
        return value

    def mark(self, value):
        self.last = value


class Gather:
    def __init__(self, order, held):
        self.order, self.held = order, held

    def start_line(self, *earlier):
        own = after(self.held, *earlier) if earlier else self.held
        self.got = [exchange(own, mask, mask) for mask in LINE_MASKS]

    def start(self, masks, *earlier):
        self.got = [exchange(after(self.held, *earlier) if earlier else self.held, *masks)]

    def join(self):
        got = [self.order.place(part) for part in self.got]
        self.held = jnp.concatenate([self.held, *got])
        self.order.mark(self.held)

    def start_cores(self):
        self.last = self.order.place(self.got[0])
        self.order.mark(self.last)
        self.far = exchange(self.held, *CORES), exchange(self.last, *CORES)

    def pieces(self):
        far = [self.order.place(part) for part in self.far]
        self.order.mark(far[1])
        return (self.held, self.last, *far)


def gather_plain(part):
    whole = lax.all_gather(part, AXES, axis=0, tiled=True)
    blocks = whole.reshape(BLOCKS, -1, whole.shape[1])
    return tuple(blocks[8 * k : 8 * k + 8] for k in range(4))


def add_low(first, second):
    return (first.astype(f32) + second.astype(f32)).astype(bf16)


class Scatter:
    def __init__(self, order, keep, send):
        self.order, self.keep, self.send = order, keep, send

    def start(self, masks, *earlier):
        self.got = exchange(after(self.send, *earlier) if earlier else self.send, *masks)

    def join(self):
        half = self.keep.shape[0] // 2
        got = self.order.place(self.got)
        self.send = add_low(self.keep[half:], got[half:])
        self.keep = add_low(self.keep[:half], got[:half])
        self.order.mark(self.send)

    def start_line(self):
        got = self.order.place(self.got)
        sends = [add_low(self.keep[p : p + 1], got[p : p + 1]) for p in (1, 2, 3)]
        self.got = [exchange(part, mask, mask) for part, mask in zip(sends, LINE_MASKS)]
        self.keep = self.keep[0].astype(f32) + got[0].astype(f32)
        self.order.mark(sends[-1])

    def finish(self, start=0, width=None):
        end = self.keep.shape[1] if width is None else start + width
        cut = lambda part: part[..., start:end]
        got = [cut(self.order.place(part)[0]).astype(f32) for part in self.got]
        return cut(self.keep) + (got[0] + got[1] + got[2])


def scatter_plain(keep, send):
    blocks = jnp.concatenate([keep, send])
    whole = blocks.reshape(-1, blocks.shape[2])
    return lax.psum_scatter(whole, AXES, scatter_dimension=0, tiled=True).astype(f32)


def merge_parts(first, second):
    peak = jnp.maximum(first[0], second[0])
    return (peak, first[1] * jnp.exp(first[0] - peak) + second[1] * jnp.exp(second[0] - peak))


def merge_start(pair, mask):
    return exchange(jnp.stack(pair), mask, mask)


def merge_join(order, pair, got):
    got = order.place(got)
    pair = merge_parts(pair, (got[0], got[1]))
    order.mark(pair[0])
    return pair


def merge_plain(pair):
    peak = lax.pmax(pair[0], AXES)
    return (peak, lax.psum(pair[1] * jnp.exp(pair[0] - peak), AXES))


def call(
    kernel, name, outs, in_specs, out_specs, args, flops, moved, scratch=(), exps=0, limit=None
):
    args = [
        pltpu.with_memory_space_constraint(arg, pltpu.HBM) if spec is HBM else arg
        for arg, spec in zip(args, in_specs)
    ]
    return pl.pallas_call(
        kernel,
        out_shape=[
            pltpu.HBM(shape, dtype) if spec is HBM else jax.ShapeDtypeStruct(shape, dtype)
            for (shape, dtype), spec in zip(outs, out_specs)
        ],
        in_specs=in_specs,
        out_specs=out_specs,
        scratch_shapes=list(scratch),
        compiler_params=pltpu.CompilerParams(vmem_limit_bytes=(limit or LIMIT) * 2**20),
        cost_estimate=pl.CostEstimate(
            flops=int(flops * SHARE), bytes_accessed=int(moved * SHARE), transcendentals=int(exps * SHARE)
        ),
        name=name,
    )(*args)


def mm(first, second):
    return jnp.dot(first, second, preferred_element_type=f32)


def mm_nt(first, second):
    return lax.dot_general(first, second, (((1,), (1,)), ((), ())), preferred_element_type=f32)


def mm_tn(first, second):
    return lax.dot_general(first, second, (((0,), (0,)), ((), ())), preferred_element_type=f32)


def row_mean(value):
    return jnp.mean(value, axis=-1, keepdims=True)


def block_copies(table_ref, pieces, start, width, target, sems):
    copies = [
        pltpu.make_async_copy(
            pieces[spot // 8].at[spot % 8, :, pl.ds(start, width)],
            target.at[table_ref[spot]],
            sems.at[spot],
        )
        for spot in range(BLOCKS)
    ]
    for copy in copies:
        copy.start()
    return copies


def fetch(pairs, sems, first=0):
    copies = [
        pltpu.make_async_copy(source, target, sems.at[first + k])
        for k, (source, target) in enumerate(pairs)
    ]
    for copy in copies:
        copy.start()
    return copies


def wait_all(copies):
    for copy in copies:
        copy.wait()


def flat(value):
    return value.reshape(-1, value.shape[-1])


SIX, QKV_AT, UP_AT, QUERY_AT = 6, 6, 8, 12
VECTORS = 8


def pack_kernel(weight_hbm, *refs):
    sources, out_ref, parts, held_ref, sems = refs[: SIX + 3], refs[SIX + 3], refs[SIX + 4 : -2], *refs[-2:]
    rows, width = out_ref.shape[1], out_ref.shape[2] - LINE
    copies = fetch(zip(sources, parts), sems)
    copies += fetch([(weight_hbm, out_ref.at[0, :, pl.ds(0, width)])], sems, len(parts))
    vectors, (qkv_ref, up_ref, query_ref) = parts[:SIX], parts[SIX:]
    held_ref[...] = jnp.zeros_like(held_ref)
    wait_all(copies)
    for k, ref in enumerate(vectors):
        held_ref[k : k + 1, :rows] = ref[...].astype(f32)
    for at, ref, count in ((QKV_AT, qkv_ref, 2), (UP_AT, up_ref, 4)):
        value = ref[...].astype(f32)
        for c in range(count):
            held_ref[at + c : at + c + 1, :rows] = value[:, c * rows : (c + 1) * rows]
    count = query_ref.shape[0]
    held_ref[QUERY_AT : QUERY_AT + count, :rows] = query_ref[...].astype(f32)
    out_ref[0, :, width:] = held_ref[...].T[:rows].astype(bf16)


def pack_first(weight, vectors, qkv_bias, up_bias, query_emb):
    rows, width = weight.shape
    parts = [part.reshape(1, -1) for part in (*vectors, qkv_bias, up_bias)] + [query_emb]
    return call(
        pack_kernel,
        "pack_first",
        [((1, rows, width + LINE), bf16)],
        [HBM] * (1 + len(parts)),
        [VMEM],
        [weight, *parts],
        0,
        1e5,
        [pltpu.VMEM(part.shape, part.dtype) for part in parts]
        + [pltpu.VMEM((LINE, LINE), f32), pltpu.SemaphoreType.DMA((len(parts) + 1,))],
    )[0]


def unpack_kernel(
    start, count, table_ref, p0, p1, p2, p3, consts_ref, qkv_ref, up_ref,
    held_ref, qkv_wide, up_wide, sems,
):
    wait_all(block_copies(table_ref, (p0, p1, p2, p3), start, LINE, held_ref, sems))
    rows = held_ref.shape[1]
    every = flat(held_ref[...]).astype(f32)
    for block in range(BLOCKS):
        value = every[block * rows : (block + 1) * rows]
        for c in range(2):
            qkv_wide[(2 * block + c) * rows : (2 * block + c + 1) * rows] = value
        for c in range(4):
            up_wide[(4 * block + c) * rows : (4 * block + c + 1) * rows] = value
    turned = every.T
    consts_ref[:VECTORS] = turned[:VECTORS]
    consts_ref[VECTORS:] = turned[QUERY_AT : QUERY_AT + count]

    def line(wide, at, count):
        picks = lax.broadcasted_iota(jnp.int32, (8, LINE), 1) == at + lax.broadcasted_iota(
            jnp.int32, (8, LINE), 0
        )
        found = mm_nt(picks.astype(bf16), wide[...].astype(bf16))
        part = lax.broadcasted_iota(jnp.int32, found.shape, 1) // rows % count
        mine = part == lax.broadcasted_iota(jnp.int32, found.shape, 0)
        return jnp.sum(jnp.where(mine, found, 0.0), axis=0, keepdims=True)

    up_ref[...] = line(up_wide, UP_AT, 4)
    width = held_ref.shape[0] * rows
    bias = line(qkv_wide, QKV_AT, 2)
    qkv_ref[:, :width] = bias[:, :width]
    qkv_ref[:, width : 2 * width] = jnp.zeros((1, width), f32)
    qkv_ref[:, 2 * width :] = bias[:, width:]


def unpack_small(table, pieces, start, query_count):
    rows = pieces[0].shape[1]
    width = BLOCKS * rows
    return call(
        functools.partial(unpack_kernel, start, query_count),
        "unpack_small",
        [((VECTORS + query_count, width), f32), ((1, 3 * width), f32), ((1, 4 * width), f32)],
        [SMEM] + [HBM] * 4,
        [VMEM] * 3,
        (table, *pieces),
        0,
        1e6,
        [
            pltpu.VMEM((BLOCKS, rows, LINE), bf16),
            pltpu.VMEM((2 * width, LINE), f32),
            pltpu.VMEM((4 * width, LINE), f32),
            pltpu.SemaphoreType.DMA((BLOCKS,)),
        ],
    )


def split_kernel(small_ref, *refs):
    vectors, (qkv_ref, up_ref, query_ref, held_ref) = refs[:SIX], refs[SIX:]
    rows = small_ref.shape[0]
    held_ref[...] = jnp.zeros_like(held_ref)
    held_ref[:rows] = small_ref[...]
    turned = held_ref[...].T
    for k, ref in enumerate(vectors):
        ref[...] = turned[k : k + 1, :rows]
    for c in range(2):
        qkv_ref[:, c * rows : (c + 1) * rows] = turned[QKV_AT + c : QKV_AT + c + 1, :rows]
    for c in range(4):
        up_ref[:, c * rows : (c + 1) * rows] = turned[UP_AT + c : UP_AT + c + 1, :rows]
    query_ref[...] = turned[QUERY_AT : QUERY_AT + query_ref.shape[0], :rows]


def split_small(small, query_count):
    rows = small.shape[0]
    outs = call(
        split_kernel,
        "split_small",
        [((1, rows), f32)] * SIX + [((1, 2 * rows), f32), ((1, 4 * rows), f32), ((query_count, rows), f32)],
        [VMEM],
        [VMEM] * (SIX + 3),
        (small,),
        0,
        1e5,
        [pltpu.VMEM((LINE, LINE), f32)],
    )
    return [part.reshape(-1) for part in outs[:-1]] + [outs[-1]]


def block_scratch(rows, width):
    return [pltpu.VMEM((BLOCKS, rows, width), bf16), pltpu.SemaphoreType.DMA((BLOCKS,))]


def head_masks(shape):
    lane = lax.broadcasted_iota(jnp.int32, shape, 1)
    return lane < HEAD


def stacked(pair, low):
    zero = jnp.zeros_like(pair)
    return jnp.concatenate([jnp.where(low, pair, zero), jnp.where(low, zero, pair)])


def unstacked(value, low, length):
    return jnp.where(low, value[:length], value[length:])


def rows_of(buffer, length):
    return slice(buffer * length, (buffer + 1) * length)


def rows_of(buffer, length):
    return slice(buffer * length, (buffer + 1) * length)


def qkv_kernel(table_ref, x_ref, bias_ref, p0, p1, p2, p3, qkv_ref, weight_ref, sems):
    width = x_ref.shape[1]
    wait_all(block_copies(table_ref, (p0, p1, p2, p3), 0, 3 * width, weight_ref, sems))
    x = x_ref[...]
    for part in range(3):
        span = slice(part * width, (part + 1) * width)
        weight = flat(weight_ref[:, :, span])
        qkv_ref[:, span] = (mm(x, weight) + bias_ref[:, span]).astype(bf16)


def qkv_forward(table, x, bias, pieces):
    tokens, width = x.shape
    rows = pieces[0].shape[1]
    return call(
        qkv_kernel,
        "qkv_forward",
        [((tokens, 3 * width), bf16), ((BLOCKS, rows, 3 * width), bf16)],
        [SMEM, VMEM, VMEM] + [HBM] * 4,
        [VMEM] * 2,
        (table, x, bias, *pieces),
        6 * tokens * width * width,
        10e6,
        [pltpu.SemaphoreType.DMA((BLOCKS,))],
    )


def attention_kernel(buffers, qkv_ref, context_ref, lse_ref):
    tokens, width = context_ref.shape
    length, pairs = tokens // buffers, width // PAIR
    scale = 1.0 / math.sqrt(HEAD)

    def step(index, carry):
        rows = pl.ds(pl.multiple_of(index // pairs * length, length), length)
        lane = pl.multiple_of(index % pairs * PAIR, PAIR)
        query = qkv_ref[rows, pl.ds(lane, PAIR)]
        key = qkv_ref[rows, pl.ds(lane + width, PAIR)]
        value = qkv_ref[rows, pl.ds(lane + 2 * width, PAIR)]
        low = head_masks(query.shape)
        scores = mm_nt(key, stacked(query, low)) * scale
        peak = jnp.max(scores, axis=0, keepdims=True)
        powers = jnp.exp(scores - peak)
        total = jnp.sum(powers, axis=0, keepdims=True)
        probs = (powers * (1.0 / total)).astype(bf16)
        mixed = mm_tn(value, probs).T
        context_ref[rows, pl.ds(lane, PAIR)] = unstacked(mixed, low, length).astype(bf16)
        lse_ref[index] = peak + jnp.log(total)
        return carry

    lax.fori_loop(0, buffers * pairs, step, 0)


def attention_forward(qkv, buffers):
    tokens, width = qkv.shape[0], qkv.shape[1] // 3
    length = tokens // buffers
    lse = (buffers * (width // PAIR), 1, 2 * length)
    return call(
        functools.partial(attention_kernel, buffers),
        "attention_forward",
        [((tokens, width), bf16), (lse, f32)],
        [VMEM],
        [VMEM] * 2,
        (qkv,),
        4 * tokens * width * length,
        4e6,
        exps=tokens * length * width // HEAD,
    )


def normed_rows(residual):
    center = residual - row_mean(residual)
    inverse = lax.rsqrt(row_mean(center * center) + eps_norm)
    return center * inverse, inverse


def up_kernel(
    table_ref, x_ref, context_ref, vectors_ref, bias_ref, p0, p1, p2, p3,
    hidden_ref, act_ref, hidden_hbm, act_hbm, slope_hbm, normed_hbm, inverse_hbm, wout_hbm, wup_hbm,
    slope_ref, normed_ref, inverse_ref, wout_ref, wup_ref, sems_out, sems_up, sems,
):
    pieces = (p0, p1, p2, p3)
    width, units = x_ref.shape[1], wup_ref.shape[2]
    first = block_copies(table_ref, pieces, 0, width, wout_ref, sems_out)
    copies = block_copies(table_ref, pieces, width, units, wup_ref, sems_up)
    wait_all(first)
    out = mm(context_ref[...], flat(wout_ref[...])) + vectors_ref[0:1]
    normed, inverse = normed_rows(x_ref[...].astype(f32) + out)
    normed_ref[...] = normed
    inverse_ref[...] = jnp.broadcast_to(inverse, inverse_ref.shape)
    hidden_ref[...] = (normed * vectors_ref[1:2] + vectors_ref[2:3]).astype(bf16)
    wait_all(copies)
    pairs = [
        (wup_ref, wup_hbm),
        (wout_ref, wout_hbm),
        (normed_ref, normed_hbm),
        (inverse_ref, inverse_hbm),
        (hidden_ref, hidden_hbm),
    ]
    stores = fetch(pairs, sems)
    wide = 512
    for part in range(units // wide):
        span = pl.ds(part * wide, wide)
        up = mm(hidden_ref[...], flat(wup_ref[:, :, span])) + bias_ref[:, span]
        chance = 0.5 + 0.5 * lax.erf(up * math.sqrt(0.5))
        act_ref[:, span] = (up * chance).astype(bf16)
        density = jnp.exp(up * up * -0.5) * (1.0 / math.sqrt(2.0 * math.pi))
        slope_ref[:, span] = (chance + up * density).astype(bf16)
        pairs = [
            (act_ref.at[:, span], act_hbm.at[:, span]),
            (slope_ref.at[:, span], slope_hbm.at[:, span]),
        ]
        stores += fetch(pairs, sems, 5 + 2 * part)
    wait_all(stores)


def up_forward(table, x, context, vectors, bias, pieces):
    tokens, width = x.shape
    rows, units = pieces[0].shape[1], pieces[0].shape[2] - width
    now = [((tokens, width), bf16), ((tokens, units), bf16)]
    later = [
        ((tokens, units), bf16),
        ((tokens, width), f32),
        ((tokens, LINE), f32),
        ((BLOCKS, rows, width), bf16),
        ((BLOCKS, rows, units), bf16),
    ]
    return call(
        up_kernel,
        "up_forward",
        now + now + later,
        [SMEM] + [VMEM] * 4 + [HBM] * 4,
        [VMEM] * 2 + [HBM] * 7,
        (table, x, context, vectors, bias, *pieces),
        2 * tokens * width * (width + units),
        20e6,
        [pltpu.VMEM(*out) for out in later]
        + [pltpu.SemaphoreType.DMA((BLOCKS,)), pltpu.SemaphoreType.DMA((BLOCKS,))]
        + [pltpu.SemaphoreType.DMA((5 + 2 * (units // 512),))],
        exps=2 * tokens * units,
        limit=24,
    )


def chosen_row(owner_ref, vectors_ref, buffer):
    queries = vectors_ref[VECTORS:]
    query = lax.broadcasted_iota(jnp.int32, queries.shape, 0)
    return jnp.sum(jnp.where(query == owner_ref[buffer], queries, 0.0), axis=0, keepdims=True)


def down_kernel(
    buffers, table_ref, owner_ref, hidden_ref, act_ref, vectors_ref, tags_ref, p0, p1, p2, p3,
    mixed_ref, like_ref, normed_ref, sides_ref, wdown_ref, mixed_hbm, sems, sems_mixed,
):
    tokens = hidden_ref.shape[0]
    length = tokens // buffers
    wait_all(block_copies(table_ref, (p0, p1, p2, p3), 0, wdown_ref.shape[2], wdown_ref, sems))
    weight = flat(wdown_ref[...])
    stores = []
    for buffer in range(buffers):
        rows = rows_of(buffer, length)
        down = mm(act_ref[rows], weight) + vectors_ref[3:4]
        normed, inverse = normed_rows(hidden_ref[rows].astype(f32) + down)
        normed_ref[rows] = normed
        mixed = (normed * vectors_ref[4:5] + vectors_ref[5:6]).astype(bf16)
        mixed_ref[rows] = mixed
        span = pl.ds(buffer * length, length)
        stores += fetch([(mixed_ref.at[span], mixed_hbm.at[span])], sems_mixed, buffer)
        chosen = chosen_row(owner_ref, vectors_ref, buffer).astype(bf16)
        logits = mm_nt(jnp.broadcast_to(chosen, (8, chosen.shape[1])), mixed)[0:1]
        tags = tags_ref[buffer : buffer + 1].astype(f32)
        tail = jnp.log(1.0 + jnp.exp(-jnp.abs(logits)))
        log_yes = jnp.minimum(logits, 0.0) - tail
        log_no = jnp.minimum(-logits, 0.0) - tail
        like = jnp.sum(tags * log_yes + (1.0 - tags) * log_no, axis=1, keepdims=True) / length
        like_ref[buffer : buffer + 1] = jnp.broadcast_to(like, (1, LINE))
        pull = (tags - 1.0 / (1.0 + jnp.exp(-logits))) * (-loss_scale / length)
        pull = jnp.broadcast_to(pull, (LINE, length)).T
        lane = lax.broadcasted_iota(jnp.int32, (length, LINE), 1)
        sides_ref[rows] = jnp.where(lane < HEAD, inverse, pull)
    wait_all(stores)


def down_forward(table, owner, hidden, act, vectors, tags, pieces, buffers):
    tokens, width = hidden.shape
    rows, units = pieces[0].shape[1], act.shape[1]
    return call(
        functools.partial(down_kernel, buffers),
        "down_forward",
        [
            ((tokens, width), bf16),
            ((buffers, LINE), f32),
            ((tokens, width), f32),
            ((tokens, LINE), f32),
            ((BLOCKS, rows, width), bf16),
            ((tokens, width), bf16),
        ],
        [SMEM, SMEM] + [VMEM] * 4 + [HBM] * 4,
        [VMEM] * 5 + [HBM],
        (table, owner, hidden, act, vectors, tags, *pieces),
        2 * tokens * width * units,
        20e6,
        [pltpu.SemaphoreType.DMA((BLOCKS,)), pltpu.SemaphoreType.DMA((buffers,))],
    )


UP_SUM, GAIN_SUM, SHIFT_SUM, QUERY_SUM, DOWN_SUM = range(5)
ATTN_GAIN_SUM, ATTN_SHIFT_SUM, OUT_SUM = range(3)


def adder(sums_ref, buffers):
    def add_up(kind, buffer, value, start=0):
        row = kind * buffers + buffer
        sums_ref[row : row + 1, start : start + value.shape[1]] = jnp.sum(
            value, axis=0, keepdims=True
        )

    return add_up


def up_back_kernel(
    buffers, owner_ref, mixed_ref, normed_ref, sides_ref, slope_ref, vectors_ref, wdown_ref,
    low_ref, up_ref, res_ref, sums_ref,
):
    tokens, width = mixed_ref.shape
    units = slope_ref.shape[1]
    length = tokens // buffers
    sums_ref[...] = jnp.zeros_like(sums_ref)
    add_up = adder(sums_ref, buffers)
    for buffer in range(buffers):
        rows = rows_of(buffer, length)
        normed = normed_ref[rows]
        inverse, pull = sides_ref[rows, 0:1], sides_ref[rows, HEAD : HEAD + 1]
        chosen = chosen_row(owner_ref, vectors_ref, buffer)
        add_up(GAIN_SUM, buffer, pull * normed * chosen)
        add_up(SHIFT_SUM, buffer, pull * chosen)
        add_up(QUERY_SUM, buffer, pull * mixed_ref[rows].astype(f32))
        slope = chosen * vectors_ref[4:5]
        grad = (inverse * pull) * (slope - row_mean(slope) - normed * row_mean(slope * normed))
        res_ref[rows] = grad
        grad = grad.astype(bf16)
        low_ref[rows] = grad
        add_up(DOWN_SUM, buffer, grad.astype(f32))
    part = BLOCKS // 4
    wide = units // 4
    for k in range(4):
        span = slice(k * wide, (k + 1) * wide)
        grad = mm_nt(low_ref[...], flat(wdown_ref[k * part : (k + 1) * part]))
        grad = (grad * slope_ref[:, span].astype(f32)).astype(bf16)
        up_ref[:, span] = grad
        for buffer in range(buffers):
            add_up(UP_SUM, buffer, grad[rows_of(buffer, length)].astype(f32), k * wide)


def up_backward(owner, mixed, normed, sides, slope, vectors, wdown, buffers):
    tokens, width = mixed.shape
    units = slope.shape[1]
    return call(
        functools.partial(up_back_kernel, buffers),
        "up_backward",
        [
            ((tokens, width), bf16),
            ((tokens, units), bf16),
            ((tokens, width), f32),
            ((5 * buffers, units), f32),
        ],
        [SMEM] + [VMEM] * 6,
        [VMEM] * 4,
        (owner, mixed, normed, sides, slope, vectors, wdown),
        2 * tokens * width * units,
        20e6,
    )


def hidden_back_kernel(
    buffers, res_in_ref, up_ref, normed_ref, inverse_ref, vectors_ref, wup_ref, wout_ref,
    res_ref, attn_ref, context_ref, sums_ref,
):
    length = res_ref.shape[0] // buffers
    add_up = adder(sums_ref, buffers)
    weight, weight_out = flat(wup_ref[...]), flat(wout_ref[...])
    for buffer in range(buffers):
        rows = rows_of(buffer, length)
        normed = normed_ref[rows]
        grad = res_in_ref[rows] + mm_nt(up_ref[rows], weight)
        add_up(ATTN_GAIN_SUM, buffer, grad * normed)
        add_up(ATTN_SHIFT_SUM, buffer, grad)
        grad = grad * vectors_ref[1:2]
        grad = inverse_ref[rows, 0:1] * (
            grad - row_mean(grad) - normed * row_mean(grad * normed)
        )
        res_ref[rows] = grad
        grad = grad.astype(bf16)
        attn_ref[rows] = grad
        add_up(OUT_SUM, buffer, grad.astype(f32))
        context_ref[rows] = mm_nt(grad, weight_out).astype(bf16)


def hidden_backward(res, up, normed, inverse, vectors, wup, wout, buffers):
    tokens, width = res.shape
    return call(
        functools.partial(hidden_back_kernel, buffers),
        "hidden_backward",
        [
            ((tokens, width), f32),
            ((tokens, width), bf16),
            ((tokens, width), bf16),
            ((3 * buffers, width), f32),
        ],
        [VMEM] * 7,
        [VMEM] * 4,
        (res, up, normed, inverse, vectors, wup, wout),
        2 * tokens * width * (up.shape[1] + width),
        20e6,
    )


def scaled_rows(ref, scale_ref, buffers, span=slice(None)):
    length = ref.shape[0] // buffers
    return jnp.concatenate(
        [
            (ref[rows_of(b, length), span].astype(f32) * scale_ref[b]).astype(bf16)
            for b in range(buffers)
        ]
    )


def place_rows(table_ref, sums_ref, keep_ref, send_ref, start, width):
    rows = keep_ref.shape[1]
    for spot in range(BLOCKS):
        target = keep_ref if spot < HALF else send_ref
        block = pl.ds(pl.multiple_of(table_ref[spot] * rows, 8), rows)
        target[spot % HALF, :, start : start + width] = sums_ref[block, :width].astype(bf16)


def weight_kernel(buffers, count, table_ref, scale_ref, *refs):
    pairs = [refs[2 * k : 2 * k + 2] for k in range(count)]
    keep_ref, send_ref, sums_ref = refs[2 * count :]
    begin = 0
    for left_ref, right_ref in pairs:
        height, columns = left_ref.shape[1], right_ref.shape[1]
        tile = min(height, columns)
        for start in range(0, columns, tile):
            right = scaled_rows(right_ref, scale_ref, buffers, slice(start, start + tile))
            for row in range(0, height, tile):
                sums_ref[row : row + tile] = mm_tn(left_ref[:, row : row + tile], right)
            place_rows(table_ref, sums_ref, keep_ref, send_ref, begin + start, tile)
        begin += columns


def weight_gradient(name, table, scale, pairs, buffers):
    tokens, height = pairs[0][0].shape
    columns = [right.shape[1] for _, right in pairs]
    operands = [part for pair in pairs for part in pair]
    return call(
        functools.partial(weight_kernel, buffers, len(pairs)),
        name,
        [((HALF, height // BLOCKS, sum(columns)), bf16)] * 2,
        [SMEM, SMEM] + [VMEM] * len(operands),
        [VMEM] * 2,
        (table, scale, *operands),
        2 * tokens * height * sum(columns),
        10e6,
        [pltpu.VMEM((height, min(height, columns[0])), f32)],
        limit=LIMIT + 4 if height > 768 else LIMIT,
    )


def small_columns(
    buffers, count, scale_ref, owner_ref, sums_ref, attn_sums_ref, pre_ref, rows_ref, columns_ref, small_ref
):
    width = rows_ref.shape[1]
    rows = width // BLOCKS

    def weigh(ref, kind, columns=width):
        first = kind * buffers
        return sum(ref[first + b : first + b + 1, :columns] * scale_ref[b] for b in range(buffers))

    rows_ref[...] = jnp.zeros_like(rows_ref)
    kinds = [(attn_sums_ref, kind) for kind in (OUT_SUM, ATTN_GAIN_SUM, ATTN_SHIFT_SUM)]
    kinds += [(sums_ref, kind) for kind in (DOWN_SUM, GAIN_SUM, SHIFT_SUM)]
    for k, (ref, kind) in enumerate(kinds):
        rows_ref[k : k + 1] = weigh(ref, kind)
    pre = sum(pre_ref[b : b + 1] * scale_ref[b] for b in range(buffers))
    for at, total in ((QKV_AT, pre), (UP_AT, weigh(sums_ref, UP_SUM, sums_ref.shape[1]))):
        for k in range(total.shape[1] // width):
            rows_ref[at + k : at + k + 1] = total[:, k * width : (k + 1) * width]
    query = lax.broadcasted_iota(jnp.int32, (count, width), 0)
    total = jnp.zeros((count, width), f32)
    for b in range(buffers):
        row = QUERY_SUM * buffers + b
        mine = sums_ref[row : row + 1, :width] * scale_ref[b]
        total += jnp.where(query == owner_ref[b], mine, 0.0)
    rows_ref[QUERY_AT : QUERY_AT + count] = total
    columns_ref[...] = rows_ref[...].T
    lane = lax.broadcasted_iota(jnp.int32, (rows, LINE), 1)
    for block in range(BLOCKS):
        value = columns_ref[block * rows : (block + 1) * rows]
        for at, per in ((QKV_AT, 2), (UP_AT, 4)):
            for c in range(per):
                spot = (block * per + c) * rows
                source = columns_ref[spot % width : spot % width + rows]
                shift = (c - spot // width) % LINE
                if shift:
                    source = pltpu.roll(source, shift, 1)
                value = jnp.where(lane == at + c, source, value)
        small_ref[block * rows : (block + 1) * rows] = value


def attention_back_kernel(buffers, qkv_ref, lse_ref, grad_ref, pre_ref, bias_ref):
    tokens, width = grad_ref.shape
    length, pairs = tokens // buffers, width // PAIR
    scale = 1.0 / math.sqrt(HEAD)

    def step(index, carry):
        rows = pl.ds(pl.multiple_of(index // pairs * length, length), length)
        lane = pl.multiple_of(index % pairs * PAIR, PAIR)
        query = qkv_ref[rows, pl.ds(lane, PAIR)]
        key = qkv_ref[rows, pl.ds(lane + width, PAIR)]
        value = qkv_ref[rows, pl.ds(lane + 2 * width, PAIR)]
        low = head_masks(query.shape)
        query = stacked(query, low)
        grad = stacked(grad_ref[rows, pl.ds(lane, PAIR)], low)
        probs = jnp.exp(mm_nt(key, query) * scale - lse_ref[index])
        grad_probs = mm_nt(value, grad)
        cross = jnp.sum(grad_probs * probs, axis=0, keepdims=True)
        grad_scores = (probs * (grad_probs - cross)).astype(bf16)
        grad_value = mm(probs.astype(bf16), grad)
        grad_key = mm(grad_scores, query) * scale
        grad_query = unstacked(mm_tn(key, grad_scores).T, low, length) * scale
        pre_ref[rows, pl.ds(lane, PAIR)] = grad_query.astype(bf16)
        pre_ref[rows, pl.ds(lane + width, PAIR)] = grad_key.astype(bf16)
        pre_ref[rows, pl.ds(lane + 2 * width, PAIR)] = grad_value.astype(bf16)
        return carry

    lax.fori_loop(0, buffers * pairs, step, 0)
    for buffer in range(buffers):
        rows = rows_of(buffer, length)
        for start, source in ((0, 0), (width, 2 * width)):
            piece = pre_ref[rows, source : source + width].astype(f32)
            bias_ref[buffer : buffer + 1, start : start + width] = jnp.sum(
                piece, axis=0, keepdims=True
            )


def attention_backward(qkv, lse, grad, buffers):
    tokens, width = grad.shape
    length = tokens // buffers
    return call(
        functools.partial(attention_back_kernel, buffers),
        "attention_backward",
        [((tokens, 3 * width), bf16), ((buffers, 2 * width), f32)],
        [VMEM] * 3,
        [VMEM] * 2,
        (qkv, lse, grad),
        10 * tokens * length * width,
        7e6,
        exps=tokens * length * width // HEAD,
    )


def qkv_gradient_kernel(
    buffers, count, table_ref, scale_ref, owner_ref, x_ref, pre_ref, bias_ref, sums_in_ref, attn_sums_ref,
    keep_ref, send_ref, sums_ref, rows_ref, columns_ref, small_ref,
):
    width = x_ref.shape[1]
    for part in range(3):
        right = scaled_rows(pre_ref, scale_ref, buffers, slice(part * width, (part + 1) * width))
        sums_ref[...] = mm_tn(x_ref[...], right)
        place_rows(table_ref, sums_ref, keep_ref, send_ref, part * width, width)
    small_columns(
        buffers, count, scale_ref, owner_ref, sums_in_ref, attn_sums_ref, bias_ref,
        rows_ref, columns_ref, small_ref,
    )
    place_rows(table_ref, small_ref, keep_ref, send_ref, 3 * width, LINE)


def qkv_gradient(table, scale, owner, count, x, pre, pre_sums, sums, attn_sums, buffers):
    tokens, width = x.shape
    blocks = ((HALF, width // BLOCKS, 3 * width + LINE), bf16)
    return call(
        functools.partial(qkv_gradient_kernel, buffers, count),
        "qkv_gradient",
        [blocks, blocks],
        [SMEM] * 3 + [VMEM] * 5,
        [VMEM] * 2,
        (table, scale, owner, x, pre, pre_sums, sums, attn_sums),
        6 * tokens * width * width,
        10e6,
        [
            pltpu.VMEM((width, width), f32),
            pltpu.VMEM((LINE, width), f32),
            pltpu.VMEM((width, LINE), f32),
            pltpu.VMEM((width, LINE), f32),
        ],
    )


def states_kernel(buffers, scale_ref, res_ref, pre_ref, weight_ref, out_ref):
    length = res_ref.shape[0] // buffers
    weight = flat(weight_ref[...])
    for buffer in range(buffers):
        rows = rows_of(buffer, length)
        grad = res_ref[rows] + mm_nt(pre_ref[rows], weight)
        out_ref[rows] = (grad * scale_ref[buffer]).astype(bf16)


def states_gradient(scale, res, pre, weight, buffers):
    tokens, width = res.shape
    return call(
        functools.partial(states_kernel, buffers),
        "states_gradient",
        [((tokens, width), bf16)],
        [SMEM] + [VMEM] * 3,
        [VMEM],
        (scale, res, pre, weight),
        6 * tokens * width * width,
        8e6,
    )[0]


def body(
    slot_states, answer_tags, slot_mask, retrieval, query_emb, qkv_weight, qkv_bias, out_weight,
    out_bias, attn_gain, attn_shift, up_weight, up_bias, down_weight, down_bias, ffn_gain, ffn_shift,
):
    group_count = lax.axis_size(AXES)
    device_index = lax.axis_index(AXES)
    tuned = group_count == BLOCKS
    buffers, length, width = slot_states.shape
    query_count, slot_count = slot_mask.shape
    tokens = buffers * length
    x = slot_states.reshape(tokens, width)

    running = jnp.cumsum(slot_mask.reshape(-1), dtype=jnp.int32)
    slot_ranks = jnp.arange(buffers, dtype=jnp.int32) * group_count + device_index
    places = jnp.sum(
        (running[None, :] <= slot_ranks[:, None]).astype(jnp.int32), axis=1, dtype=jnp.int32
    )
    slot_pick = places[:, None] == jnp.arange(query_count * slot_count, dtype=jnp.int32)[None, :]
    owner = places // slot_count
    owner_mask = owner[:, None] == jnp.arange(query_count, dtype=jnp.int32)[None]
    prior_score = jnp.sum(jnp.where(slot_pick, retrieval.reshape(-1)[None, :], 0.0), axis=1)

    order = Order(tuned)
    if tuned:
        table = position_table(device_index)
        vectors = (out_bias, attn_gain, attn_shift, down_bias, ffn_gain, ffn_shift)
        g1 = Gather(order, pack_first(qkv_weight, vectors, qkv_bias, up_bias, query_emb))
        g2 = Gather(order, jnp.concatenate([out_weight, up_weight], axis=1)[None])
        g3 = Gather(order, down_weight[None])
        g1.start_line()
        g1.join()
        g1.start(SIDE)
        g2.start_line(g1.held)
        g1.join()
        g1.start(OTHER)
        owner = order.place(owner)
        prior_score = order.place(prior_score)
        g2.join()
        g3.start_line(g2.held)
        g1.start_cores()
        g2.start(SIDE, g1.last)
        first = g1.pieces()
        vectors, bias, up_bias_all = unpack_small(table, first, 3 * width, query_count)
    else:
        table = jnp.arange(BLOCKS, dtype=jnp.int32)
        everything = lambda part: lax.all_gather(part, AXES, axis=0, tiled=True).astype(f32)
        first = gather_plain(qkv_weight)
        second = gather_plain(jnp.concatenate([out_weight, up_weight], axis=1))
        third = gather_plain(down_weight)
        vectors = jnp.stack(
            [
                everything(part)
                for part in (out_bias, attn_gain, attn_shift, down_bias, ffn_gain, ffn_shift)
            ]
        )
        bias = everything(qkv_bias)
        bias = jnp.concatenate([bias[:width], jnp.zeros((width,), f32), bias[width:]]).reshape(1, -1)
        up_bias_all = everything(up_bias).reshape(1, -1)
        query_table = lax.all_gather(query_emb, AXES, axis=1, tiled=True).astype(f32)
        vectors = jnp.concatenate([vectors, jnp.zeros((VECTORS - SIX, width), f32), query_table])

    qkv, wqkv = qkv_forward(table, x, bias, first)
    if tuned:
        order.mark(qkv)
        g2.join()
        g2.start(OTHER)
        g3.join()
        g3.start(SIDE)
    context, lse = attention_forward(order.place(qkv), buffers)
    if tuned:
        order.mark(context)
        g2.start_cores()
        g3.join()
        g3.start(OTHER)
        second = g2.pieces()
    hidden, act, hidden_late, act_late, slope, normed, inverse, wout, wup = up_forward(
        table, x, context, vectors, up_bias_all, second
    )
    if tuned:
        order.mark(act)
        g3.start_cores()
        third = g3.pieces()
    mixed, like, normed_out, sides, wdown, mixed_out = down_forward(
        table, owner, hidden, act, vectors, answer_tags, third, buffers
    )

    scores = like[:, 0] + prior_score
    masked = jnp.where(owner_mask, scores[:, None], neg_fill)
    local_peak = jnp.max(masked, axis=0)
    local_total = jnp.sum(jnp.where(owner_mask, jnp.exp(masked - local_peak[None, :]), 0.0), axis=0)
    merged = (local_peak, local_total)
    if tuned:
        order.mark(local_total)
        merged = merge_join(order, merged, merge_start(merged, CORE_BIT))
        got = merge_start(merged, Z_FAR)
    else:
        merged = merge_plain(merged)

    grad_low, grad_up, grad_res, sums = up_backward(
        owner, order.place(mixed), normed_out, sides, slope, vectors, wdown, buffers
    )
    if tuned:
        order.mark(grad_low)
        merged = merge_join(order, merged, got)
        got = merge_start(merged, X_BIT)
    grad_hidden, grad_attn, grad_context, attn_sums = hidden_backward(
        order.place(grad_res), grad_up, normed, inverse, vectors, wup, wout, buffers
    )
    if tuned:
        order.mark(grad_attn)
        merged = merge_join(order, merged, got)
        got = merge_start(merged, Y_BIT)
    grad_pre, pre_sums = attention_backward(qkv, lse, order.place(grad_context), buffers)
    if tuned:
        order.mark(pre_sums)
        merged = merge_join(order, merged, got)
        merged = merge_join(order, merged, merge_start(merged, Z_NEAR))
    totals = merged[0] + jnp.log(merged[1])
    loss = -jnp.sum(totals)
    scale = jnp.sum(
        jnp.where(owner_mask, jnp.exp(scores[:, None] - totals[None, :]), 0.0), axis=1
    )

    halves3 = weight_gradient("down_gradient", table, scale, [(act_late, grad_low)], buffers)
    if tuned:
        order.mark(halves3[1])
        s3 = Scatter(order, *halves3)
        s3.start(CORES)
        s3.join()
        s3.start(OTHER)
    pairs = [(context, grad_attn), (order.place(hidden_late), grad_up)]
    halves2 = weight_gradient("up_gradient", table, scale, pairs, buffers)
    if tuned:
        order.mark(halves2[1])
        s2 = Scatter(order, *halves2)
        s2.start(CORES)
    halves1 = qkv_gradient(
        table, scale, owner, query_count, x, order.place(grad_pre), pre_sums, sums, attn_sums, buffers
    )
    if tuned:
        order.mark(halves1[1])
        s1 = Scatter(order, *halves1)
        s1.start(CORES)
        s2.join()
        s2.start(OTHER)
        s3.join()
        s3.start(SIDE)
    states = states_gradient(scale, grad_hidden, order.place(grad_pre), wqkv, buffers)
    if tuned:
        order.mark(states)
        s1.join()
        s1.start(OTHER)
        s3.start_line()
        s2.join()
        s2.start(SIDE)
        s1.join()
        s1.start(SIDE)
        third_grad = s3.finish()
        order.mark(third_grad)
        s2.start_line()
        s1.start_line()
        second_grad = s2.finish(0, width), s2.finish(width)
        order.mark(second_grad[1])
        first_grad = s1.finish(0, 3 * width)
        small = s1.finish(3 * width)
    else:
        third_grad = scatter_plain(*halves3)
        cut = lambda halves, start, end: scatter_plain(*(half[:, :, start:end] for half in halves))
        second_grad = cut(halves2, 0, width), cut(halves2, width, width + up_weight.shape[1])
        first_grad = cut(halves1, 0, 3 * width)
    if tuned:
        *six, qkv_bias_sum, up_bias_sum, query_sum = split_small(
            small, query_count
        )
    else:
        weigh = lambda part: jnp.sum(scale[:, None] * part, axis=0)
        mine = lambda part: lax.psum_scatter(weigh(part), AXES, scatter_dimension=0, tiled=True)
        rows_for = lambda part, kind: part[kind * buffers : (kind + 1) * buffers, :width]
        six = [mine(rows_for(attn_sums, kind)) for kind in (OUT_SUM, ATTN_GAIN_SUM, ATTN_SHIFT_SUM)]
        six += [mine(rows_for(sums, kind)) for kind in (DOWN_SUM, GAIN_SUM, SHIFT_SUM)]
        qkv_bias_sum, up_bias_sum = mine(pre_sums), mine(sums[:buffers])
        weighed = jnp.where(owner_mask, scale[:, None], 0.0)
        query_sum = jnp.sum(weighed[:, :, None] * rows_for(sums, QUERY_SUM)[:, None, :], axis=0)
        query_sum = lax.psum_scatter(query_sum, AXES, scatter_dimension=1, tiled=True)
    return (
        mixed_out.reshape(slot_states.shape),
        loss,
        states.reshape(slot_states.shape),
        query_sum,
        first_grad,
        qkv_bias_sum,
        second_grad[0],
        six[0],
        six[1],
        six[2],
        second_grad[1],
        up_bias_sum,
        third_grad,
        six[3],
        six[4],
        six[5],
    )


def solution(mesh):
    split = P(AXES)
    in_specs = (split, split, P(), P(), P(None, AXES)) + (split,) * 12
    out_specs = (split, P(), split, P(None, AXES)) + (split,) * 12
    return jax.shard_map(body, mesh=mesh, in_specs=in_specs, out_specs=out_specs, check_vma=False)
```

```python
import functools
import math

import jax
import jax.numpy as jnp
import numpy as np
from jax import lax
from jax.experimental import pallas as pl
from jax.experimental.pallas import tpu as pltpu
from jax.sharding import PartitionSpec as P

HEAD = 64
PAIR = 2 * HEAD
LINE = 128
AXES = ("dp", "fsdp")
X_BIT, CORE_BIT, Z_FAR, Z_NEAR, Y_BIT = 16, 8, 4, 2, 1
BLOCKS = 32
HALF = BLOCKS // 2
SHARE = 0.02
LIMIT = 12

eps_norm = 1e-12
loss_scale = 65536.0
neg_fill = -1e30
f32 = jnp.float32
bf16 = jnp.bfloat16
VMEM = pl.BlockSpec(memory_space=pltpu.VMEM)
SMEM = pl.BlockSpec(memory_space=pltpu.SMEM)
HBM = pl.BlockSpec(memory_space=pltpu.HBM)


def device_offsets(first, second):
    masks = (Z_FAR, Z_NEAR, first, second)
    return np.array(
        [sum(m for k, m in enumerate(masks) if p >> k & 1) for p in range(HALF)], np.int32
    )


def position_table(device_index):
    even = device_offsets(X_BIT, Y_BIT)
    odd = device_offsets(Y_BIT, X_BIT)
    table_even = jnp.asarray(np.concatenate([even, odd ^ CORE_BIT]))
    table_odd = jnp.asarray(np.concatenate([odd, even ^ CORE_BIT]))
    core = (device_index // CORE_BIT) % 2
    return jnp.where(core == 0, table_even, table_odd) ^ device_index


def exchange(value, even_mask, odd_mask):
    pairs = [(i, i ^ (odd_mask if i & CORE_BIT else even_mask)) for i in range(BLOCKS)]
    return lax.ppermute(value, AXES, pairs)


def after(value, *earlier):
    return lax.optimization_barrier((value, *earlier))[0]


SIDE, OTHER, CORES = (X_BIT, Y_BIT), (Y_BIT, X_BIT), (CORE_BIT, CORE_BIT)
LINE_MASKS = (Z_FAR, Z_NEAR, Z_FAR | Z_NEAR)


class Order:
    def __init__(self, tuned):
        self.tuned, self.last = tuned, None

    def place(self, value):
        if self.tuned and self.last is not None:
            return after(value, self.last)
        return value

    def mark(self, value):
        self.last = value


class Gather:
    def __init__(self, order, shard):
        self.order, self.shard = order, shard

    def start_line(self, *earlier):
        own = after(self.shard, *earlier) if earlier else self.shard
        self.got = [exchange(own, mask, mask) for mask in LINE_MASKS]

    def join_line(self):
        got = [self.order.place(part) for part in self.got]
        self.held = lax.optimization_barrier(jnp.concatenate([self.shard, *got]))
        self.order.mark(self.held)

    def start_near(self, *earlier):
        held = after(self.held, *earlier) if earlier else self.held
        self.near = exchange(held, *SIDE)

    def start_other(self, *earlier):
        held = after(self.held, *earlier) if earlier else self.held
        self.other = exchange(held, *OTHER)
        self.far_held = exchange(held, *CORES)

    def join_near(self):
        self.near = self.order.place(self.near)
        self.order.mark(self.near)
        self.last = exchange(self.near, *OTHER)
        self.far_near = exchange(self.near, *CORES)

    def join_other(self):
        self.other = self.order.place(self.other)
        self.order.mark(self.other)
        self.far_other = exchange(self.other, *CORES)

    def join_last(self):
        self.last = self.order.place(self.last)
        self.order.mark(self.last)
        self.far_last = exchange(self.last, *CORES)

    def pieces(self):
        far = (self.far_held, self.far_near, self.far_other, self.far_last)
        far = [self.order.place(part) for part in far]
        self.order.mark(far[-1])
        return (self.held, self.near, self.other, self.last, *far)


def gather_plain(part):
    whole = lax.all_gather(part, AXES, axis=0, tiled=True)
    blocks = whole.reshape(BLOCKS, -1, whole.shape[1])
    return tuple(blocks[4 * k : 4 * k + 4] for k in range(8))


def add_low(first, second):
    return (first.astype(f32) + second.astype(f32)).astype(bf16)


def add_up_parts(*parts):
    return sum(part.astype(f32) for part in parts)


class Scatter:
    def __init__(self, order, keep, send):
        self.order, self.keep, self.send = order, keep, send

    def start_core(self, *earlier):
        self.got = exchange(after(self.send, *earlier) if earlier else self.send, *CORES)

    def quarter(self, k, *more):
        span = slice(4 * k, 4 * k + 4)
        return add_up_parts(self.keep[span], self.got[span], *more)

    def join_core(self):
        self.got = self.order.place(self.got)
        last, other = self.quarter(3).astype(bf16), self.quarter(2).astype(bf16)
        self.last = exchange(last, *OTHER)
        self.other = other
        self.order.mark(other)

    def start_other(self, *earlier):
        other = after(self.other, *earlier) if earlier else self.other
        self.other = exchange(other, *OTHER)

    def join_last(self):
        near = self.quarter(1, self.order.place(self.last)).astype(bf16)
        self.near = exchange(near, *SIDE)
        self.order.mark(near)

    def join_sides(self):
        more = self.order.place(self.other), self.order.place(self.near)
        block = lambda p: add_up_parts(self.keep[p], self.got[p], more[0][p], more[1][p])
        sends = [block(p).astype(bf16) for p in (1, 2, 3)]
        self.line = [exchange(part, mask, mask) for part, mask in zip(sends, LINE_MASKS)]
        self.own = block(0)
        self.order.mark(sends[-1])

    def finish(self, start=0, width=None):
        end = self.own.shape[1] if width is None else start + width
        cut = lambda part: part[..., start:end]
        return add_up_parts(cut(self.own), *(cut(self.order.place(part)) for part in self.line))


def scatter_plain(keep, send):
    blocks = jnp.concatenate([keep, send])
    whole = blocks.reshape(-1, blocks.shape[2])
    return lax.psum_scatter(whole, AXES, scatter_dimension=0, tiled=True).astype(f32)


def merge_start(pair, masks):
    both = jnp.stack(pair)
    return [exchange(both, mask, mask) for mask in masks]


def merge_join(order, pair, got):
    got = [order.place(part) for part in got]
    peak = functools.reduce(jnp.maximum, [part[0] for part in got], pair[0])
    total = pair[1] * jnp.exp(pair[0] - peak)
    total += sum(part[1] * jnp.exp(part[0] - peak) for part in got)
    order.mark(total)
    return (peak, total)


def merge_plain(pair):
    peak = lax.pmax(pair[0], AXES)
    return (peak, lax.psum(pair[1] * jnp.exp(pair[0] - peak), AXES))


def call(
    kernel, name, outs, in_specs, out_specs, args, flops, moved, scratch=(), exps=0, limit=None
):
    args = [
        pltpu.with_memory_space_constraint(arg, pltpu.HBM) if spec is HBM else arg
        for arg, spec in zip(args, in_specs)
    ]
    return pl.pallas_call(
        kernel,
        out_shape=[
            pltpu.HBM(shape, dtype) if spec is HBM else jax.ShapeDtypeStruct(shape, dtype)
            for (shape, dtype), spec in zip(outs, out_specs)
        ],
        in_specs=in_specs,
        out_specs=out_specs,
        scratch_shapes=list(scratch),
        compiler_params=pltpu.CompilerParams(vmem_limit_bytes=(limit or LIMIT) * 2**20),
        cost_estimate=pl.CostEstimate(
            flops=int(flops * SHARE), bytes_accessed=int(moved * SHARE), transcendentals=int(exps * SHARE)
        ),
        name=name,
    )(*args)


def mm(first, second):
    return jnp.dot(first, second, preferred_element_type=f32)


def mm_nt(first, second):
    return lax.dot_general(first, second, (((1,), (1,)), ((), ())), preferred_element_type=f32)


def mm_tn(first, second):
    return lax.dot_general(first, second, (((0,), (0,)), ((), ())), preferred_element_type=f32)


def row_mean(value):
    return jnp.mean(value, axis=-1, keepdims=True)


def block_copies(table_ref, pieces, start, width, target, sems):
    copies = [
        pltpu.make_async_copy(
            pieces[spot // 4].at[spot % 4, :, pl.ds(start, width)],
            target.at[table_ref[spot]],
            sems.at[spot],
        )
        for spot in range(BLOCKS)
    ]
    for copy in copies:
        copy.start()
    return copies


def fetch(pairs, sems, first=0):
    copies = [
        pltpu.make_async_copy(source, target, sems.at[first + k])
        for k, (source, target) in enumerate(pairs)
    ]
    for copy in copies:
        copy.start()
    return copies


def wait_all(copies):
    for copy in copies:
        copy.wait()


def flat(value):
    return value.reshape(-1, value.shape[-1])


SIX, QKV_AT, UP_AT, QUERY_AT = 6, 6, 8, 12
VECTORS = 8


def pack_kernel(weight_hbm, *refs):
    sources, out_ref, parts, held_ref, sems = refs[: SIX + 3], refs[SIX + 3], refs[SIX + 4 : -2], *refs[-2:]
    rows, width = out_ref.shape[1], out_ref.shape[2] - LINE
    copies = fetch(zip(sources, parts), sems)
    copies += fetch([(weight_hbm, out_ref.at[0, :, pl.ds(0, width)])], sems, len(parts))
    vectors, (qkv_ref, up_ref, query_ref) = parts[:SIX], parts[SIX:]
    held_ref[...] = jnp.zeros_like(held_ref)
    wait_all(copies)
    for k, ref in enumerate(vectors):
        held_ref[k : k + 1, :rows] = ref[...].astype(f32)
    for at, ref, count in ((QKV_AT, qkv_ref, 2), (UP_AT, up_ref, 4)):
        value = ref[...].astype(f32)
        for c in range(count):
            held_ref[at + c : at + c + 1, :rows] = value[:, c * rows : (c + 1) * rows]
    count = query_ref.shape[0]
    held_ref[QUERY_AT : QUERY_AT + count, :rows] = query_ref[...].astype(f32)
    out_ref[0, :, width:] = held_ref[...].T[:rows].astype(bf16)


def pack_first(weight, vectors, qkv_bias, up_bias, query_emb):
    rows, width = weight.shape
    parts = [part.reshape(1, -1) for part in (*vectors, qkv_bias, up_bias)] + [query_emb]
    return call(
        pack_kernel,
        "pack_first",
        [((1, rows, width + LINE), bf16)],
        [HBM] * (1 + len(parts)),
        [VMEM],
        [weight, *parts],
        0,
        1e5,
        [pltpu.VMEM(part.shape, part.dtype) for part in parts]
        + [pltpu.VMEM((LINE, LINE), f32), pltpu.SemaphoreType.DMA((len(parts) + 1,))],
    )[0]


def unpack_kernel(
    start, count, table_ref, p0, p1, p2, p3, p4, p5, p6, p7, consts_ref, qkv_ref, up_ref,
    held_ref, qkv_wide, up_wide, sems,
):
    wait_all(block_copies(table_ref, (p0, p1, p2, p3, p4, p5, p6, p7), start, LINE, held_ref, sems))
    rows = held_ref.shape[1]
    every = flat(held_ref[...]).astype(f32)
    for block in range(BLOCKS):
        value = every[block * rows : (block + 1) * rows]
        for c in range(2):
            qkv_wide[(2 * block + c) * rows : (2 * block + c + 1) * rows] = value
        for c in range(4):
            up_wide[(4 * block + c) * rows : (4 * block + c + 1) * rows] = value
    turned = every.T
    consts_ref[:VECTORS] = turned[:VECTORS]
    consts_ref[VECTORS:] = turned[QUERY_AT : QUERY_AT + count]

    def line(wide, at, count):
        picks = lax.broadcasted_iota(jnp.int32, (8, LINE), 1) == at + lax.broadcasted_iota(
            jnp.int32, (8, LINE), 0
        )
        found = mm_nt(picks.astype(bf16), wide[...].astype(bf16))
        part = lax.broadcasted_iota(jnp.int32, found.shape, 1) // rows % count
        mine = part == lax.broadcasted_iota(jnp.int32, found.shape, 0)
        return jnp.sum(jnp.where(mine, found, 0.0), axis=0, keepdims=True)

    up_ref[...] = line(up_wide, UP_AT, 4)
    width = held_ref.shape[0] * rows
    bias = line(qkv_wide, QKV_AT, 2)
    qkv_ref[:, :width] = bias[:, :width]
    qkv_ref[:, width : 2 * width] = jnp.zeros((1, width), f32)
    qkv_ref[:, 2 * width :] = bias[:, width:]


def unpack_small(table, pieces, start, query_count):
    rows = pieces[0].shape[1]
    width = BLOCKS * rows
    return call(
        functools.partial(unpack_kernel, start, query_count),
        "unpack_small",
        [((VECTORS + query_count, width), f32), ((1, 3 * width), f32), ((1, 4 * width), f32)],
        [SMEM] + [HBM] * 8,
        [VMEM] * 3,
        (table, *pieces),
        0,
        1e6,
        [
            pltpu.VMEM((BLOCKS, rows, LINE), bf16),
            pltpu.VMEM((2 * width, LINE), f32),
            pltpu.VMEM((4 * width, LINE), f32),
            pltpu.SemaphoreType.DMA((BLOCKS,)),
        ],
    )


def split_kernel(own_ref, g0_ref, g1_ref, g2_ref, first_ref, *refs):
    vectors, (qkv_ref, up_ref, query_ref, held_ref) = refs[:SIX], refs[SIX:]
    rows, width = first_ref.shape
    total = own_ref[...] + (
        g0_ref[...].astype(f32) + g1_ref[...].astype(f32) + g2_ref[...].astype(f32)
    )
    first_ref[...] = total[:, :width]
    held_ref[...] = jnp.zeros_like(held_ref)
    held_ref[:rows] = total[:, width:]
    turned = held_ref[...].T
    for k, ref in enumerate(vectors):
        ref[...] = turned[k : k + 1, :rows]
    for c in range(2):
        qkv_ref[:, c * rows : (c + 1) * rows] = turned[QKV_AT + c : QKV_AT + c + 1, :rows]
    for c in range(4):
        up_ref[:, c * rows : (c + 1) * rows] = turned[UP_AT + c : UP_AT + c + 1, :rows]
    query_ref[...] = turned[QUERY_AT : QUERY_AT + query_ref.shape[0], :rows]


def split_first(own, got, query_count):
    rows, width = own.shape[0], own.shape[1] - LINE
    outs = call(
        split_kernel,
        "split_first",
        [((rows, width), f32)]
        + [((1, rows), f32)] * SIX
        + [((1, 2 * rows), f32), ((1, 4 * rows), f32), ((query_count, rows), f32)],
        [VMEM] * 4,
        [VMEM] * (SIX + 4),
        (own, *got),
        0,
        1e6,
        [pltpu.VMEM((LINE, LINE), f32)],
    )
    return [outs[0]] + [part.reshape(-1) for part in outs[1:-1]] + [outs[-1]]


def block_scratch(rows, width):
    return [pltpu.VMEM((BLOCKS, rows, width), bf16), pltpu.SemaphoreType.DMA((BLOCKS,))]


def head_masks(shape):
    lane = lax.broadcasted_iota(jnp.int32, shape, 1)
    return lane < HEAD


def stacked(pair, low):
    zero = jnp.zeros_like(pair)
    return jnp.concatenate([jnp.where(low, pair, zero), jnp.where(low, zero, pair)])


def unstacked(value, low, length):
    return jnp.where(low, value[:length], value[length:])


def rows_of(buffer, length):
    return slice(buffer * length, (buffer + 1) * length)


def rows_of(buffer, length):
    return slice(buffer * length, (buffer + 1) * length)


def qkv_kernel(
    table_ref, x_ref, bias_ref, p0, p1, p2, p3, p4, p5, p6, p7, qkv_ref, weight_hbm, weight_ref, sems, sems_out
):
    width = x_ref.shape[1]
    wait_all(block_copies(table_ref, (p0, p1, p2, p3, p4, p5, p6, p7), 0, 3 * width, weight_ref, sems))
    stores = fetch([(weight_ref, weight_hbm)], sems_out)
    x = x_ref[...]
    for part in range(3):
        span = slice(part * width, (part + 1) * width)
        weight = flat(weight_ref[:, :, span])
        qkv_ref[:, span] = (mm(x, weight) + bias_ref[:, span]).astype(bf16)
    wait_all(stores)


def qkv_forward(table, x, bias, pieces):
    tokens, width = x.shape
    rows = pieces[0].shape[1]
    return call(
        qkv_kernel,
        "qkv_forward",
        [((tokens, 3 * width), bf16), ((BLOCKS, rows, 3 * width), bf16)],
        [SMEM, VMEM, VMEM] + [HBM] * 8,
        [VMEM, HBM],
        (table, x, bias, *pieces),
        6 * tokens * width * width,
        10e6,
        block_scratch(rows, 3 * width) + [pltpu.SemaphoreType.DMA((1,))],
    )


def attention_kernel(buffers, qkv_ref, context_ref, lse_ref):
    tokens, width = context_ref.shape
    length, pairs = tokens // buffers, width // PAIR
    scale = 1.0 / math.sqrt(HEAD)

    def step(index, carry):
        rows = pl.ds(pl.multiple_of(index // pairs * length, length), length)
        lane = pl.multiple_of(index % pairs * PAIR, PAIR)
        query = qkv_ref[rows, pl.ds(lane, PAIR)]
        key = qkv_ref[rows, pl.ds(lane + width, PAIR)]
        value = qkv_ref[rows, pl.ds(lane + 2 * width, PAIR)]
        low = head_masks(query.shape)
        scores = mm_nt(key, stacked(query, low)) * scale
        peak = jnp.max(scores, axis=0, keepdims=True)
        powers = jnp.exp(scores - peak)
        total = jnp.sum(powers, axis=0, keepdims=True)
        probs = (powers * (1.0 / total)).astype(bf16)
        mixed = mm_tn(value, probs).T
        context_ref[rows, pl.ds(lane, PAIR)] = unstacked(mixed, low, length).astype(bf16)
        lse_ref[index] = peak + jnp.log(total)
        return carry

    lax.fori_loop(0, buffers * pairs, step, 0, unroll=2)


def attention_forward(qkv, buffers):
    tokens, width = qkv.shape[0], qkv.shape[1] // 3
    length = tokens // buffers
    lse = (buffers * (width // PAIR), 1, 2 * length)
    return call(
        functools.partial(attention_kernel, buffers),
        "attention_forward",
        [((tokens, width), bf16), (lse, f32)],
        [VMEM],
        [VMEM] * 2,
        (qkv,),
        4 * tokens * width * length,
        4e6,
        exps=tokens * length * width // HEAD,
    )


def normed_rows(residual):
    center = residual - row_mean(residual)
    inverse = lax.rsqrt(row_mean(center * center) + eps_norm)
    return center * inverse, inverse


def up_kernel(
    table_ref, x_ref, context_ref, vectors_ref, bias_ref, p0, p1, p2, p3, p4, p5, p6, p7,
    hidden_hbm, act_hbm, slope_hbm, normed_hbm, inverse_hbm, wout_hbm, wup_hbm,
    hidden_ref, act_ref, slope_ref, normed_ref, inverse_ref, wout_ref, wup_ref, sems_out, sems_up, sems,
):
    pieces = (p0, p1, p2, p3, p4, p5, p6, p7)
    width, units = x_ref.shape[1], wup_ref.shape[2]
    first = block_copies(table_ref, pieces, 0, width, wout_ref, sems_out)
    copies = block_copies(table_ref, pieces, width, units, wup_ref, sems_up)
    wait_all(first)
    out = mm(context_ref[...], flat(wout_ref[...])) + vectors_ref[0:1]
    normed, inverse = normed_rows(x_ref[...].astype(f32) + out)
    normed_ref[...] = normed
    inverse_ref[...] = jnp.broadcast_to(inverse, inverse_ref.shape)
    hidden_ref[...] = (normed * vectors_ref[1:2] + vectors_ref[2:3]).astype(bf16)
    wait_all(copies)
    pairs = [
        (wup_ref, wup_hbm),
        (wout_ref, wout_hbm),
        (normed_ref, normed_hbm),
        (inverse_ref, inverse_hbm),
        (hidden_ref, hidden_hbm),
    ]
    stores = fetch(pairs, sems)
    wide = 512
    for part in range(units // wide):
        span = pl.ds(part * wide, wide)
        up = mm(hidden_ref[...], flat(wup_ref[:, :, span])) + bias_ref[:, span]
        chance = 0.5 + 0.5 * lax.erf(up * math.sqrt(0.5))
        act_ref[:, span] = (up * chance).astype(bf16)
        density = jnp.exp(up * up * -0.5) * (1.0 / math.sqrt(2.0 * math.pi))
        slope_ref[:, span] = (chance + up * density).astype(bf16)
        pairs = [
            (act_ref.at[:, span], act_hbm.at[:, span]),
            (slope_ref.at[:, span], slope_hbm.at[:, span]),
        ]
        stores += fetch(pairs, sems, 5 + 2 * part)
    wait_all(stores)


def up_forward(table, x, context, vectors, bias, pieces):
    tokens, width = x.shape
    rows, units = pieces[0].shape[1], pieces[0].shape[2] - width
    outs = [
        ((tokens, width), bf16),
        ((tokens, units), bf16),
        ((tokens, units), bf16),
        ((tokens, width), f32),
        ((tokens, LINE), f32),
        ((BLOCKS, rows, width), bf16),
        ((BLOCKS, rows, units), bf16),
    ]
    return call(
        up_kernel,
        "up_forward",
        outs,
        [SMEM] + [VMEM] * 4 + [HBM] * 8,
        [HBM] * 7,
        (table, x, context, vectors, bias, *pieces),
        2 * tokens * width * (width + units),
        20e6,
        [pltpu.VMEM(*out) for out in outs]
        + [pltpu.SemaphoreType.DMA((BLOCKS,)), pltpu.SemaphoreType.DMA((BLOCKS,))]
        + [pltpu.SemaphoreType.DMA((5 + 2 * (units // 512),))],
        exps=2 * tokens * units,
        limit=28,
    )


def chosen_row(owner_ref, vectors_ref, buffer):
    queries = vectors_ref[VECTORS:]
    query = lax.broadcasted_iota(jnp.int32, queries.shape, 0)
    return jnp.sum(jnp.where(query == owner_ref[buffer], queries, 0.0), axis=0, keepdims=True)


def down_kernel(
    buffers, table_ref, owner_ref, hidden_hbm, act_hbm, vectors_hbm, tags_ref, p0, p1, p2, p3, p4, p5, p6, p7,
    mixed_ref, like_ref, normed_ref, sides_ref, wdown_ref, mixed_hbm,
    hidden_ref, act_ref, vectors_ref, sems, sems_held,
):
    tokens = hidden_ref.shape[0]
    length = tokens // buffers
    loads = []
    constants = fetch([(vectors_hbm, vectors_ref)], sems_held, 3 * buffers)
    for buffer in range(buffers):
        span = pl.ds(buffer * length, length)
        pairs = [(act_hbm.at[span], act_ref.at[span]), (hidden_hbm.at[span], hidden_ref.at[span])]
        loads.append(fetch(pairs, sems_held, buffers + 2 * buffer))
        if buffer == 0:
            pieces = (p0, p1, p2, p3, p4, p5, p6, p7)
            copies = block_copies(table_ref, pieces, 0, wdown_ref.shape[2], wdown_ref, sems)
    wait_all(copies + constants)
    weight = flat(wdown_ref[...])
    stores = []
    for buffer in range(buffers):
        rows = rows_of(buffer, length)
        wait_all(loads[buffer])
        down = mm(act_ref[rows], weight) + vectors_ref[3:4]
        normed, inverse = normed_rows(hidden_ref[rows].astype(f32) + down)
        normed_ref[rows] = normed
        mixed = (normed * vectors_ref[4:5] + vectors_ref[5:6]).astype(bf16)
        mixed_ref[rows] = mixed
        span = pl.ds(buffer * length, length)
        stores += fetch([(mixed_ref.at[span], mixed_hbm.at[span])], sems_held, buffer)
        chosen = chosen_row(owner_ref, vectors_ref, buffer).astype(bf16)
        logits = mm_nt(jnp.broadcast_to(chosen, (8, chosen.shape[1])), mixed)[0:1]
        tags = tags_ref[buffer : buffer + 1].astype(f32)
        tail = jnp.log(1.0 + jnp.exp(-jnp.abs(logits)))
        log_yes = jnp.minimum(logits, 0.0) - tail
        log_no = jnp.minimum(-logits, 0.0) - tail
        like = jnp.sum(tags * log_yes + (1.0 - tags) * log_no, axis=1, keepdims=True) / length
        like_ref[buffer : buffer + 1] = jnp.broadcast_to(like, (1, LINE))
        pull = (tags - 1.0 / (1.0 + jnp.exp(-logits))) * (-loss_scale / length)
        pull = jnp.broadcast_to(pull, (LINE, length)).T
        lane = lax.broadcasted_iota(jnp.int32, (length, LINE), 1)
        sides_ref[rows] = jnp.where(lane < HEAD, inverse, pull)
    wait_all(stores)


def down_forward(table, owner, hidden, act, vectors, tags, pieces, buffers):
    tokens, width = hidden.shape
    rows, units = pieces[0].shape[1], act.shape[1]
    return call(
        functools.partial(down_kernel, buffers),
        "down_forward",
        [
            ((tokens, width), bf16),
            ((buffers, LINE), f32),
            ((tokens, width), f32),
            ((tokens, LINE), f32),
            ((BLOCKS, rows, width), bf16),
            ((tokens, width), bf16),
        ],
        [SMEM, SMEM, HBM, HBM, HBM, VMEM] + [HBM] * 8,
        [VMEM] * 5 + [HBM],
        (table, owner, hidden, act, vectors, tags, *pieces),
        2 * tokens * width * units,
        20e6,
        [
            pltpu.VMEM((tokens, width), bf16),
            pltpu.VMEM((tokens, units), bf16),
            pltpu.VMEM(vectors.shape, f32),
            pltpu.SemaphoreType.DMA((BLOCKS,)),
            pltpu.SemaphoreType.DMA((3 * buffers + 1,)),
        ],
        limit=16,
    )


UP_SUM, GAIN_SUM, SHIFT_SUM, QUERY_SUM, DOWN_SUM = range(5)
ATTN_GAIN_SUM, ATTN_SHIFT_SUM, OUT_SUM = range(3)


def adder(sums_ref, buffers):
    def add_up(kind, buffer, value, start=0):
        row = kind * buffers + buffer
        sums_ref[row : row + 1, start : start + value.shape[1]] = jnp.sum(
            value, axis=0, keepdims=True
        )

    return add_up


def up_back_kernel(
    buffers, owner_ref, mixed_ref, normed_ref, sides_ref, slope_ref, vectors_ref, wdown_ref,
    low_ref, up_ref, res_ref, sums_ref,
):
    tokens, width = mixed_ref.shape
    units = slope_ref.shape[1]
    length = tokens // buffers
    sums_ref[...] = jnp.zeros_like(sums_ref)
    add_up = adder(sums_ref, buffers)
    for buffer in range(buffers):
        rows = rows_of(buffer, length)
        normed = normed_ref[rows]
        inverse, pull = sides_ref[rows, 0:1], sides_ref[rows, HEAD : HEAD + 1]
        chosen = chosen_row(owner_ref, vectors_ref, buffer)
        add_up(GAIN_SUM, buffer, pull * normed * chosen)
        add_up(SHIFT_SUM, buffer, pull * chosen)
        add_up(QUERY_SUM, buffer, pull * mixed_ref[rows].astype(f32))
        slope = chosen * vectors_ref[4:5]
        grad = (inverse * pull) * (slope - row_mean(slope) - normed * row_mean(slope * normed))
        res_ref[rows] = grad
        grad = grad.astype(bf16)
        low_ref[rows] = grad
        add_up(DOWN_SUM, buffer, grad.astype(f32))
    part = BLOCKS // 4
    wide = units // 4
    for k in range(4):
        span = slice(k * wide, (k + 1) * wide)
        grad = mm_nt(low_ref[...], flat(wdown_ref[k * part : (k + 1) * part]))
        grad = (grad * slope_ref[:, span].astype(f32)).astype(bf16)
        up_ref[:, span] = grad
        for buffer in range(buffers):
            add_up(UP_SUM, buffer, grad[rows_of(buffer, length)].astype(f32), k * wide)


def up_backward(owner, mixed, normed, sides, slope, vectors, wdown, buffers):
    tokens, width = mixed.shape
    units = slope.shape[1]
    return call(
        functools.partial(up_back_kernel, buffers),
        "up_backward",
        [
            ((tokens, width), bf16),
            ((tokens, units), bf16),
            ((tokens, width), f32),
            ((5 * buffers, units), f32),
        ],
        [SMEM] + [VMEM] * 6,
        [VMEM] * 4,
        (owner, mixed, normed, sides, slope, vectors, wdown),
        2 * tokens * width * units,
        20e6,
    )


def hidden_back_kernel(
    buffers, res_in_ref, up_ref, normed_ref, inverse_ref, vectors_ref, wup_ref, wout_ref,
    res_hbm, attn_ref, context_ref, sums_ref, res_ref, sems,
):
    length = res_ref.shape[0] // buffers
    add_up = adder(sums_ref, buffers)
    stores = []
    weight, weight_out = flat(wup_ref[...]), flat(wout_ref[...])
    for buffer in range(buffers):
        rows = rows_of(buffer, length)
        normed = normed_ref[rows]
        grad = res_in_ref[rows] + mm_nt(up_ref[rows], weight)
        add_up(ATTN_GAIN_SUM, buffer, grad * normed)
        add_up(ATTN_SHIFT_SUM, buffer, grad)
        grad = grad * vectors_ref[1:2]
        grad = inverse_ref[rows, 0:1] * (
            grad - row_mean(grad) - normed * row_mean(grad * normed)
        )
        res_ref[rows] = grad
        span = pl.ds(buffer * length, length)
        stores += fetch([(res_ref.at[span], res_hbm.at[span])], sems, buffer)
        grad = grad.astype(bf16)
        attn_ref[rows] = grad
        add_up(OUT_SUM, buffer, grad.astype(f32))
        context_ref[rows] = mm_nt(grad, weight_out).astype(bf16)
    wait_all(stores)


def hidden_backward(res, up, normed, inverse, vectors, wup, wout, buffers):
    tokens, width = res.shape
    return call(
        functools.partial(hidden_back_kernel, buffers),
        "hidden_backward",
        [
            ((tokens, width), f32),
            ((tokens, width), bf16),
            ((tokens, width), bf16),
            ((3 * buffers, width), f32),
        ],
        [VMEM] * 7,
        [HBM] + [VMEM] * 3,
        (res, up, normed, inverse, vectors, wup, wout),
        2 * tokens * width * (up.shape[1] + width),
        20e6,
        [pltpu.VMEM((tokens, width), f32), pltpu.SemaphoreType.DMA((buffers,))],
    )


def scaled_rows(ref, scale_ref, buffers, span=slice(None)):
    length = ref.shape[0] // buffers
    return jnp.concatenate(
        [
            (ref[rows_of(b, length), span].astype(f32) * scale_ref[b]).astype(bf16)
            for b in range(buffers)
        ]
    )


def place_rows(table_ref, sums_ref, keep_ref, send_ref, start, width):
    rows = keep_ref.shape[1]
    for spot in range(BLOCKS):
        target = keep_ref if spot < HALF else send_ref
        block = pl.ds(pl.multiple_of(table_ref[spot] * rows, 8), rows)
        target[spot % HALF, :, start : start + width] = sums_ref[block, :width].astype(bf16)


def weight_blocks(table_ref, scale_ref, buffers, left_ref, right_ref, keep_ref, send_ref, begin, sums_ref):
    height, columns = left_ref.shape[1], right_ref.shape[1]
    tile = min(height, columns)
    for start in range(0, columns, tile):
        right = scaled_rows(right_ref, scale_ref, buffers, slice(start, start + tile))
        for row in range(0, height, tile):
            sums_ref[row : row + tile] = mm_tn(left_ref[:, row : row + tile], right)
        place_rows(table_ref, sums_ref, keep_ref, send_ref, begin + start, tile)


def weight_kernel(buffers, count, table_ref, scale_ref, *refs):
    pairs = [refs[2 * k : 2 * k + 2] for k in range(count)]
    keep_ref, send_ref, sums_ref = refs[2 * count :]
    begin = 0
    for left_ref, right_ref in pairs:
        weight_blocks(
            table_ref, scale_ref, buffers, left_ref, right_ref, keep_ref, send_ref, begin, sums_ref
        )
        begin += right_ref.shape[1]


def weight_gradient(name, table, scale, pairs, buffers):
    tokens, height = pairs[0][0].shape
    columns = [right.shape[1] for _, right in pairs]
    operands = [part for pair in pairs for part in pair]
    return call(
        functools.partial(weight_kernel, buffers, len(pairs)),
        name,
        [((HALF, height // BLOCKS, sum(columns)), bf16)] * 2,
        [SMEM, SMEM] + [VMEM] * len(operands),
        [VMEM] * 2,
        (table, scale, *operands),
        2 * tokens * height * sum(columns),
        10e6,
        [pltpu.VMEM((height, min(height, columns[0])), f32)],
        limit=LIMIT + 4 if height > 768 else LIMIT,
    )


def small_columns(
    buffers, count, scale_ref, owner_ref, sums_ref, attn_sums_ref, pre_ref, rows_ref, columns_ref, small_ref
):
    width = rows_ref.shape[1]
    rows = width // BLOCKS

    def weigh(ref, kind, columns=width):
        first = kind * buffers
        return sum(ref[first + b : first + b + 1, :columns] * scale_ref[b] for b in range(buffers))

    rows_ref[...] = jnp.zeros_like(rows_ref)
    kinds = [(attn_sums_ref, kind) for kind in (OUT_SUM, ATTN_GAIN_SUM, ATTN_SHIFT_SUM)]
    kinds += [(sums_ref, kind) for kind in (DOWN_SUM, GAIN_SUM, SHIFT_SUM)]
    for k, (ref, kind) in enumerate(kinds):
        rows_ref[k : k + 1] = weigh(ref, kind)
    pre = sum(pre_ref[b : b + 1] * scale_ref[b] for b in range(buffers))
    for at, total in ((QKV_AT, pre), (UP_AT, weigh(sums_ref, UP_SUM, sums_ref.shape[1]))):
        for k in range(total.shape[1] // width):
            rows_ref[at + k : at + k + 1] = total[:, k * width : (k + 1) * width]
    query = lax.broadcasted_iota(jnp.int32, (count, width), 0)
    total = jnp.zeros((count, width), f32)
    for b in range(buffers):
        row = QUERY_SUM * buffers + b
        mine = sums_ref[row : row + 1, :width] * scale_ref[b]
        total += jnp.where(query == owner_ref[b], mine, 0.0)
    rows_ref[QUERY_AT : QUERY_AT + count] = total
    columns_ref[...] = rows_ref[...].T
    lane = lax.broadcasted_iota(jnp.int32, (rows, LINE), 1)
    for block in range(BLOCKS):
        value = columns_ref[block * rows : (block + 1) * rows]
        for at, per in ((QKV_AT, 2), (UP_AT, 4)):
            for c in range(per):
                spot = (block * per + c) * rows
                source = columns_ref[spot % width : spot % width + rows]
                shift = (c - spot // width) % LINE
                if shift:
                    source = pltpu.roll(source, shift, 1)
                value = jnp.where(lane == at + c, source, value)
        small_ref[block * rows : (block + 1) * rows] = value


def attention_back_kernel(
    buffers, count, table_ref, scale_ref, owner_ref, qkv_ref, lse_ref, grad_ref, x_ref,
    sums_in_ref, attn_sums_ref, pre_hbm, keep_ref, send_ref, bias_ref,
    pre_ref, sums_ref, rows_ref, columns_ref, small_ref, sems,
):
    tokens, width = grad_ref.shape
    length, pairs = tokens // buffers, width // PAIR
    scale = 1.0 / math.sqrt(HEAD)

    def step(index, carry):
        rows = pl.ds(pl.multiple_of(index // pairs * length, length), length)
        lane = pl.multiple_of(index % pairs * PAIR, PAIR)
        query = qkv_ref[rows, pl.ds(lane, PAIR)]
        key = qkv_ref[rows, pl.ds(lane + width, PAIR)]
        value = qkv_ref[rows, pl.ds(lane + 2 * width, PAIR)]
        low = head_masks(query.shape)
        query = stacked(query, low)
        grad = stacked(grad_ref[rows, pl.ds(lane, PAIR)], low)
        probs = jnp.exp(mm_nt(key, query) * scale - lse_ref[index])
        grad_probs = mm_nt(value, grad)
        cross = jnp.sum(grad_probs * probs, axis=0, keepdims=True)
        grad_scores = (probs * (grad_probs - cross)).astype(bf16)
        grad_value = mm(probs.astype(bf16), grad)
        grad_key = mm(grad_scores, query) * scale
        grad_query = unstacked(mm_tn(key, grad_scores).T, low, length) * scale
        pre_ref[rows, pl.ds(lane, PAIR)] = grad_query.astype(bf16)
        pre_ref[rows, pl.ds(lane + width, PAIR)] = grad_key.astype(bf16)
        pre_ref[rows, pl.ds(lane + 2 * width, PAIR)] = grad_value.astype(bf16)
        return carry

    lax.fori_loop(0, buffers * pairs, step, 0, unroll=2)
    for buffer in range(buffers):
        rows = rows_of(buffer, length)
        for start, source in ((0, 0), (width, 2 * width)):
            piece = pre_ref[rows, source : source + width].astype(f32)
            bias_ref[buffer : buffer + 1, start : start + width] = jnp.sum(
                piece, axis=0, keepdims=True
            )
    stores = fetch([(pre_ref, pre_hbm)], sems)
    halves = keep_ref, send_ref
    weight_blocks(table_ref, scale_ref, buffers, x_ref, pre_ref, *halves, 0, sums_ref)
    small_columns(
        buffers, count, scale_ref, owner_ref, sums_in_ref, attn_sums_ref, bias_ref,
        rows_ref, columns_ref, small_ref,
    )
    place_rows(table_ref, small_ref, *halves, 3 * width, LINE)
    wait_all(stores)


def attention_gradient(table, scale, owner, count, qkv, lse, grad, x, sums, attn_sums, buffers):
    tokens, width = grad.shape
    length = tokens // buffers
    blocks = ((HALF, width // BLOCKS, 3 * width + LINE), bf16)
    return call(
        functools.partial(attention_back_kernel, buffers, count),
        "attention_gradient",
        [((tokens, 3 * width), bf16), blocks, blocks, ((buffers, 2 * width), f32)],
        [SMEM] * 3 + [VMEM] * 6,
        [HBM] + [VMEM] * 3,
        (table, scale, owner, qkv, lse, grad, x, sums, attn_sums),
        10 * tokens * length * width + 6 * tokens * width * width,
        20e6,
        [
            pltpu.VMEM((tokens, 3 * width), bf16),
            pltpu.VMEM((width, width), f32),
            pltpu.VMEM((LINE, width), f32),
            pltpu.VMEM((width, LINE), f32),
            pltpu.VMEM((width, LINE), f32),
            pltpu.SemaphoreType.DMA((1,)),
        ],
        exps=tokens * length * width // HEAD,
        limit=16,
    )


def states_kernel(
    buffers, scale_ref, res_hbm, pre_hbm, weight_hbm, out_hbm, res_ref, pre_ref, weight_ref, out_ref, sems
):
    length = res_ref.shape[0] // buffers
    spans = [pl.ds(b * length, length) for b in range(buffers)]
    loads = fetch([(weight_hbm, weight_ref)], sems)
    for b, span in enumerate(spans):
        pairs = [(pre_hbm.at[span], pre_ref.at[span]), (res_hbm.at[span], res_ref.at[span])]
        loads += fetch(pairs, sems, 1 + 2 * b)
    stores = []
    for b, span in enumerate(spans):
        wait_all(loads[:3] if b == 0 else loads[1 + 2 * b : 3 + 2 * b])
        grad = res_ref[span] + mm_nt(pre_ref[span], flat(weight_ref[...]))
        out_ref[span] = (grad * scale_ref[b]).astype(bf16)
        stores += fetch([(out_ref.at[span], out_hbm.at[span])], sems, 1 + 2 * buffers + b)
    wait_all(stores)


def states_gradient(scale, res, pre, weight, buffers):
    tokens, width = res.shape
    return call(
        functools.partial(states_kernel, buffers),
        "states_gradient",
        [((tokens, width), bf16)],
        [SMEM] + [HBM] * 3,
        [HBM],
        (scale, res, pre, weight),
        6 * tokens * width * width,
        8e6,
        [
            pltpu.VMEM(res.shape, f32),
            pltpu.VMEM(pre.shape, bf16),
            pltpu.VMEM(weight.shape, bf16),
            pltpu.VMEM(res.shape, bf16),
            pltpu.SemaphoreType.DMA((1 + 3 * buffers,)),
        ],
        limit=16,
    )[0]


def body(
    slot_states, answer_tags, slot_mask, retrieval, query_emb, qkv_weight, qkv_bias, out_weight,
    out_bias, attn_gain, attn_shift, up_weight, up_bias, down_weight, down_bias, ffn_gain, ffn_shift,
):
    group_count = lax.axis_size(AXES)
    device_index = lax.axis_index(AXES)
    tuned = group_count == BLOCKS
    buffers, length, width = slot_states.shape
    query_count, slot_count = slot_mask.shape
    tokens = buffers * length
    x = slot_states.reshape(tokens, width)

    running = jnp.cumsum(slot_mask.reshape(-1), dtype=jnp.int32)
    slot_ranks = jnp.arange(buffers, dtype=jnp.int32) * group_count + device_index
    places = jnp.sum(
        (running[None, :] <= slot_ranks[:, None]).astype(jnp.int32), axis=1, dtype=jnp.int32
    )
    slot_pick = places[:, None] == jnp.arange(query_count * slot_count, dtype=jnp.int32)[None, :]
    owner = places // slot_count
    owner_mask = owner[:, None] == jnp.arange(query_count, dtype=jnp.int32)[None]
    prior_score = jnp.sum(jnp.where(slot_pick, retrieval.reshape(-1)[None, :], 0.0), axis=1)

    order = Order(tuned)
    if tuned:
        table = position_table(device_index)
        vectors = (out_bias, attn_gain, attn_shift, down_bias, ffn_gain, ffn_shift)
        g1 = Gather(order, pack_first(qkv_weight, vectors, qkv_bias, up_bias, query_emb))
        g2 = Gather(order, jnp.concatenate([out_weight, up_weight], axis=1)[None])
        g3 = Gather(order, down_weight[None])
        g1.start_line()
        g1.join_line()
        g1.start_near()
        g2.start_line(g1.held)
        g1.join_near()
        g1.start_other(g1.near, owner, prior_score)
        g2.join_line()
        g2.start_near()
        g2.start_other()
        g1.join_last()
        g1.join_other()
        g3.start_line(g2.held)
        first = g1.pieces()
        vectors, bias, up_bias_all = unpack_small(table, first, 3 * width, query_count)
        order.mark(vectors)
    else:
        table = jnp.arange(BLOCKS, dtype=jnp.int32)
        everything = lambda part: lax.all_gather(part, AXES, axis=0, tiled=True).astype(f32)
        first = gather_plain(qkv_weight)
        second = gather_plain(jnp.concatenate([out_weight, up_weight], axis=1))
        third = gather_plain(down_weight)
        vectors = jnp.stack(
            [
                everything(part)
                for part in (out_bias, attn_gain, attn_shift, down_bias, ffn_gain, ffn_shift)
            ]
        )
        bias = everything(qkv_bias)
        bias = jnp.concatenate([bias[:width], jnp.zeros((width,), f32), bias[width:]]).reshape(1, -1)
        up_bias_all = everything(up_bias).reshape(1, -1)
        query_table = lax.all_gather(query_emb, AXES, axis=1, tiled=True).astype(f32)
        vectors = jnp.concatenate([vectors, jnp.zeros((VECTORS - SIX, width), f32), query_table])

    qkv, wqkv = qkv_forward(table, order.place(x), bias, first)
    if tuned:
        order.mark(qkv)
        g3.join_line()
        g3.start_near()
        g2.join_near()
    context, lse = attention_forward(order.place(qkv), buffers)
    if tuned:
        order.mark(context)
        g3.start_other(order.last)
        g2.join_other()
        g2.join_last()
        g3.join_near()
        second = g2.pieces()
    hidden, act, slope, normed, inverse, wout, wup = up_forward(
        table, x, context, vectors, up_bias_all, second
    )
    if tuned:
        order.mark(act)
        g3.join_other()
        g3.join_last()
        third = g3.pieces()
    mixed, like, normed_out, sides, wdown, mixed_out = down_forward(
        table, owner, hidden, act, vectors, answer_tags, third, buffers
    )

    scores = like[:, 0] + prior_score
    masked = jnp.where(owner_mask, scores[:, None], neg_fill)
    local_peak = jnp.max(masked, axis=0)
    local_total = jnp.sum(jnp.where(owner_mask, jnp.exp(masked - local_peak[None, :]), 0.0), axis=0)
    merged = (local_peak, local_total)
    if tuned:
        order.mark(local_total)
        merged = merge_join(order, merged, merge_start(merged, (CORE_BIT,)))
        got = merge_start(merged, LINE_MASKS)
    else:
        merged = merge_plain(merged)

    grad_low, grad_up, grad_res, sums = up_backward(
        owner, order.place(mixed), normed_out, sides, slope, vectors, wdown, buffers
    )
    if tuned:
        order.mark(grad_low)
        merged = merge_join(order, merged, got)
        got = merge_start(merged, (X_BIT, Y_BIT, X_BIT | Y_BIT))
    grad_hidden, grad_attn, grad_context, attn_sums = hidden_backward(
        order.place(grad_res), grad_up, normed, inverse, vectors, wup, wout, buffers
    )
    if tuned:
        order.mark(grad_attn)
        merged = merge_join(order, merged, got)
    totals = merged[0] + jnp.log(merged[1])
    loss = -jnp.sum(totals)
    scale = jnp.sum(
        jnp.where(owner_mask, jnp.exp(scores[:, None] - totals[None, :]), 0.0), axis=1
    )

    pairs = [(context, grad_attn), (hidden, grad_up)]
    halves2 = weight_gradient("up_gradient", table, scale, pairs, buffers)
    if tuned:
        order.mark(halves2[1])
        s2 = Scatter(order, *halves2)
        s2.start_core()
    pairs = [(order.place(act), grad_low)]
    halves3 = weight_gradient("down_gradient", table, scale, pairs, buffers)
    if tuned:
        order.mark(halves3[1])
        s3 = Scatter(order, *halves3)
        s3.start_core()
        s2.join_core()
        s2.start_other()
    grad_pre, *halves1, pre_sums = attention_gradient(
        table, scale, owner, query_count, qkv, lse, order.place(grad_context), x, sums, attn_sums, buffers
    )
    if tuned:
        order.mark(halves1[1])
        s1 = Scatter(order, *halves1)
        s1.start_core()
        s2.join_last()
        s3.join_core()
    states = states_gradient(scale, grad_hidden, order.place(grad_pre), wqkv, buffers)
    if tuned:
        order.mark(states)
        s2.join_sides()
        s3.start_other(order.last)
        s1.join_core()
        s3.join_last()
        s1.start_other(order.last)
        s1.join_last()
        s3.join_sides()
        second_grad = s2.finish(0, width), s2.finish(width)
        order.mark(second_grad[1])
        s1.join_sides()
        third_grad = s3.finish()
        order.mark(third_grad)
        first_grad, *six, qkv_bias_sum, up_bias_sum, query_sum = split_first(
            s1.own, [order.place(part) for part in s1.line], query_count
        )
    else:
        third_grad = scatter_plain(*halves3)
        cut = lambda halves, start, end: scatter_plain(*(half[:, :, start:end] for half in halves))
        second_grad = cut(halves2, 0, width), cut(halves2, width, width + up_weight.shape[1])
        first_grad = cut(halves1, 0, 3 * width)
    if not tuned:
        weigh = lambda part: jnp.sum(scale[:, None] * part, axis=0)
        mine = lambda part: lax.psum_scatter(weigh(part), AXES, scatter_dimension=0, tiled=True)
        rows_for = lambda part, kind: part[kind * buffers : (kind + 1) * buffers, :width]
        six = [mine(rows_for(attn_sums, kind)) for kind in (OUT_SUM, ATTN_GAIN_SUM, ATTN_SHIFT_SUM)]
        six += [mine(rows_for(sums, kind)) for kind in (DOWN_SUM, GAIN_SUM, SHIFT_SUM)]
        qkv_bias_sum, up_bias_sum = mine(pre_sums), mine(sums[:buffers])
        weighed = jnp.where(owner_mask, scale[:, None], 0.0)
        query_sum = jnp.sum(weighed[:, :, None] * rows_for(sums, QUERY_SUM)[:, None, :], axis=0)
        query_sum = lax.psum_scatter(query_sum, AXES, scatter_dimension=1, tiled=True)
    return (
        mixed_out.reshape(slot_states.shape),
        loss,
        states.reshape(slot_states.shape),
        query_sum,
        first_grad,
        qkv_bias_sum,
        second_grad[0],
        six[0],
        six[1],
        six[2],
        second_grad[1],
        up_bias_sum,
        third_grad,
        six[3],
        six[4],
        six[5],
    )


def solution(mesh):
    split = P(AXES)
    in_specs = (split, split, P(), P(), P(None, AXES)) + (split,) * 12
    out_specs = (split, P(), split, P(None, AXES)) + (split,) * 12
    return jax.shard_map(body, mesh=mesh, in_specs=in_specs, out_specs=out_specs, check_vma=False)
```

```python
import functools
import math

import jax
import jax.numpy as jnp
import numpy as np
from jax import lax
from jax.experimental import pallas as pl
from jax.experimental.pallas import tpu as pltpu
from jax.sharding import PartitionSpec as P

HEAD = 64
PAIR = 2 * HEAD
LINE = 128
AXES = ("dp", "fsdp")
X_BIT, CORE_BIT, Z_FAR, Z_NEAR, Y_BIT = 16, 8, 4, 2, 1
BLOCKS = 32
HALF = BLOCKS // 2
SHARE = 0.02
LIMIT = 16

eps_norm = 1e-12
loss_scale = 65536.0
neg_fill = -1e30
f32 = jnp.float32
bf16 = jnp.bfloat16
VMEM = pl.BlockSpec(memory_space=pltpu.VMEM)
SMEM = pl.BlockSpec(memory_space=pltpu.SMEM)
HBM = pl.BlockSpec(memory_space=pltpu.HBM)
ANYWHERE = pl.BlockSpec(memory_space=pl.ANY)


def device_offsets(first, second):
    masks = (Z_FAR, Z_NEAR, first, second)
    return np.array(
        [sum(m for k, m in enumerate(masks) if p >> k & 1) for p in range(HALF)], np.int32
    )


def position_table(device_index):
    even = device_offsets(X_BIT, Y_BIT)
    odd = device_offsets(Y_BIT, X_BIT)
    table_even = jnp.asarray(np.concatenate([even, odd ^ CORE_BIT]))
    table_odd = jnp.asarray(np.concatenate([odd, even ^ CORE_BIT]))
    core = (device_index // CORE_BIT) % 2
    return jnp.where(core == 0, table_even, table_odd) ^ device_index


def exchange(value, even_mask, odd_mask):
    pairs = [(i, i ^ (odd_mask if i & CORE_BIT else even_mask)) for i in range(BLOCKS)]
    return lax.ppermute(value, AXES, pairs)


def after(value, *earlier):
    return lax.optimization_barrier((value, *earlier))[0]


SIDE, OTHER, CORES = (X_BIT, Y_BIT), (Y_BIT, X_BIT), (CORE_BIT, CORE_BIT)
LINE_MASKS = (Z_FAR, Z_NEAR, Z_FAR | Z_NEAR)


class Order:
    def __init__(self, tuned):
        self.tuned, self.last = tuned, None

    def place(self, value):
        if self.tuned and self.last is not None:
            return after(value, self.last)
        return value

    def mark(self, value):
        self.last = value


class Gather:
    def __init__(self, order, shard):
        self.order, self.shard = order, shard

    def start_line(self, *earlier):
        own = after(self.shard, *earlier) if earlier else self.shard
        self.got = [exchange(own, mask, mask) for mask in LINE_MASKS]

    def join_line(self):
        got = [self.order.place(part) for part in self.got]
        self.held = lax.optimization_barrier(jnp.concatenate([self.shard, *got]))
        self.order.mark(self.held)

    def start_near(self, *earlier):
        held = after(self.held, *earlier) if earlier else self.held
        self.near = exchange(held, *SIDE)

    def start_other(self, *earlier):
        held = after(self.held, *earlier) if earlier else self.held
        self.other = exchange(held, *OTHER)
        self.far_held = exchange(held, *CORES)

    def join_near(self):
        self.near = self.order.place(self.near)
        self.order.mark(self.near)
        self.last = exchange(self.near, *OTHER)
        self.far_near = exchange(self.near, *CORES)

    def join_other(self):
        self.other = self.order.place(self.other)
        self.order.mark(self.other)
        self.far_other = exchange(self.other, *CORES)

    def join_last(self):
        self.last = self.order.place(self.last)
        self.order.mark(self.last)
        self.far_last = exchange(self.last, *CORES)

    def pieces(self):
        far = (self.far_held, self.far_near, self.far_other, self.far_last)
        far = [self.order.place(part) for part in far]
        self.order.mark(far[-1])
        return (self.held, self.near, self.other, self.last, *far)


def gather_plain(part):
    whole = lax.all_gather(part, AXES, axis=0, tiled=True)
    blocks = whole.reshape(BLOCKS, -1, whole.shape[1])
    return tuple(blocks[4 * k : 4 * k + 4] for k in range(8))


def add_low(first, second):
    return (first.astype(f32) + second.astype(f32)).astype(bf16)


def add_up_parts(*parts):
    return sum(part.astype(f32) for part in parts)


class Scatter:
    def __init__(self, order, keep, send):
        self.order, self.keep, self.send = order, keep, send

    def start_core(self, *earlier):
        self.got = exchange(after(self.send, *earlier) if earlier else self.send, *CORES)

    def quarter(self, k, *more):
        span = slice(4 * k, 4 * k + 4)
        return add_up_parts(self.keep[span], self.got[span], *more)

    def join_core(self):
        self.got = self.order.place(self.got)
        last, other = self.quarter(3).astype(bf16), self.quarter(2).astype(bf16)
        self.last = exchange(last, *OTHER)
        self.other = other
        self.order.mark(other)

    def start_other(self, *earlier):
        other = after(self.other, *earlier) if earlier else self.other
        self.other = exchange(other, *OTHER)

    def join_last(self):
        near = self.quarter(1, self.order.place(self.last)).astype(bf16)
        self.near = exchange(near, *SIDE)
        self.order.mark(near)

    def join_sides(self):
        more = self.order.place(self.other), self.order.place(self.near)
        block = lambda p: add_up_parts(self.keep[p], self.got[p], more[0][p], more[1][p])
        sends = [block(p).astype(bf16) for p in (1, 2, 3)]
        self.line = [exchange(part, mask, mask) for part, mask in zip(sends, LINE_MASKS)]
        self.own = block(0)
        self.order.mark(sends[-1])

    def finish(self, start=0, width=None):
        end = self.own.shape[1] if width is None else start + width
        cut = lambda part: part[..., start:end]
        return add_up_parts(cut(self.own), *(cut(self.order.place(part)) for part in self.line))


def scatter_plain(keep, send):
    blocks = jnp.concatenate([keep, send])
    whole = blocks.reshape(-1, blocks.shape[2])
    return lax.psum_scatter(whole, AXES, scatter_dimension=0, tiled=True).astype(f32)


def merge_start(pair, masks):
    both = jnp.stack(pair)
    return [exchange(both, mask, mask) for mask in masks]


def merge_join(order, pair, got):
    got = [order.place(part) for part in got]
    peak = functools.reduce(jnp.maximum, [part[0] for part in got], pair[0])
    total = pair[1] * jnp.exp(pair[0] - peak)
    total += sum(part[1] * jnp.exp(part[0] - peak) for part in got)
    order.mark(total)
    return (peak, total)


def merge_plain(pair):
    peak = lax.pmax(pair[0], AXES)
    return (peak, lax.psum(pair[1] * jnp.exp(pair[0] - peak), AXES))


def call(
    kernel, name, outs, in_specs, out_specs, args, flops, moved, scratch=(), exps=0, limit=None
):
    args = [
        pltpu.with_memory_space_constraint(arg, pltpu.HBM) if spec is HBM else arg
        for arg, spec in zip(args, in_specs)
    ]
    return pl.pallas_call(
        kernel,
        out_shape=[
            pltpu.HBM(shape, dtype) if spec is HBM else jax.ShapeDtypeStruct(shape, dtype)
            for (shape, dtype), spec in zip(outs, out_specs)
        ],
        in_specs=in_specs,
        out_specs=out_specs,
        scratch_shapes=list(scratch),
        compiler_params=pltpu.CompilerParams(vmem_limit_bytes=(limit or LIMIT) * 2**20),
        cost_estimate=pl.CostEstimate(
            flops=int(flops * SHARE), bytes_accessed=int(moved * SHARE), transcendentals=int(exps * SHARE)
        ),
        name=name,
    )(*args)


def mm(first, second):
    return jnp.dot(first, second, preferred_element_type=f32)


def mm_nt(first, second):
    return lax.dot_general(first, second, (((1,), (1,)), ((), ())), preferred_element_type=f32)


def mm_tn(first, second):
    return lax.dot_general(first, second, (((0,), (0,)), ((), ())), preferred_element_type=f32)


def row_mean(value):
    return jnp.mean(value, axis=-1, keepdims=True)


def block_copies(table_ref, pieces, start, width, target, sems, spots=range(BLOCKS)):
    copies = [
        pltpu.make_async_copy(
            pieces[spot // 4].at[spot % 4, :, pl.ds(start, width)],
            target.at[table_ref[spot]],
            sems.at[spot],
        )
        for spot in spots
    ]
    for copy in copies:
        copy.start()
    return copies


def fetch(pairs, sems, first=0):
    copies = [
        pltpu.make_async_copy(source, target, sems.at[first + k])
        for k, (source, target) in enumerate(pairs)
    ]
    for copy in copies:
        copy.start()
    return copies


def wait_all(copies):
    for copy in copies:
        copy.wait()


def flat(value):
    return value.reshape(-1, value.shape[-1])


SIX, QKV_AT, UP_AT, QUERY_AT = 6, 6, 8, 12
VECTORS = 8


def pack_kernel(weight_hbm, *refs):
    sources, out_ref, parts, held_ref, sems = refs[: SIX + 3], refs[SIX + 3], refs[SIX + 4 : -2], *refs[-2:]
    rows, width = out_ref.shape[1], out_ref.shape[2] - LINE
    copies = fetch(zip(sources, parts), sems)
    copies += fetch([(weight_hbm, out_ref.at[0, :, pl.ds(0, width)])], sems, len(parts))
    vectors, (qkv_ref, up_ref, query_ref) = parts[:SIX], parts[SIX:]
    held_ref[...] = jnp.zeros_like(held_ref)
    wait_all(copies)
    for k, ref in enumerate(vectors):
        held_ref[k : k + 1, :rows] = ref[...].astype(f32)
    for at, ref, count in ((QKV_AT, qkv_ref, 2), (UP_AT, up_ref, 4)):
        value = ref[...].astype(f32)
        for c in range(count):
            held_ref[at + c : at + c + 1, :rows] = value[:, c * rows : (c + 1) * rows]
    count = query_ref.shape[0]
    held_ref[QUERY_AT : QUERY_AT + count, :rows] = query_ref[...].astype(f32)
    out_ref[0, :, width:] = held_ref[...].T[:rows].astype(bf16)


def pack_first(weight, vectors, qkv_bias, up_bias, query_emb):
    rows, width = weight.shape
    parts = [part.reshape(1, -1) for part in (*vectors, qkv_bias, up_bias)] + [query_emb]
    return call(
        pack_kernel,
        "pack_first",
        [((1, rows, width + LINE), bf16)],
        [HBM] * (1 + len(parts)),
        [VMEM],
        [weight, *parts],
        0,
        1e5,
        [pltpu.VMEM(part.shape, part.dtype) for part in parts]
        + [pltpu.VMEM((LINE, LINE), f32), pltpu.SemaphoreType.DMA((len(parts) + 1,))],
    )[0]


def unpack_kernel(
    start, count, table_ref, p0, p1, p2, p3, p4, p5, p6, p7, consts_ref, qkv_ref, up_ref,
    held_ref, qkv_wide, up_wide, sems,
):
    wait_all(block_copies(table_ref, (p0, p1, p2, p3, p4, p5, p6, p7), start, LINE, held_ref, sems))
    rows = held_ref.shape[1]
    every = flat(held_ref[...]).astype(f32)
    for block in range(BLOCKS):
        value = every[block * rows : (block + 1) * rows]
        for c in range(2):
            qkv_wide[(2 * block + c) * rows : (2 * block + c + 1) * rows] = value
        for c in range(4):
            up_wide[(4 * block + c) * rows : (4 * block + c + 1) * rows] = value
    turned = every.T
    consts_ref[:VECTORS] = turned[:VECTORS]
    consts_ref[VECTORS:] = turned[QUERY_AT : QUERY_AT + count]

    def line(wide, at, count):
        picks = lax.broadcasted_iota(jnp.int32, (8, LINE), 1) == at + lax.broadcasted_iota(
            jnp.int32, (8, LINE), 0
        )
        found = mm_nt(picks.astype(bf16), wide[...].astype(bf16))
        part = lax.broadcasted_iota(jnp.int32, found.shape, 1) // rows % count
        mine = part == lax.broadcasted_iota(jnp.int32, found.shape, 0)
        return jnp.sum(jnp.where(mine, found, 0.0), axis=0, keepdims=True)

    up_ref[...] = line(up_wide, UP_AT, 4)
    width = held_ref.shape[0] * rows
    bias = line(qkv_wide, QKV_AT, 2)
    qkv_ref[:, :width] = bias[:, :width]
    qkv_ref[:, width : 2 * width] = jnp.zeros((1, width), f32)
    qkv_ref[:, 2 * width :] = bias[:, width:]


def unpack_small(table, pieces, start, query_count):
    rows = pieces[0].shape[1]
    width = BLOCKS * rows
    return call(
        functools.partial(unpack_kernel, start, query_count),
        "unpack_small",
        [((VECTORS + query_count, width), f32), ((1, 3 * width), f32), ((1, 4 * width), f32)],
        [SMEM] + [HBM] * 8,
        [VMEM] * 3,
        (table, *pieces),
        0,
        1e6,
        [
            pltpu.VMEM((BLOCKS, rows, LINE), bf16),
            pltpu.VMEM((2 * width, LINE), f32),
            pltpu.VMEM((4 * width, LINE), f32),
            pltpu.SemaphoreType.DMA((BLOCKS,)),
        ],
    )


def split_kernel(own_ref, g0_ref, g1_ref, g2_ref, first_ref, *refs):
    vectors, (qkv_ref, up_ref, query_ref, held_ref) = refs[:SIX], refs[SIX:]
    rows, width = first_ref.shape
    total = own_ref[...] + (
        g0_ref[...].astype(f32) + g1_ref[...].astype(f32) + g2_ref[...].astype(f32)
    )
    first_ref[...] = total[:, :width]
    held_ref[...] = jnp.zeros_like(held_ref)
    held_ref[:rows] = total[:, width:]
    turned = held_ref[...].T
    for k, ref in enumerate(vectors):
        ref[...] = turned[k : k + 1, :rows]
    for c in range(2):
        qkv_ref[:, c * rows : (c + 1) * rows] = turned[QKV_AT + c : QKV_AT + c + 1, :rows]
    for c in range(4):
        up_ref[:, c * rows : (c + 1) * rows] = turned[UP_AT + c : UP_AT + c + 1, :rows]
    query_ref[...] = turned[QUERY_AT : QUERY_AT + query_ref.shape[0], :rows]


def split_first(own, got, query_count):
    rows, width = own.shape[0], own.shape[1] - LINE
    outs = call(
        split_kernel,
        "split_first",
        [((rows, width), f32)]
        + [((1, rows), f32)] * SIX
        + [((1, 2 * rows), f32), ((1, 4 * rows), f32), ((query_count, rows), f32)],
        [VMEM] * 4,
        [VMEM] * (SIX + 4),
        (own, *got),
        0,
        1e6,
        [pltpu.VMEM((LINE, LINE), f32)],
    )
    return [outs[0]] + [part.reshape(-1) for part in outs[1:-1]] + [outs[-1]]


def block_scratch(rows, width):
    return [pltpu.VMEM((BLOCKS, rows, width), bf16), pltpu.SemaphoreType.DMA((BLOCKS,))]


def head_masks(shape):
    lane = lax.broadcasted_iota(jnp.int32, shape, 1)
    return lane < HEAD


def stacked(pair, low):
    zero = jnp.zeros_like(pair)
    return jnp.concatenate([jnp.where(low, pair, zero), jnp.where(low, zero, pair)])


def unstacked(value, low, length):
    return jnp.where(low, value[:length], value[length:])


def rows_of(buffer, length):
    return slice(buffer * length, (buffer + 1) * length)


def rows_of(buffer, length):
    return slice(buffer * length, (buffer + 1) * length)


def qkv_kernel(
    table_ref, x_ref, bias_ref, p0, p1, p2, p3, p4, p5, p6, p7, qkv_ref, weight_hbm, weight_ref, sems, sems_out
):
    width = x_ref.shape[1]
    wait_all(block_copies(table_ref, (p0, p1, p2, p3, p4, p5, p6, p7), 0, 3 * width, weight_ref, sems))
    stores = fetch([(weight_ref, weight_hbm)], sems_out)
    x = x_ref[...]
    for part in range(3):
        span = slice(part * width, (part + 1) * width)
        weight = flat(weight_ref[:, :, span])
        qkv_ref[:, span] = (mm(x, weight) + bias_ref[:, span]).astype(bf16)
    wait_all(stores)


def qkv_forward(table, x, bias, pieces):
    tokens, width = x.shape
    rows = pieces[0].shape[1]
    return call(
        qkv_kernel,
        "qkv_forward",
        [((tokens, 3 * width), bf16), ((BLOCKS, rows, 3 * width), bf16)],
        [SMEM, VMEM, VMEM] + [HBM] * 8,
        [VMEM, HBM],
        (table, x, bias, *pieces),
        6 * tokens * width * width,
        10e6,
        block_scratch(rows, 3 * width) + [pltpu.SemaphoreType.DMA((1,))],
    )


def attention_kernel(buffers, qkv_ref, context_ref, lse_ref):
    tokens, width = context_ref.shape
    length, pairs = tokens // buffers, width // PAIR
    scale = 1.0 / math.sqrt(HEAD)

    def step(index, carry):
        rows = pl.ds(pl.multiple_of(index // pairs * length, length), length)
        lane = pl.multiple_of(index % pairs * PAIR, PAIR)
        query = qkv_ref[rows, pl.ds(lane, PAIR)]
        key = qkv_ref[rows, pl.ds(lane + width, PAIR)]
        value = qkv_ref[rows, pl.ds(lane + 2 * width, PAIR)]
        low = head_masks(query.shape)
        scores = mm_nt(key, stacked(query, low)) * scale
        peak = jnp.max(scores, axis=0, keepdims=True)
        powers = jnp.exp(scores - peak)
        total = jnp.sum(powers, axis=0, keepdims=True)
        probs = (powers * (1.0 / total)).astype(bf16)
        mixed = mm_tn(value, probs).T
        context_ref[rows, pl.ds(lane, PAIR)] = unstacked(mixed, low, length).astype(bf16)
        lse_ref[index] = peak + jnp.log(total)
        return carry

    lax.fori_loop(0, buffers * pairs, step, 0, unroll=3)


def attention_forward(qkv, buffers):
    tokens, width = qkv.shape[0], qkv.shape[1] // 3
    length = tokens // buffers
    lse = (buffers * (width // PAIR), 1, 2 * length)
    return call(
        functools.partial(attention_kernel, buffers),
        "attention_forward",
        [((tokens, width), bf16), (lse, f32)],
        [VMEM],
        [VMEM] * 2,
        (qkv,),
        4 * tokens * width * length,
        4e6,
        exps=tokens * length * width // HEAD,
    )


def normed_rows(residual):
    center = residual - row_mean(residual)
    inverse = lax.rsqrt(row_mean(center * center) + eps_norm)
    return center * inverse, inverse


def up_kernel(
    table_ref, x_ref, context_ref, vectors_ref, bias_ref, p0, p1, p2, p3, p4, p5, p6, p7,
    hidden_hbm, act_hbm, slope_hbm, normed_hbm, inverse_hbm, wout_hbm, wup_hbm,
    hidden_ref, act_ref, slope_ref, normed_ref, inverse_ref, wout_ref, wup_ref, sems_out, sems_up, sems,
):
    pieces = (p0, p1, p2, p3, p4, p5, p6, p7)
    width, units = x_ref.shape[1], wup_ref.shape[2]
    first = block_copies(table_ref, pieces, 0, width, wout_ref, sems_out)
    copies = block_copies(table_ref, pieces, width, units, wup_ref, sems_up)
    wait_all(first)
    out = mm(context_ref[...], flat(wout_ref[...])) + vectors_ref[0:1]
    normed, inverse = normed_rows(x_ref[...].astype(f32) + out)
    normed_ref[...] = normed
    inverse_ref[...] = jnp.broadcast_to(inverse, inverse_ref.shape)
    hidden_ref[...] = (normed * vectors_ref[1:2] + vectors_ref[2:3]).astype(bf16)
    wait_all(copies)
    pairs = [
        (wup_ref, wup_hbm),
        (wout_ref, wout_hbm),
        (normed_ref, normed_hbm),
        (inverse_ref, inverse_hbm),
        (hidden_ref, hidden_hbm),
    ]
    stores = fetch(pairs, sems)
    wide = 512
    for part in range(units // wide):
        span = pl.ds(part * wide, wide)
        up = mm(hidden_ref[...], flat(wup_ref[:, :, span])) + bias_ref[:, span]
        chance = 0.5 + 0.5 * lax.erf(up * math.sqrt(0.5))
        act_ref[:, span] = (up * chance).astype(bf16)
        density = jnp.exp(up * up * -0.5) * (1.0 / math.sqrt(2.0 * math.pi))
        slope_ref[:, span] = (chance + up * density).astype(bf16)
        pairs = [
            (act_ref.at[:, span], act_hbm.at[:, span]),
            (slope_ref.at[:, span], slope_hbm.at[:, span]),
        ]
        stores += fetch(pairs, sems, 5 + 2 * part)
    wait_all(stores)


def up_forward(table, x, context, vectors, bias, pieces):
    tokens, width = x.shape
    rows, units = pieces[0].shape[1], pieces[0].shape[2] - width
    outs = [
        ((tokens, width), bf16),
        ((tokens, units), bf16),
        ((tokens, units), bf16),
        ((tokens, width), f32),
        ((tokens, LINE), f32),
        ((BLOCKS, rows, width), bf16),
        ((BLOCKS, rows, units), bf16),
    ]
    return call(
        up_kernel,
        "up_forward",
        outs,
        [SMEM] + [VMEM] * 4 + [HBM] * 8,
        [HBM] * 7,
        (table, x, context, vectors, bias, *pieces),
        2 * tokens * width * (width + units),
        20e6,
        [pltpu.VMEM(*out) for out in outs]
        + [pltpu.SemaphoreType.DMA((BLOCKS,)), pltpu.SemaphoreType.DMA((BLOCKS,))]
        + [pltpu.SemaphoreType.DMA((5 + 2 * (units // 512),))],
        exps=2 * tokens * units,
        limit=28,
    )


def chosen_row(owner_ref, vectors_ref, buffer):
    queries = vectors_ref[VECTORS:]
    query = lax.broadcasted_iota(jnp.int32, queries.shape, 0)
    return jnp.sum(jnp.where(query == owner_ref[buffer], queries, 0.0), axis=0, keepdims=True)


QUARTERS = (((0, 1, 2), 0), ((3,), 12), ((4, 5, 6), 16), ((7,), 28))


def down_kernel(
    buffers, table_ref, owner_ref, hidden_hbm, act_hbm, vectors_hbm, tags_ref, p0, p1, p2, p3, p4, p5, p6, p7,
    mixed_ref, like_ref, normed_ref, sides_ref, wdown_ref, mixed_hbm,
    hidden_ref, act_ref, vectors_ref, down_ref, sems, sems_held,
):
    tokens, width = hidden_ref.shape
    length = tokens // buffers
    pieces = (p0, p1, p2, p3, p4, p5, p6, p7)
    count = len(QUARTERS)
    part, wide = BLOCKS // count, act_ref.shape[2]
    places = [table_ref[spot] // part for _, spot in QUARTERS]
    loads = []
    for k, (names, _) in enumerate(QUARTERS):
        lanes = pl.ds(pl.multiple_of(places[k] * wide, LINE), wide)
        copies = fetch([(act_hbm.at[:, lanes], act_ref.at[k])], sems_held, k)
        for name in names:
            spots = range(4 * name, 4 * name + 4)
            copies += block_copies(table_ref, pieces, 0, width, wdown_ref, sems, spots)
        loads.append(copies)
    last = fetch([(hidden_hbm, hidden_ref), (vectors_hbm, vectors_ref)], sems_held, count)

    def product(k, rows):
        weight = flat(wdown_ref[pl.ds(places[k] * part, part)])
        return mm(act_ref[k, rows], weight)

    for k in range(count - 1):
        wait_all(loads[k])
        value = product(k, slice(None))
        down_ref[...] = value if k == 0 else down_ref[...] + value
    wait_all(loads[-1] + last)
    stores = []
    for buffer in range(buffers):
        rows = rows_of(buffer, length)
        down = down_ref[rows] + product(count - 1, rows) + vectors_ref[3:4]
        normed, inverse = normed_rows(hidden_ref[rows].astype(f32) + down)
        normed_ref[rows] = normed
        mixed = (normed * vectors_ref[4:5] + vectors_ref[5:6]).astype(bf16)
        mixed_ref[rows] = mixed
        span = pl.ds(buffer * length, length)
        stores += fetch([(mixed_ref.at[span], mixed_hbm.at[span])], sems_held, count + 2 + buffer)
        chosen = chosen_row(owner_ref, vectors_ref, buffer).astype(bf16)
        logits = mm_nt(jnp.broadcast_to(chosen, (8, chosen.shape[1])), mixed)[0:1]
        tags = tags_ref[buffer : buffer + 1].astype(f32)
        tail = jnp.log(1.0 + jnp.exp(-jnp.abs(logits)))
        log_yes = jnp.minimum(logits, 0.0) - tail
        log_no = jnp.minimum(-logits, 0.0) - tail
        like = jnp.sum(tags * log_yes + (1.0 - tags) * log_no, axis=1, keepdims=True) / length
        like_ref[buffer : buffer + 1] = jnp.broadcast_to(like, (1, LINE))
        pull = (tags - 1.0 / (1.0 + jnp.exp(-logits))) * (-loss_scale / length)
        pull = jnp.broadcast_to(pull, (LINE, length)).T
        lane = lax.broadcasted_iota(jnp.int32, (length, LINE), 1)
        sides_ref[rows] = jnp.where(lane < HEAD, inverse, pull)
    wait_all(stores)


def down_forward(table, owner, hidden, act, vectors, tags, pieces, buffers):
    tokens, width = hidden.shape
    rows, units = pieces[0].shape[1], act.shape[1]
    return call(
        functools.partial(down_kernel, buffers),
        "down_forward",
        [
            ((tokens, width), bf16),
            ((buffers, LINE), f32),
            ((tokens, width), f32),
            ((tokens, LINE), f32),
            ((BLOCKS, rows, width), bf16),
            ((tokens, width), bf16),
        ],
        [SMEM, SMEM, HBM, HBM, HBM, VMEM] + [HBM] * 8,
        [VMEM] * 5 + [HBM],
        (table, owner, hidden, act, vectors, tags, *pieces),
        2 * tokens * width * units,
        20e6,
        [
            pltpu.VMEM((tokens, width), bf16),
            pltpu.VMEM((len(QUARTERS), tokens, units // len(QUARTERS)), bf16),
            pltpu.VMEM(vectors.shape, f32),
            pltpu.VMEM((tokens, width), f32),
            pltpu.SemaphoreType.DMA((BLOCKS,)),
            pltpu.SemaphoreType.DMA((len(QUARTERS) + 2 + buffers,)),
        ],
        limit=18,
    )


UP_SUM, GAIN_SUM, SHIFT_SUM, QUERY_SUM, DOWN_SUM = range(5)
ATTN_GAIN_SUM, ATTN_SHIFT_SUM, OUT_SUM = range(3)


def adder(sums_ref, buffers):
    def add_up(kind, buffer, value, start=0):
        row = kind * buffers + buffer
        sums_ref[row : row + 1, start : start + value.shape[1]] = jnp.sum(
            value, axis=0, keepdims=True
        )

    return add_up


def up_back_kernel(
    buffers, owner_ref, mixed_ref, normed_ref, sides_ref, slope_ref, vectors_ref, wdown_ref,
    low_ref, up_ref, res_ref, sums_ref,
):
    tokens, width = mixed_ref.shape
    units = slope_ref.shape[1]
    length = tokens // buffers
    sums_ref[...] = jnp.zeros_like(sums_ref)
    add_up = adder(sums_ref, buffers)
    for buffer in range(buffers):
        rows = rows_of(buffer, length)
        normed = normed_ref[rows]
        inverse, pull = sides_ref[rows, 0:1], sides_ref[rows, HEAD : HEAD + 1]
        chosen = chosen_row(owner_ref, vectors_ref, buffer)
        add_up(GAIN_SUM, buffer, pull * normed * chosen)
        add_up(SHIFT_SUM, buffer, pull * chosen)
        add_up(QUERY_SUM, buffer, pull * mixed_ref[rows].astype(f32))
        slope = chosen * vectors_ref[4:5]
        grad = (inverse * pull) * (slope - row_mean(slope) - normed * row_mean(slope * normed))
        res_ref[rows] = grad
        grad = grad.astype(bf16)
        low_ref[rows] = grad
        add_up(DOWN_SUM, buffer, grad.astype(f32))
    part = BLOCKS // 4
    wide = units // 4
    for k in range(4):
        span = slice(k * wide, (k + 1) * wide)
        weight = flat(wdown_ref[k * part : (k + 1) * part])
        for buffer in range(buffers):
            rows = rows_of(buffer, length)
            grad = mm_nt(low_ref[rows], weight) * slope_ref[rows, span].astype(f32)
            grad = grad.astype(bf16)
            up_ref[rows, span] = grad
            add_up(UP_SUM, buffer, grad.astype(f32), k * wide)


def up_backward(owner, mixed, normed, sides, slope, vectors, wdown, buffers):
    tokens, width = mixed.shape
    units = slope.shape[1]
    return call(
        functools.partial(up_back_kernel, buffers),
        "up_backward",
        [
            ((tokens, width), bf16),
            ((tokens, units), bf16),
            ((tokens, width), f32),
            ((5 * buffers, units), f32),
        ],
        [SMEM] + [VMEM] * 6,
        [VMEM] * 4,
        (owner, mixed, normed, sides, slope, vectors, wdown),
        2 * tokens * width * units,
        20e6,
    )


def hidden_back_kernel(
    buffers, res_in_ref, up_ref, normed_ref, inverse_ref, vectors_ref, wup_ref, wout_ref,
    res_hbm, attn_ref, context_ref, sums_ref, res_ref, sems,
):
    length = res_ref.shape[0] // buffers
    add_up = adder(sums_ref, buffers)
    stores = []
    weight, weight_out = flat(wup_ref[...]), flat(wout_ref[...])
    for buffer in range(buffers):
        rows = rows_of(buffer, length)
        normed = normed_ref[rows]
        grad = res_in_ref[rows] + mm_nt(up_ref[rows], weight)
        add_up(ATTN_GAIN_SUM, buffer, grad * normed)
        add_up(ATTN_SHIFT_SUM, buffer, grad)
        grad = grad * vectors_ref[1:2]
        grad = inverse_ref[rows, 0:1] * (
            grad - row_mean(grad) - normed * row_mean(grad * normed)
        )
        res_ref[rows] = grad
        span = pl.ds(buffer * length, length)
        stores += fetch([(res_ref.at[span], res_hbm.at[span])], sems, buffer)
        grad = grad.astype(bf16)
        attn_ref[rows] = grad
        add_up(OUT_SUM, buffer, grad.astype(f32))
        context_ref[rows] = mm_nt(grad, weight_out).astype(bf16)
    wait_all(stores)


def hidden_backward(res, up, normed, inverse, vectors, wup, wout, buffers):
    tokens, width = res.shape
    return call(
        functools.partial(hidden_back_kernel, buffers),
        "hidden_backward",
        [
            ((tokens, width), f32),
            ((tokens, width), bf16),
            ((tokens, width), bf16),
            ((3 * buffers, width), f32),
        ],
        [VMEM] * 7,
        [HBM] + [VMEM] * 3,
        (res, up, normed, inverse, vectors, wup, wout),
        2 * tokens * width * (up.shape[1] + width),
        20e6,
        [pltpu.VMEM((tokens, width), f32), pltpu.SemaphoreType.DMA((buffers,))],
    )


def scaled_rows(ref, scale_ref, buffers, span=slice(None)):
    length = ref.shape[0] // buffers
    return jnp.concatenate(
        [
            (ref[rows_of(b, length), span].astype(f32) * scale_ref[b]).astype(bf16)
            for b in range(buffers)
        ]
    )


def place_rows(table_ref, sums_ref, keep_ref, send_ref, start, width):
    rows = keep_ref.shape[1]
    for spot in range(BLOCKS):
        target = keep_ref if spot < HALF else send_ref
        block = pl.ds(pl.multiple_of(table_ref[spot] * rows, 8), rows)
        target[spot % HALF, :, start : start + width] = sums_ref[block, :width].astype(bf16)


def weight_blocks(table_ref, scale_ref, buffers, left_ref, right_ref, keep_ref, send_ref, begin, sums_ref):
    height, columns = left_ref.shape[1], right_ref.shape[1]
    tile = min(height, columns)
    for start in range(0, columns, tile):
        right = scaled_rows(right_ref, scale_ref, buffers, slice(start, start + tile))
        for row in range(0, height, tile):
            sums_ref[row : row + tile] = mm_tn(left_ref[:, row : row + tile], right)
        place_rows(table_ref, sums_ref, keep_ref, send_ref, begin + start, tile)


def weight_kernel(buffers, count, table_ref, scale_ref, *refs):
    pairs = [refs[2 * k : 2 * k + 2] for k in range(count)]
    keep_ref, send_ref, sums_ref = refs[2 * count :]
    begin = 0
    for left_ref, right_ref in pairs:
        weight_blocks(
            table_ref, scale_ref, buffers, left_ref, right_ref, keep_ref, send_ref, begin, sums_ref
        )
        begin += right_ref.shape[1]


def weight_gradient(name, table, scale, pairs, buffers):
    tokens, height = pairs[0][0].shape
    columns = [right.shape[1] for _, right in pairs]
    operands = [part for pair in pairs for part in pair]
    return call(
        functools.partial(weight_kernel, buffers, len(pairs)),
        name,
        [((HALF, height // BLOCKS, sum(columns)), bf16)] * 2,
        [SMEM, SMEM] + [VMEM] * len(operands),
        [VMEM] * 2,
        (table, scale, *operands),
        2 * tokens * height * sum(columns),
        10e6,
        [pltpu.VMEM((height, min(height, columns[0])), f32)],
        limit=LIMIT + 4 if height > 768 else LIMIT,
    )


def small_columns(
    buffers, count, scale_ref, owner_ref, sums_ref, attn_sums_ref, pre_ref, rows_ref, columns_ref, small_ref
):
    width = rows_ref.shape[1]
    rows = width // BLOCKS

    def weigh(ref, kind, columns=width):
        first = kind * buffers
        return sum(ref[first + b : first + b + 1, :columns] * scale_ref[b] for b in range(buffers))

    rows_ref[...] = jnp.zeros_like(rows_ref)
    kinds = [(attn_sums_ref, kind) for kind in (OUT_SUM, ATTN_GAIN_SUM, ATTN_SHIFT_SUM)]
    kinds += [(sums_ref, kind) for kind in (DOWN_SUM, GAIN_SUM, SHIFT_SUM)]
    for k, (ref, kind) in enumerate(kinds):
        rows_ref[k : k + 1] = weigh(ref, kind)
    pre = sum(pre_ref[b : b + 1] * scale_ref[b] for b in range(buffers))
    for at, total in ((QKV_AT, pre), (UP_AT, weigh(sums_ref, UP_SUM, sums_ref.shape[1]))):
        for k in range(total.shape[1] // width):
            rows_ref[at + k : at + k + 1] = total[:, k * width : (k + 1) * width]
    query = lax.broadcasted_iota(jnp.int32, (count, width), 0)
    total = jnp.zeros((count, width), f32)
    for b in range(buffers):
        row = QUERY_SUM * buffers + b
        mine = sums_ref[row : row + 1, :width] * scale_ref[b]
        total += jnp.where(query == owner_ref[b], mine, 0.0)
    rows_ref[QUERY_AT : QUERY_AT + count] = total
    columns_ref[...] = rows_ref[...].T
    lane = lax.broadcasted_iota(jnp.int32, (rows, LINE), 1)
    for block in range(BLOCKS):
        value = columns_ref[block * rows : (block + 1) * rows]
        for at, per in ((QKV_AT, 2), (UP_AT, 4)):
            for c in range(per):
                spot = (block * per + c) * rows
                source = columns_ref[spot % width : spot % width + rows]
                shift = (c - spot // width) % LINE
                if shift:
                    source = pltpu.roll(source, shift, 1)
                value = jnp.where(lane == at + c, source, value)
        small_ref[block * rows : (block + 1) * rows] = value


def attention_back_kernel(
    buffers, count, table_ref, scale_ref, owner_ref, qkv_ref, lse_ref, grad_ref, x_ref,
    sums_in_ref, attn_sums_ref, pre_hbm, keep_ref, send_ref, bias_ref,
    pre_ref, sums_ref, rows_ref, columns_ref, small_ref, sems,
):
    tokens, width = grad_ref.shape
    length, pairs = tokens // buffers, width // PAIR
    scale = 1.0 / math.sqrt(HEAD)

    def step(index, carry):
        rows = pl.ds(pl.multiple_of(index // pairs * length, length), length)
        lane = pl.multiple_of(index % pairs * PAIR, PAIR)
        query = qkv_ref[rows, pl.ds(lane, PAIR)]
        key = qkv_ref[rows, pl.ds(lane + width, PAIR)]
        value = qkv_ref[rows, pl.ds(lane + 2 * width, PAIR)]
        low = head_masks(query.shape)
        query = stacked(query, low)
        grad = stacked(grad_ref[rows, pl.ds(lane, PAIR)], low)
        probs = jnp.exp(mm_nt(key, query) * scale - lse_ref[index])
        grad_probs = mm_nt(value, grad)
        cross = jnp.sum(grad_probs * probs, axis=0, keepdims=True)
        grad_scores = (probs * (grad_probs - cross)).astype(bf16)
        grad_value = mm(probs.astype(bf16), grad)
        grad_key = mm(grad_scores, query) * scale
        grad_query = unstacked(mm_tn(key, grad_scores).T, low, length) * scale
        pre_ref[rows, pl.ds(lane, PAIR)] = grad_query.astype(bf16)
        pre_ref[rows, pl.ds(lane + width, PAIR)] = grad_key.astype(bf16)
        pre_ref[rows, pl.ds(lane + 2 * width, PAIR)] = grad_value.astype(bf16)
        return carry

    lax.fori_loop(0, buffers * pairs, step, 0, unroll=3)
    for buffer in range(buffers):
        rows = rows_of(buffer, length)
        for start, source in ((0, 0), (width, 2 * width)):
            piece = pre_ref[rows, source : source + width].astype(f32)
            bias_ref[buffer : buffer + 1, start : start + width] = jnp.sum(
                piece, axis=0, keepdims=True
            )
    stores = fetch([(pre_ref, pre_hbm)], sems)
    halves = keep_ref, send_ref
    weight_blocks(table_ref, scale_ref, buffers, x_ref, pre_ref, *halves, 0, sums_ref)
    small_columns(
        buffers, count, scale_ref, owner_ref, sums_in_ref, attn_sums_ref, bias_ref,
        rows_ref, columns_ref, small_ref,
    )
    place_rows(table_ref, small_ref, *halves, 3 * width, LINE)
    wait_all(stores)


def attention_gradient(table, scale, owner, count, qkv, lse, grad, x, sums, attn_sums, buffers):
    tokens, width = grad.shape
    length = tokens // buffers
    blocks = ((HALF, width // BLOCKS, 3 * width + LINE), bf16)
    return call(
        functools.partial(attention_back_kernel, buffers, count),
        "attention_gradient",
        [((tokens, 3 * width), bf16), blocks, blocks, ((buffers, 2 * width), f32)],
        [SMEM] * 3 + [VMEM] * 6,
        [HBM] + [VMEM] * 3,
        (table, scale, owner, qkv, lse, grad, x, sums, attn_sums),
        10 * tokens * length * width + 6 * tokens * width * width,
        20e6,
        [
            pltpu.VMEM((tokens, 3 * width), bf16),
            pltpu.VMEM((width, width), f32),
            pltpu.VMEM((LINE, width), f32),
            pltpu.VMEM((width, LINE), f32),
            pltpu.VMEM((width, LINE), f32),
            pltpu.SemaphoreType.DMA((1,)),
        ],
        exps=tokens * length * width // HEAD,
        limit=16,
    )


def states_kernel(
    buffers, scale_ref, res_hbm, pre_hbm, weight_hbm, out_hbm, res_ref, pre_ref, weight_ref, out_ref, sems
):
    length = res_ref.shape[0] // buffers
    spans = [pl.ds(b * length, length) for b in range(buffers)]
    loads = fetch([(weight_hbm, weight_ref)], sems)
    for b, span in enumerate(spans):
        pairs = [(pre_hbm.at[span], pre_ref.at[span]), (res_hbm.at[span], res_ref.at[span])]
        loads += fetch(pairs, sems, 1 + 2 * b)
    stores = []
    for b, span in enumerate(spans):
        wait_all(loads[:3] if b == 0 else loads[1 + 2 * b : 3 + 2 * b])
        grad = res_ref[span] + mm_nt(pre_ref[span], flat(weight_ref[...]))
        out_ref[span] = (grad * scale_ref[b]).astype(bf16)
        stores += fetch([(out_ref.at[span], out_hbm.at[span])], sems, 1 + 2 * buffers + b)
    wait_all(stores)


def states_gradient(scale, res, pre, weight, buffers):
    tokens, width = res.shape
    return call(
        functools.partial(states_kernel, buffers),
        "states_gradient",
        [((tokens, width), bf16)],
        [SMEM] + [HBM] * 3,
        [HBM],
        (scale, res, pre, weight),
        6 * tokens * width * width,
        8e6,
        [
            pltpu.VMEM(res.shape, f32),
            pltpu.VMEM(pre.shape, bf16),
            pltpu.VMEM(weight.shape, bf16),
            pltpu.VMEM(res.shape, bf16),
            pltpu.SemaphoreType.DMA((1 + 3 * buffers,)),
        ],
        limit=16,
    )[0]


def body(
    slot_states, answer_tags, slot_mask, retrieval, query_emb, qkv_weight, qkv_bias, out_weight,
    out_bias, attn_gain, attn_shift, up_weight, up_bias, down_weight, down_bias, ffn_gain, ffn_shift,
):
    group_count = lax.axis_size(AXES)
    device_index = lax.axis_index(AXES)
    tuned = group_count == BLOCKS
    buffers, length, width = slot_states.shape
    query_count, slot_count = slot_mask.shape
    tokens = buffers * length
    x = slot_states.reshape(tokens, width)

    running = jnp.cumsum(slot_mask.reshape(-1), dtype=jnp.int32)
    slot_ranks = jnp.arange(buffers, dtype=jnp.int32) * group_count + device_index
    places = jnp.sum(
        (running[None, :] <= slot_ranks[:, None]).astype(jnp.int32), axis=1, dtype=jnp.int32
    )
    slot_pick = places[:, None] == jnp.arange(query_count * slot_count, dtype=jnp.int32)[None, :]
    owner = places // slot_count
    owner_mask = owner[:, None] == jnp.arange(query_count, dtype=jnp.int32)[None]
    prior_score = jnp.sum(jnp.where(slot_pick, retrieval.reshape(-1)[None, :], 0.0), axis=1)

    order = Order(tuned)
    if tuned:
        table = position_table(device_index)
        vectors = (out_bias, attn_gain, attn_shift, down_bias, ffn_gain, ffn_shift)
        g1 = Gather(order, pack_first(qkv_weight, vectors, qkv_bias, up_bias, query_emb))
        g2 = Gather(order, jnp.concatenate([out_weight, up_weight], axis=1)[None])
        g3 = Gather(order, down_weight[None])
        g1.start_line()
        g1.join_line()
        g1.start_near()
        g2.start_line(g1.held)
        g1.join_near()
        g1.start_other(g1.near, owner, prior_score)
        g2.join_line()
        g2.start_near()
        g2.start_other()
        g1.join_last()
        g1.join_other()
        g3.start_line(g2.held)
        first = g1.pieces()
        vectors, bias, up_bias_all = unpack_small(table, first, 3 * width, query_count)
        order.mark(vectors)
    else:
        table = jnp.arange(BLOCKS, dtype=jnp.int32)
        everything = lambda part: lax.all_gather(part, AXES, axis=0, tiled=True).astype(f32)
        first = gather_plain(qkv_weight)
        second = gather_plain(jnp.concatenate([out_weight, up_weight], axis=1))
        third = gather_plain(down_weight)
        vectors = jnp.stack(
            [
                everything(part)
                for part in (out_bias, attn_gain, attn_shift, down_bias, ffn_gain, ffn_shift)
            ]
        )
        bias = everything(qkv_bias)
        bias = jnp.concatenate([bias[:width], jnp.zeros((width,), f32), bias[width:]]).reshape(1, -1)
        up_bias_all = everything(up_bias).reshape(1, -1)
        query_table = lax.all_gather(query_emb, AXES, axis=1, tiled=True).astype(f32)
        vectors = jnp.concatenate([vectors, jnp.zeros((VECTORS - SIX, width), f32), query_table])

    qkv, wqkv = qkv_forward(table, order.place(x), bias, first)
    if tuned:
        order.mark(qkv)
        g3.join_line()
        g3.start_near()
        g2.join_near()
    context, lse = attention_forward(order.place(qkv), buffers)
    if tuned:
        order.mark(context)
        g3.start_other(order.last)
        g2.join_other()
        g2.join_last()
        g3.join_near()
        second = g2.pieces()
    hidden, act, slope, normed, inverse, wout, wup = up_forward(
        table, x, context, vectors, up_bias_all, second
    )
    if tuned:
        order.mark(act)
        g3.join_other()
        g3.join_last()
        third = g3.pieces()
    mixed, like, normed_out, sides, wdown, mixed_out = down_forward(
        table, owner, hidden, act, vectors, answer_tags, third, buffers
    )

    scores = like[:, 0] + prior_score
    masked = jnp.where(owner_mask, scores[:, None], neg_fill)
    local_peak = jnp.max(masked, axis=0)
    local_total = jnp.sum(jnp.where(owner_mask, jnp.exp(masked - local_peak[None, :]), 0.0), axis=0)
    merged = (local_peak, local_total)
    if tuned:
        order.mark(local_total)
        merged = merge_join(order, merged, merge_start(merged, (CORE_BIT,)))
        got = merge_start(merged, LINE_MASKS)
    else:
        merged = merge_plain(merged)

    grad_low, grad_up, grad_res, sums = up_backward(
        owner, order.place(mixed), normed_out, sides, slope, vectors, wdown, buffers
    )
    if tuned:
        order.mark(grad_low)
        merged = merge_join(order, merged, got)
        got = merge_start(merged, (X_BIT, Y_BIT, X_BIT | Y_BIT))
    grad_hidden, grad_attn, grad_context, attn_sums = hidden_backward(
        order.place(grad_res), grad_up, normed, inverse, vectors, wup, wout, buffers
    )
    if tuned:
        order.mark(grad_attn)
        merged = merge_join(order, merged, got)
    totals = merged[0] + jnp.log(merged[1])
    scale = jnp.sum(
        jnp.where(owner_mask, jnp.exp(scores[:, None] - totals[None, :]), 0.0), axis=1
    )

    pairs = [(context, grad_attn), (hidden, grad_up)]
    halves2 = weight_gradient("up_gradient", table, scale, pairs, buffers)
    if tuned:
        order.mark(halves2[1])
        s2 = Scatter(order, *halves2)
        s2.start_core()
    pairs = [(order.place(act), grad_low)]
    halves3 = weight_gradient("down_gradient", table, scale, pairs, buffers)
    if tuned:
        order.mark(halves3[1])
        s3 = Scatter(order, *halves3)
        s3.start_core()
        s2.join_core()
        s2.start_other()
    grad_pre, *halves1, pre_sums = attention_gradient(
        table, scale, owner, query_count, qkv, lse, order.place(grad_context), x, sums, attn_sums, buffers
    )
    if tuned:
        order.mark(halves1[1])
        s1 = Scatter(order, *halves1)
        s1.start_core()
        s2.join_last()
        s3.join_core()
    states = states_gradient(scale, grad_hidden, order.place(grad_pre), wqkv, buffers)
    if tuned:
        order.mark(states)
        s3.start_other(order.last)
        s2.join_sides()
        s1.join_core()
        s3.join_last()
        s1.join_last()
        s1.start_other(order.last)
        s3.join_sides()
        second_grad = s2.finish(0, width), s2.finish(width)
        order.mark(second_grad[1])
        s1.join_sides()
        third_grad = s3.finish()
        order.mark(third_grad)
        totals = order.place(totals)
        first_grad, *six, qkv_bias_sum, up_bias_sum, query_sum = split_first(
            s1.own, [order.place(part) for part in s1.line], query_count
        )
    else:
        third_grad = scatter_plain(*halves3)
        cut = lambda halves, start, end: scatter_plain(*(half[:, :, start:end] for half in halves))
        second_grad = cut(halves2, 0, width), cut(halves2, width, width + up_weight.shape[1])
        first_grad = cut(halves1, 0, 3 * width)
    if not tuned:
        weigh = lambda part: jnp.sum(scale[:, None] * part, axis=0)
        mine = lambda part: lax.psum_scatter(weigh(part), AXES, scatter_dimension=0, tiled=True)
        rows_for = lambda part, kind: part[kind * buffers : (kind + 1) * buffers, :width]
        six = [mine(rows_for(attn_sums, kind)) for kind in (OUT_SUM, ATTN_GAIN_SUM, ATTN_SHIFT_SUM)]
        six += [mine(rows_for(sums, kind)) for kind in (DOWN_SUM, GAIN_SUM, SHIFT_SUM)]
        qkv_bias_sum, up_bias_sum = mine(pre_sums), mine(sums[:buffers])
        weighed = jnp.where(owner_mask, scale[:, None], 0.0)
        query_sum = jnp.sum(weighed[:, :, None] * rows_for(sums, QUERY_SUM)[:, None, :], axis=0)
        query_sum = lax.psum_scatter(query_sum, AXES, scatter_dimension=1, tiled=True)
    loss = -jnp.sum(totals)
    return (
        mixed_out.reshape(slot_states.shape),
        loss,
        states.reshape(slot_states.shape),
        query_sum,
        first_grad,
        qkv_bias_sum,
        second_grad[0],
        six[0],
        six[1],
        six[2],
        second_grad[1],
        up_bias_sum,
        third_grad,
        six[3],
        six[4],
        six[5],
    )


def solution(mesh):
    split = P(AXES)
    in_specs = (split, split, P(), P(), P(None, AXES)) + (split,) * 12
    out_specs = (split, P(), split, P(None, AXES)) + (split,) * 12
    return jax.shard_map(body, mesh=mesh, in_specs=in_specs, out_specs=out_specs, check_vma=False)
```

```python
import functools
import math

import jax
import jax.numpy as jnp
import numpy as np
from jax import lax
from jax.experimental import pallas as pl
from jax.experimental.pallas import tpu as pltpu
from jax.sharding import PartitionSpec as P

HEAD = 64
PAIR = 2 * HEAD
LINE = 128
AXES = ("dp", "fsdp")
X_BIT, CORE_BIT, Z_FAR, Z_NEAR, Y_BIT = 16, 8, 4, 2, 1
BLOCKS = 32
HALF = BLOCKS // 2
SHARE = 0.02
LIMIT = 16

eps_norm = 1e-12
loss_scale = 65536.0
neg_fill = -1e30
f32 = jnp.float32
bf16 = jnp.bfloat16
VMEM = pl.BlockSpec(memory_space=pltpu.VMEM)
SMEM = pl.BlockSpec(memory_space=pltpu.SMEM)
HBM = pl.BlockSpec(memory_space=pltpu.HBM)
ANYWHERE = pl.BlockSpec(memory_space=pl.ANY)


def device_offsets(first, second):
    masks = (Z_FAR, Z_NEAR, first, second)
    return np.array(
        [sum(m for k, m in enumerate(masks) if p >> k & 1) for p in range(HALF)], np.int32
    )


def position_table(device_index):
    even = device_offsets(X_BIT, Y_BIT)
    odd = device_offsets(Y_BIT, X_BIT)
    table_even = jnp.asarray(np.concatenate([even, odd ^ CORE_BIT]))
    table_odd = jnp.asarray(np.concatenate([odd, even ^ CORE_BIT]))
    core = (device_index // CORE_BIT) % 2
    return jnp.where(core == 0, table_even, table_odd) ^ device_index


def exchange(value, even_mask, odd_mask):
    pairs = [(i, i ^ (odd_mask if i & CORE_BIT else even_mask)) for i in range(BLOCKS)]
    return lax.ppermute(value, AXES, pairs)


def after(value, *earlier):
    return lax.optimization_barrier((value, *earlier))[0]


SIDE, OTHER, CORES = (X_BIT, Y_BIT), (Y_BIT, X_BIT), (CORE_BIT, CORE_BIT)
LINE_MASKS = (Z_FAR, Z_NEAR, Z_FAR | Z_NEAR)


class Order:
    def __init__(self, tuned):
        self.tuned, self.last = tuned, None

    def place(self, value):
        if self.tuned and self.last is not None:
            return after(value, self.last)
        return value

    def mark(self, value):
        self.last = value


class Gather:
    def __init__(self, order, shard):
        self.order, self.shard = order, shard

    def start_line(self, *earlier):
        own = after(self.shard, *earlier) if earlier else self.shard
        self.got = [exchange(own, mask, mask) for mask in LINE_MASKS]

    def join_line(self):
        got = [self.order.place(part) for part in self.got]
        self.held = lax.optimization_barrier(jnp.concatenate([self.shard, *got]))
        self.order.mark(self.held)

    def start_near(self, *earlier):
        held = after(self.held, *earlier) if earlier else self.held
        self.near = exchange(held, *SIDE)

    def start_other(self, *earlier):
        held = after(self.held, *earlier) if earlier else self.held
        self.other = exchange(held, *OTHER)
        self.far_held = exchange(held, *CORES)

    def join_near(self):
        self.near = self.order.place(self.near)
        self.order.mark(self.near)
        self.last = exchange(self.near, *OTHER)
        self.far_near = exchange(self.near, *CORES)

    def join_other(self):
        self.other = self.order.place(self.other)
        self.order.mark(self.other)
        self.far_other = exchange(self.other, *CORES)

    def join_last(self):
        self.last = self.order.place(self.last)
        self.order.mark(self.last)
        self.far_last = exchange(self.last, *CORES)

    def pieces(self):
        far = (self.far_held, self.far_near, self.far_other, self.far_last)
        far = [self.order.place(part) for part in far]
        self.order.mark(far[-1])
        return (self.held, self.near, self.other, self.last, *far)


def gather_plain(part):
    whole = lax.all_gather(part, AXES, axis=0, tiled=True)
    blocks = whole.reshape(BLOCKS, -1, whole.shape[1])
    return tuple(blocks[4 * k : 4 * k + 4] for k in range(8))


def add_low(first, second):
    return (first.astype(f32) + second.astype(f32)).astype(bf16)


def add_up_parts(*parts):
    return sum(part.astype(f32) for part in parts)


class Scatter:
    def __init__(self, order, keep, send):
        self.order, self.keep, self.send = order, keep, send

    def start_core(self, *earlier):
        self.got = exchange(after(self.send, *earlier) if earlier else self.send, *CORES)

    def quarter(self, k, *more):
        span = slice(4 * k, 4 * k + 4)
        return add_up_parts(self.keep[span], self.got[span], *more)

    def join_core(self):
        self.got = self.order.place(self.got)
        last, other = self.quarter(3).astype(bf16), self.quarter(2).astype(bf16)
        self.last = exchange(last, *OTHER)
        self.other = other
        self.order.mark(other)

    def start_other(self, *earlier):
        other = after(self.other, *earlier) if earlier else self.other
        self.other = exchange(other, *OTHER)

    def join_last(self):
        near = self.quarter(1, self.order.place(self.last)).astype(bf16)
        self.near = exchange(near, *SIDE)
        self.order.mark(near)

    def join_sides(self):
        more = self.order.place(self.other), self.order.place(self.near)
        block = lambda p: add_up_parts(self.keep[p], self.got[p], more[0][p], more[1][p])
        sends = [block(p).astype(bf16) for p in (1, 2, 3)]
        self.line = [exchange(part, mask, mask) for part, mask in zip(sends, LINE_MASKS)]
        self.own = block(0)
        self.order.mark(sends[-1])

    def finish(self, start=0, width=None):
        end = self.own.shape[1] if width is None else start + width
        cut = lambda part: part[..., start:end]
        return add_up_parts(cut(self.own), *(cut(self.order.place(part)) for part in self.line))


def scatter_plain(keep, send):
    blocks = jnp.concatenate([keep, send])
    whole = blocks.reshape(-1, blocks.shape[2])
    return lax.psum_scatter(whole, AXES, scatter_dimension=0, tiled=True).astype(f32)


def merge_start(pair, masks):
    both = jnp.stack(pair)
    return [exchange(both, mask, mask) for mask in masks]


def merge_join(order, pair, got):
    got = [order.place(part) for part in got]
    peak = functools.reduce(jnp.maximum, [part[0] for part in got], pair[0])
    total = pair[1] * jnp.exp(pair[0] - peak)
    total += sum(part[1] * jnp.exp(part[0] - peak) for part in got)
    order.mark(total)
    return (peak, total)


def merge_plain(pair):
    peak = lax.pmax(pair[0], AXES)
    return (peak, lax.psum(pair[1] * jnp.exp(pair[0] - peak), AXES))


def call(
    kernel, name, outs, in_specs, out_specs, args, flops, moved, scratch=(), exps=0, limit=None
):
    args = [
        pltpu.with_memory_space_constraint(arg, pltpu.HBM) if spec is HBM else arg
        for arg, spec in zip(args, in_specs)
    ]
    return pl.pallas_call(
        kernel,
        out_shape=[
            pltpu.HBM(shape, dtype) if spec is HBM else jax.ShapeDtypeStruct(shape, dtype)
            for (shape, dtype), spec in zip(outs, out_specs)
        ],
        in_specs=in_specs,
        out_specs=out_specs,
        scratch_shapes=list(scratch),
        compiler_params=pltpu.CompilerParams(vmem_limit_bytes=(limit or LIMIT) * 2**20),
        cost_estimate=pl.CostEstimate(
            flops=int(flops * SHARE), bytes_accessed=int(moved * SHARE), transcendentals=int(exps * SHARE)
        ),
        name=name,
    )(*args)


def mm(first, second):
    return jnp.dot(first, second, preferred_element_type=f32)


def mm_nt(first, second):
    return lax.dot_general(first, second, (((1,), (1,)), ((), ())), preferred_element_type=f32)


def mm_tn(first, second):
    return lax.dot_general(first, second, (((0,), (0,)), ((), ())), preferred_element_type=f32)


def row_mean(value):
    return jnp.mean(value, axis=-1, keepdims=True)


def block_copies(table_ref, pieces, start, width, target, sems, spots=range(BLOCKS)):
    copies = [
        pltpu.make_async_copy(
            pieces[spot // 4].at[spot % 4, :, pl.ds(start, width)],
            target.at[table_ref[spot]],
            sems.at[spot],
        )
        for spot in spots
    ]
    for copy in copies:
        copy.start()
    return copies


def fetch(pairs, sems, first=0):
    copies = [
        pltpu.make_async_copy(source, target, sems.at[first + k])
        for k, (source, target) in enumerate(pairs)
    ]
    for copy in copies:
        copy.start()
    return copies


def wait_all(copies):
    for copy in copies:
        copy.wait()


def flat(value):
    return value.reshape(-1, value.shape[-1])


SIX, QKV_AT, UP_AT, QUERY_AT = 6, 6, 8, 12
VECTORS = 8


def pack_kernel(weight_hbm, *refs):
    sources, out_ref, parts, held_ref, sems = refs[: SIX + 3], refs[SIX + 3], refs[SIX + 4 : -2], *refs[-2:]
    rows, width = out_ref.shape[1], out_ref.shape[2] - LINE
    copies = fetch(zip(sources, parts), sems)
    copies += fetch([(weight_hbm, out_ref.at[0, :, pl.ds(0, width)])], sems, len(parts))
    vectors, (qkv_ref, up_ref, query_ref) = parts[:SIX], parts[SIX:]
    held_ref[...] = jnp.zeros_like(held_ref)
    wait_all(copies)
    for k, ref in enumerate(vectors):
        held_ref[k : k + 1, :rows] = ref[...].astype(f32)
    for at, ref, count in ((QKV_AT, qkv_ref, 2), (UP_AT, up_ref, 4)):
        value = ref[...].astype(f32)
        for c in range(count):
            held_ref[at + c : at + c + 1, :rows] = value[:, c * rows : (c + 1) * rows]
    count = query_ref.shape[0]
    held_ref[QUERY_AT : QUERY_AT + count, :rows] = query_ref[...].astype(f32)
    out_ref[0, :, width:] = held_ref[...].T[:rows].astype(bf16)


def pack_first(weight, vectors, qkv_bias, up_bias, query_emb):
    rows, width = weight.shape
    parts = [part.reshape(1, -1) for part in (*vectors, qkv_bias, up_bias)] + [query_emb]
    return call(
        pack_kernel,
        "pack_first",
        [((1, rows, width + LINE), bf16)],
        [HBM] * (1 + len(parts)),
        [VMEM],
        [weight, *parts],
        0,
        1e5,
        [pltpu.VMEM(part.shape, part.dtype) for part in parts]
        + [pltpu.VMEM((LINE, LINE), f32), pltpu.SemaphoreType.DMA((len(parts) + 1,))],
    )[0]


def unpack_kernel(
    start, count, table_ref, p0, p1, p2, p3, p4, p5, p6, p7, consts_ref, qkv_ref, up_ref,
    held_ref, qkv_wide, up_wide, sems,
):
    wait_all(block_copies(table_ref, (p0, p1, p2, p3, p4, p5, p6, p7), start, LINE, held_ref, sems))
    rows = held_ref.shape[1]
    every = flat(held_ref[...]).astype(f32)
    for block in range(BLOCKS):
        value = every[block * rows : (block + 1) * rows]
        for c in range(2):
            qkv_wide[(2 * block + c) * rows : (2 * block + c + 1) * rows] = value
        for c in range(4):
            up_wide[(4 * block + c) * rows : (4 * block + c + 1) * rows] = value
    turned = every.T
    consts_ref[:VECTORS] = turned[:VECTORS]
    consts_ref[VECTORS:] = turned[QUERY_AT : QUERY_AT + count]

    def line(wide, at, count):
        picks = lax.broadcasted_iota(jnp.int32, (8, LINE), 1) == at + lax.broadcasted_iota(
            jnp.int32, (8, LINE), 0
        )
        found = mm_nt(picks.astype(bf16), wide[...].astype(bf16))
        part = lax.broadcasted_iota(jnp.int32, found.shape, 1) // rows % count
        mine = part == lax.broadcasted_iota(jnp.int32, found.shape, 0)
        return jnp.sum(jnp.where(mine, found, 0.0), axis=0, keepdims=True)

    up_ref[...] = line(up_wide, UP_AT, 4)
    width = held_ref.shape[0] * rows
    bias = line(qkv_wide, QKV_AT, 2)
    qkv_ref[:, :width] = bias[:, :width]
    qkv_ref[:, width : 2 * width] = jnp.zeros((1, width), f32)
    qkv_ref[:, 2 * width :] = bias[:, width:]


def unpack_small(table, pieces, start, query_count):
    rows = pieces[0].shape[1]
    width = BLOCKS * rows
    return call(
        functools.partial(unpack_kernel, start, query_count),
        "unpack_small",
        [((VECTORS + query_count, width), f32), ((1, 3 * width), f32), ((1, 4 * width), f32)],
        [SMEM] + [HBM] * 8,
        [VMEM] * 3,
        (table, *pieces),
        0,
        1e6,
        [
            pltpu.VMEM((BLOCKS, rows, LINE), bf16),
            pltpu.VMEM((2 * width, LINE), f32),
            pltpu.VMEM((4 * width, LINE), f32),
            pltpu.SemaphoreType.DMA((BLOCKS,)),
        ],
    )


def split_kernel(own_ref, g0_ref, g1_ref, g2_ref, first_ref, *refs):
    vectors, (qkv_ref, up_ref, query_ref, held_ref) = refs[:SIX], refs[SIX:]
    rows, width = first_ref.shape
    total = own_ref[...] + (
        g0_ref[...].astype(f32) + g1_ref[...].astype(f32) + g2_ref[...].astype(f32)
    )
    first_ref[...] = total[:, :width]
    held_ref[...] = jnp.zeros_like(held_ref)
    held_ref[:rows] = total[:, width:]
    turned = held_ref[...].T
    for k, ref in enumerate(vectors):
        ref[...] = turned[k : k + 1, :rows]
    for c in range(2):
        qkv_ref[:, c * rows : (c + 1) * rows] = turned[QKV_AT + c : QKV_AT + c + 1, :rows]
    for c in range(4):
        up_ref[:, c * rows : (c + 1) * rows] = turned[UP_AT + c : UP_AT + c + 1, :rows]
    query_ref[...] = turned[QUERY_AT : QUERY_AT + query_ref.shape[0], :rows]


def split_first(own, got, query_count):
    rows, width = own.shape[0], own.shape[1] - LINE
    outs = call(
        split_kernel,
        "split_first",
        [((rows, width), f32)]
        + [((1, rows), f32)] * SIX
        + [((1, 2 * rows), f32), ((1, 4 * rows), f32), ((query_count, rows), f32)],
        [VMEM] * 4,
        [VMEM] * (SIX + 4),
        (own, *got),
        0,
        1e6,
        [pltpu.VMEM((LINE, LINE), f32)],
    )
    return [outs[0]] + [part.reshape(-1) for part in outs[1:-1]] + [outs[-1]]


def block_scratch(rows, width):
    return [pltpu.VMEM((BLOCKS, rows, width), bf16), pltpu.SemaphoreType.DMA((BLOCKS,))]


def head_masks(shape):
    lane = lax.broadcasted_iota(jnp.int32, shape, 1)
    return lane < HEAD


def stacked(pair, low):
    zero = jnp.zeros_like(pair)
    return jnp.concatenate([jnp.where(low, pair, zero), jnp.where(low, zero, pair)])


def unstacked(value, low, length):
    return jnp.where(low, value[:length], value[length:])


def rows_of(buffer, length):
    return slice(buffer * length, (buffer + 1) * length)


def rows_of(buffer, length):
    return slice(buffer * length, (buffer + 1) * length)


def qkv_kernel(
    table_ref, x_ref, bias_ref, p0, p1, p2, p3, p4, p5, p6, p7, qkv_ref, weight_hbm, weight_ref, sems, sems_out
):
    width = x_ref.shape[1]
    wait_all(block_copies(table_ref, (p0, p1, p2, p3, p4, p5, p6, p7), 0, 3 * width, weight_ref, sems))
    stores = fetch([(weight_ref, weight_hbm)], sems_out)
    x = x_ref[...]
    for part in range(3):
        span = slice(part * width, (part + 1) * width)
        weight = flat(weight_ref[:, :, span])
        qkv_ref[:, span] = (mm(x, weight) + bias_ref[:, span]).astype(bf16)
    wait_all(stores)


def qkv_forward(table, x, bias, pieces):
    tokens, width = x.shape
    rows = pieces[0].shape[1]
    return call(
        qkv_kernel,
        "qkv_forward",
        [((tokens, 3 * width), bf16), ((BLOCKS, rows, 3 * width), bf16)],
        [SMEM, VMEM, VMEM] + [HBM] * 8,
        [VMEM, HBM],
        (table, x, bias, *pieces),
        6 * tokens * width * width,
        10e6,
        block_scratch(rows, 3 * width) + [pltpu.SemaphoreType.DMA((1,))],
    )


def attention_kernel(buffers, qkv_ref, context_ref, lse_ref):
    tokens, width = context_ref.shape
    length, pairs = tokens // buffers, width // PAIR
    scale = 1.0 / math.sqrt(HEAD)

    def step(index, carry):
        rows = pl.ds(pl.multiple_of(index // pairs * length, length), length)
        lane = pl.multiple_of(index % pairs * PAIR, PAIR)
        query = qkv_ref[rows, pl.ds(lane, PAIR)]
        key = qkv_ref[rows, pl.ds(lane + width, PAIR)]
        value = qkv_ref[rows, pl.ds(lane + 2 * width, PAIR)]
        low = head_masks(query.shape)
        scores = mm_nt(key, stacked(query, low)) * scale
        peak = jnp.max(scores, axis=0, keepdims=True)
        powers = jnp.exp(scores - peak)
        total = jnp.sum(powers, axis=0, keepdims=True)
        probs = (powers * (1.0 / total)).astype(bf16)
        mixed = mm_tn(value, probs).T
        context_ref[rows, pl.ds(lane, PAIR)] = unstacked(mixed, low, length).astype(bf16)
        lse_ref[index] = peak + jnp.log(total)
        return carry

    lax.fori_loop(0, buffers * pairs, step, 0, unroll=4)


def attention_forward(qkv, buffers):
    tokens, width = qkv.shape[0], qkv.shape[1] // 3
    length = tokens // buffers
    lse = (buffers * (width // PAIR), 1, 2 * length)
    return call(
        functools.partial(attention_kernel, buffers),
        "attention_forward",
        [((tokens, width), bf16), (lse, f32)],
        [VMEM],
        [VMEM] * 2,
        (qkv,),
        4 * tokens * width * length,
        4e6,
        exps=tokens * length * width // HEAD,
    )


def normed_rows(residual):
    center = residual - row_mean(residual)
    inverse = lax.rsqrt(row_mean(center * center) + eps_norm)
    return center * inverse, inverse


def up_kernel(
    table_ref, x_ref, context_ref, vectors_ref, bias_ref, p0, p1, p2, p3, p4, p5, p6, p7,
    hidden_hbm, act_hbm, slope_hbm, normed_hbm, inverse_hbm, wout_hbm, wup_hbm,
    hidden_ref, act_ref, slope_ref, normed_ref, inverse_ref, wout_ref, wup_ref, sems_out, sems_up, sems,
):
    pieces = (p0, p1, p2, p3, p4, p5, p6, p7)
    width, units = x_ref.shape[1], wup_ref.shape[2]
    first = block_copies(table_ref, pieces, 0, width, wout_ref, sems_out)
    copies = block_copies(table_ref, pieces, width, units, wup_ref, sems_up)
    wait_all(first)
    out = mm(context_ref[...], flat(wout_ref[...])) + vectors_ref[0:1]
    normed, inverse = normed_rows(x_ref[...].astype(f32) + out)
    normed_ref[...] = normed
    inverse_ref[...] = jnp.broadcast_to(inverse, inverse_ref.shape)
    hidden_ref[...] = (normed * vectors_ref[1:2] + vectors_ref[2:3]).astype(bf16)
    wait_all(copies)
    pairs = [
        (wup_ref, wup_hbm),
        (wout_ref, wout_hbm),
        (normed_ref, normed_hbm),
        (inverse_ref, inverse_hbm),
        (hidden_ref, hidden_hbm),
    ]
    stores = fetch(pairs, sems)
    wide = 512
    for part in range(units // wide):
        span = pl.ds(part * wide, wide)
        up = mm(hidden_ref[...], flat(wup_ref[:, :, span])) + bias_ref[:, span]
        chance = 0.5 + 0.5 * lax.erf(up * math.sqrt(0.5))
        act_ref[:, span] = (up * chance).astype(bf16)
        density = jnp.exp(up * up * -0.5) * (1.0 / math.sqrt(2.0 * math.pi))
        slope_ref[:, span] = (chance + up * density).astype(bf16)
        pairs = [
            (act_ref.at[:, span], act_hbm.at[:, span]),
            (slope_ref.at[:, span], slope_hbm.at[:, span]),
        ]
        stores += fetch(pairs, sems, 5 + 2 * part)
    wait_all(stores)


def up_forward(table, x, context, vectors, bias, pieces):
    tokens, width = x.shape
    rows, units = pieces[0].shape[1], pieces[0].shape[2] - width
    outs = [
        ((tokens, width), bf16),
        ((tokens, units), bf16),
        ((tokens, units), bf16),
        ((tokens, width), f32),
        ((tokens, LINE), f32),
        ((BLOCKS, rows, width), bf16),
        ((BLOCKS, rows, units), bf16),
    ]
    return call(
        up_kernel,
        "up_forward",
        outs,
        [SMEM] + [VMEM] * 4 + [HBM] * 8,
        [HBM] * 7,
        (table, x, context, vectors, bias, *pieces),
        2 * tokens * width * (width + units),
        20e6,
        [pltpu.VMEM(*out) for out in outs]
        + [pltpu.SemaphoreType.DMA((BLOCKS,)), pltpu.SemaphoreType.DMA((BLOCKS,))]
        + [pltpu.SemaphoreType.DMA((5 + 2 * (units // 512),))],
        exps=2 * tokens * units,
        limit=28,
    )


def chosen_row(owner_ref, vectors_ref, buffer):
    queries = vectors_ref[VECTORS:]
    query = lax.broadcasted_iota(jnp.int32, queries.shape, 0)
    return jnp.sum(jnp.where(query == owner_ref[buffer], queries, 0.0), axis=0, keepdims=True)


QUARTERS = (((0, 1, 2), 0), ((3,), 12), ((4, 5, 6), 16), ((7,), 28))


def down_kernel(
    buffers, table_ref, owner_ref, hidden_hbm, act_hbm, vectors_hbm, tags_ref, p0, p1, p2, p3, p4, p5, p6, p7,
    mixed_ref, like_ref, normed_ref, sides_ref, wdown_ref, mixed_hbm,
    hidden_ref, act_ref, vectors_ref, down_ref, sems, sems_held,
):
    tokens, width = hidden_ref.shape
    length = tokens // buffers
    pieces = (p0, p1, p2, p3, p4, p5, p6, p7)
    count = len(QUARTERS)
    part, wide = BLOCKS // count, act_ref.shape[2]
    places = [table_ref[spot] // part for _, spot in QUARTERS]
    loads = []
    for k, (names, _) in enumerate(QUARTERS):
        lanes = pl.ds(pl.multiple_of(places[k] * wide, LINE), wide)
        copies = fetch([(act_hbm.at[:, lanes], act_ref.at[k])], sems_held, k)
        for name in names:
            spots = range(4 * name, 4 * name + 4)
            copies += block_copies(table_ref, pieces, 0, width, wdown_ref, sems, spots)
        loads.append(copies)
    last = fetch([(hidden_hbm, hidden_ref), (vectors_hbm, vectors_ref)], sems_held, count)

    def product(k, rows):
        weight = flat(wdown_ref[pl.ds(places[k] * part, part)])
        return mm(act_ref[k, rows], weight)

    for k in range(count - 1):
        wait_all(loads[k])
        value = product(k, slice(None))
        down_ref[...] = value if k == 0 else down_ref[...] + value
    wait_all(loads[-1] + last)
    stores = []
    for buffer in range(buffers):
        rows = rows_of(buffer, length)
        down = down_ref[rows] + product(count - 1, rows) + vectors_ref[3:4]
        normed, inverse = normed_rows(hidden_ref[rows].astype(f32) + down)
        normed_ref[rows] = normed
        mixed = (normed * vectors_ref[4:5] + vectors_ref[5:6]).astype(bf16)
        mixed_ref[rows] = mixed
        span = pl.ds(buffer * length, length)
        stores += fetch([(mixed_ref.at[span], mixed_hbm.at[span])], sems_held, count + 2 + buffer)
        chosen = chosen_row(owner_ref, vectors_ref, buffer).astype(bf16)
        logits = mm_nt(jnp.broadcast_to(chosen, (8, chosen.shape[1])), mixed)[0:1]
        tags = tags_ref[buffer : buffer + 1].astype(f32)
        tail = jnp.log(1.0 + jnp.exp(-jnp.abs(logits)))
        log_yes = jnp.minimum(logits, 0.0) - tail
        log_no = jnp.minimum(-logits, 0.0) - tail
        like = jnp.sum(tags * log_yes + (1.0 - tags) * log_no, axis=1, keepdims=True) / length
        like_ref[buffer : buffer + 1] = jnp.broadcast_to(like, (1, LINE))
        pull = (tags - 1.0 / (1.0 + jnp.exp(-logits))) * (-loss_scale / length)
        pull = jnp.broadcast_to(pull, (LINE, length)).T
        lane = lax.broadcasted_iota(jnp.int32, (length, LINE), 1)
        sides_ref[rows] = jnp.where(lane < HEAD, inverse, pull)
    wait_all(stores)


def down_forward(table, owner, hidden, act, vectors, tags, pieces, buffers):
    tokens, width = hidden.shape
    rows, units = pieces[0].shape[1], act.shape[1]
    return call(
        functools.partial(down_kernel, buffers),
        "down_forward",
        [
            ((tokens, width), bf16),
            ((buffers, LINE), f32),
            ((tokens, width), f32),
            ((tokens, LINE), f32),
            ((BLOCKS, rows, width), bf16),
            ((tokens, width), bf16),
        ],
        [SMEM, SMEM, HBM, HBM, HBM, VMEM] + [HBM] * 8,
        [VMEM] * 5 + [HBM],
        (table, owner, hidden, act, vectors, tags, *pieces),
        2 * tokens * width * units,
        20e6,
        [
            pltpu.VMEM((tokens, width), bf16),
            pltpu.VMEM((len(QUARTERS), tokens, units // len(QUARTERS)), bf16),
            pltpu.VMEM(vectors.shape, f32),
            pltpu.VMEM((tokens, width), f32),
            pltpu.SemaphoreType.DMA((BLOCKS,)),
            pltpu.SemaphoreType.DMA((len(QUARTERS) + 2 + buffers,)),
        ],
        limit=18,
    )


UP_SUM, GAIN_SUM, SHIFT_SUM, QUERY_SUM, DOWN_SUM = range(5)
ATTN_GAIN_SUM, ATTN_SHIFT_SUM, OUT_SUM = range(3)


def adder(sums_ref, buffers):
    def add_up(kind, buffer, value, start=0):
        row = kind * buffers + buffer
        sums_ref[row : row + 1, start : start + value.shape[1]] = jnp.sum(
            value, axis=0, keepdims=True
        )

    return add_up


def up_back_kernel(
    buffers, owner_ref, mixed_ref, normed_ref, sides_ref, slope_ref, vectors_ref, wdown_ref,
    low_ref, up_ref, res_ref, sums_ref,
):
    tokens, width = mixed_ref.shape
    units = slope_ref.shape[1]
    length = tokens // buffers
    sums_ref[...] = jnp.zeros_like(sums_ref)
    add_up = adder(sums_ref, buffers)
    for buffer in range(buffers):
        rows = rows_of(buffer, length)
        normed = normed_ref[rows]
        inverse, pull = sides_ref[rows, 0:1], sides_ref[rows, HEAD : HEAD + 1]
        chosen = chosen_row(owner_ref, vectors_ref, buffer)
        add_up(GAIN_SUM, buffer, pull * normed * chosen)
        add_up(SHIFT_SUM, buffer, pull * chosen)
        add_up(QUERY_SUM, buffer, pull * mixed_ref[rows].astype(f32))
        slope = chosen * vectors_ref[4:5]
        grad = (inverse * pull) * (slope - row_mean(slope) - normed * row_mean(slope * normed))
        res_ref[rows] = grad
        grad = grad.astype(bf16)
        low_ref[rows] = grad
        add_up(DOWN_SUM, buffer, grad.astype(f32))
    part = BLOCKS // 4
    wide = units // 4
    for k in range(4):
        span = slice(k * wide, (k + 1) * wide)
        weight = flat(wdown_ref[k * part : (k + 1) * part])
        for buffer in range(buffers):
            rows = rows_of(buffer, length)
            grad = mm_nt(low_ref[rows], weight) * slope_ref[rows, span].astype(f32)
            grad = grad.astype(bf16)
            up_ref[rows, span] = grad
            add_up(UP_SUM, buffer, grad.astype(f32), k * wide)


def up_backward(owner, mixed, normed, sides, slope, vectors, wdown, buffers):
    tokens, width = mixed.shape
    units = slope.shape[1]
    return call(
        functools.partial(up_back_kernel, buffers),
        "up_backward",
        [
            ((tokens, width), bf16),
            ((tokens, units), bf16),
            ((tokens, width), f32),
            ((5 * buffers, units), f32),
        ],
        [SMEM] + [VMEM] * 6,
        [VMEM] * 4,
        (owner, mixed, normed, sides, slope, vectors, wdown),
        2 * tokens * width * units,
        20e6,
    )


def hidden_back_kernel(
    buffers, res_in_ref, up_ref, normed_ref, inverse_ref, vectors_ref, wup_ref, wout_ref,
    res_hbm, attn_ref, context_ref, sums_ref, res_ref, sems,
):
    length = res_ref.shape[0] // buffers
    add_up = adder(sums_ref, buffers)
    stores = []
    weight, weight_out = flat(wup_ref[...]), flat(wout_ref[...])
    for buffer in range(buffers):
        rows = rows_of(buffer, length)
        normed = normed_ref[rows]
        grad = res_in_ref[rows] + mm_nt(up_ref[rows], weight)
        add_up(ATTN_GAIN_SUM, buffer, grad * normed)
        add_up(ATTN_SHIFT_SUM, buffer, grad)
        grad = grad * vectors_ref[1:2]
        grad = inverse_ref[rows, 0:1] * (
            grad - row_mean(grad) - normed * row_mean(grad * normed)
        )
        res_ref[rows] = grad
        span = pl.ds(buffer * length, length)
        stores += fetch([(res_ref.at[span], res_hbm.at[span])], sems, buffer)
        grad = grad.astype(bf16)
        attn_ref[rows] = grad
        add_up(OUT_SUM, buffer, grad.astype(f32))
        context_ref[rows] = mm_nt(grad, weight_out).astype(bf16)
    wait_all(stores)


def hidden_backward(res, up, normed, inverse, vectors, wup, wout, buffers):
    tokens, width = res.shape
    return call(
        functools.partial(hidden_back_kernel, buffers),
        "hidden_backward",
        [
            ((tokens, width), f32),
            ((tokens, width), bf16),
            ((tokens, width), bf16),
            ((3 * buffers, width), f32),
        ],
        [VMEM] * 7,
        [HBM] + [VMEM] * 3,
        (res, up, normed, inverse, vectors, wup, wout),
        2 * tokens * width * (up.shape[1] + width),
        20e6,
        [pltpu.VMEM((tokens, width), f32), pltpu.SemaphoreType.DMA((buffers,))],
    )


def scaled_rows(ref, scale_ref, buffers, span=slice(None)):
    length = ref.shape[0] // buffers
    return jnp.concatenate(
        [
            (ref[rows_of(b, length), span].astype(f32) * scale_ref[b]).astype(bf16)
            for b in range(buffers)
        ]
    )


def place_rows(table_ref, sums_ref, keep_ref, send_ref, start, width):
    rows = keep_ref.shape[1]
    for spot in range(BLOCKS):
        target = keep_ref if spot < HALF else send_ref
        block = pl.ds(pl.multiple_of(table_ref[spot] * rows, 8), rows)
        target[spot % HALF, :, start : start + width] = sums_ref[block, :width].astype(bf16)


def weight_blocks(table_ref, scale_ref, buffers, left_ref, right_ref, keep_ref, send_ref, begin, sums_ref):
    height, columns = left_ref.shape[1], right_ref.shape[1]
    tile = min(height, columns)
    for start in range(0, columns, tile):
        right = scaled_rows(right_ref, scale_ref, buffers, slice(start, start + tile))
        for row in range(0, height, tile):
            sums_ref[row : row + tile] = mm_tn(left_ref[:, row : row + tile], right)
        place_rows(table_ref, sums_ref, keep_ref, send_ref, begin + start, tile)


def weight_kernel(buffers, count, table_ref, scale_ref, *refs):
    pairs = [refs[2 * k : 2 * k + 2] for k in range(count)]
    keep_ref, send_ref, sums_ref = refs[2 * count :]
    begin = 0
    for left_ref, right_ref in pairs:
        weight_blocks(
            table_ref, scale_ref, buffers, left_ref, right_ref, keep_ref, send_ref, begin, sums_ref
        )
        begin += right_ref.shape[1]


def weight_gradient(name, table, scale, pairs, buffers):
    tokens, height = pairs[0][0].shape
    columns = [right.shape[1] for _, right in pairs]
    operands = [part for pair in pairs for part in pair]
    return call(
        functools.partial(weight_kernel, buffers, len(pairs)),
        name,
        [((HALF, height // BLOCKS, sum(columns)), bf16)] * 2,
        [SMEM, SMEM] + [VMEM] * len(operands),
        [VMEM] * 2,
        (table, scale, *operands),
        2 * tokens * height * sum(columns),
        10e6,
        [pltpu.VMEM((height, min(height, columns[0])), f32)],
        limit=LIMIT + 4 if height > 768 else LIMIT,
    )


def small_columns(
    buffers, count, scale_ref, owner_ref, sums_ref, attn_sums_ref, pre_ref, rows_ref, columns_ref, small_ref
):
    width = rows_ref.shape[1]
    rows = width // BLOCKS

    def weigh(ref, kind, columns=width):
        first = kind * buffers
        return sum(ref[first + b : first + b + 1, :columns] * scale_ref[b] for b in range(buffers))

    rows_ref[...] = jnp.zeros_like(rows_ref)
    kinds = [(attn_sums_ref, kind) for kind in (OUT_SUM, ATTN_GAIN_SUM, ATTN_SHIFT_SUM)]
    kinds += [(sums_ref, kind) for kind in (DOWN_SUM, GAIN_SUM, SHIFT_SUM)]
    for k, (ref, kind) in enumerate(kinds):
        rows_ref[k : k + 1] = weigh(ref, kind)
    pre = sum(pre_ref[b : b + 1] * scale_ref[b] for b in range(buffers))
    for at, total in ((QKV_AT, pre), (UP_AT, weigh(sums_ref, UP_SUM, sums_ref.shape[1]))):
        for k in range(total.shape[1] // width):
            rows_ref[at + k : at + k + 1] = total[:, k * width : (k + 1) * width]
    query = lax.broadcasted_iota(jnp.int32, (count, width), 0)
    total = jnp.zeros((count, width), f32)
    for b in range(buffers):
        row = QUERY_SUM * buffers + b
        mine = sums_ref[row : row + 1, :width] * scale_ref[b]
        total += jnp.where(query == owner_ref[b], mine, 0.0)
    rows_ref[QUERY_AT : QUERY_AT + count] = total
    columns_ref[...] = rows_ref[...].T
    lane = lax.broadcasted_iota(jnp.int32, (rows, LINE), 1)
    for block in range(BLOCKS):
        value = columns_ref[block * rows : (block + 1) * rows]
        for at, per in ((QKV_AT, 2), (UP_AT, 4)):
            for c in range(per):
                spot = (block * per + c) * rows
                source = columns_ref[spot % width : spot % width + rows]
                shift = (c - spot // width) % LINE
                if shift:
                    source = pltpu.roll(source, shift, 1)
                value = jnp.where(lane == at + c, source, value)
        small_ref[block * rows : (block + 1) * rows] = value


def attention_back_kernel(
    buffers, count, table_ref, scale_ref, owner_ref, qkv_ref, lse_ref, grad_ref, x_ref,
    sums_in_ref, attn_sums_ref, pre_hbm, keep_ref, send_ref, bias_ref,
    pre_ref, sums_ref, rows_ref, columns_ref, small_ref, sems,
):
    tokens, width = grad_ref.shape
    length, pairs = tokens // buffers, width // PAIR
    scale = 1.0 / math.sqrt(HEAD)

    def step(index, carry):
        rows = pl.ds(pl.multiple_of(index // pairs * length, length), length)
        lane = pl.multiple_of(index % pairs * PAIR, PAIR)
        query = qkv_ref[rows, pl.ds(lane, PAIR)]
        key = qkv_ref[rows, pl.ds(lane + width, PAIR)]
        value = qkv_ref[rows, pl.ds(lane + 2 * width, PAIR)]
        low = head_masks(query.shape)
        query = stacked(query, low)
        grad = stacked(grad_ref[rows, pl.ds(lane, PAIR)], low)
        probs = jnp.exp(mm_nt(key, query) * scale - lse_ref[index])
        grad_probs = mm_nt(value, grad)
        cross = jnp.sum(grad_probs * probs, axis=0, keepdims=True)
        grad_scores = (probs * (grad_probs - cross)).astype(bf16)
        grad_value = mm(probs.astype(bf16), grad)
        grad_key = mm(grad_scores, query) * scale
        grad_query = unstacked(mm_tn(key, grad_scores).T, low, length) * scale
        pre_ref[rows, pl.ds(lane, PAIR)] = grad_query.astype(bf16)
        pre_ref[rows, pl.ds(lane + width, PAIR)] = grad_key.astype(bf16)
        pre_ref[rows, pl.ds(lane + 2 * width, PAIR)] = grad_value.astype(bf16)
        return carry

    lax.fori_loop(0, buffers * pairs, step, 0, unroll=4)
    for buffer in range(buffers):
        rows = rows_of(buffer, length)
        for start, source in ((0, 0), (width, 2 * width)):
            piece = pre_ref[rows, source : source + width].astype(f32)
            bias_ref[buffer : buffer + 1, start : start + width] = jnp.sum(
                piece, axis=0, keepdims=True
            )
    stores = fetch([(pre_ref, pre_hbm)], sems)
    halves = keep_ref, send_ref
    weight_blocks(table_ref, scale_ref, buffers, x_ref, pre_ref, *halves, 0, sums_ref)
    small_columns(
        buffers, count, scale_ref, owner_ref, sums_in_ref, attn_sums_ref, bias_ref,
        rows_ref, columns_ref, small_ref,
    )
    place_rows(table_ref, small_ref, *halves, 3 * width, LINE)
    wait_all(stores)


def attention_gradient(table, scale, owner, count, qkv, lse, grad, x, sums, attn_sums, buffers):
    tokens, width = grad.shape
    length = tokens // buffers
    blocks = ((HALF, width // BLOCKS, 3 * width + LINE), bf16)
    return call(
        functools.partial(attention_back_kernel, buffers, count),
        "attention_gradient",
        [((tokens, 3 * width), bf16), blocks, blocks, ((buffers, 2 * width), f32)],
        [SMEM] * 3 + [VMEM] * 6,
        [HBM] + [VMEM] * 3,
        (table, scale, owner, qkv, lse, grad, x, sums, attn_sums),
        10 * tokens * length * width + 6 * tokens * width * width,
        20e6,
        [
            pltpu.VMEM((tokens, 3 * width), bf16),
            pltpu.VMEM((width, width), f32),
            pltpu.VMEM((LINE, width), f32),
            pltpu.VMEM((width, LINE), f32),
            pltpu.VMEM((width, LINE), f32),
            pltpu.SemaphoreType.DMA((1,)),
        ],
        exps=tokens * length * width // HEAD,
        limit=16,
    )


def states_kernel(
    buffers, scale_ref, res_hbm, pre_hbm, weight_hbm, out_hbm, res_ref, pre_ref, weight_ref, out_ref, sems
):
    length = res_ref.shape[0] // buffers
    spans = [pl.ds(b * length, length) for b in range(buffers)]
    loads = fetch([(weight_hbm, weight_ref)], sems)
    for b, span in enumerate(spans):
        pairs = [(pre_hbm.at[span], pre_ref.at[span]), (res_hbm.at[span], res_ref.at[span])]
        loads += fetch(pairs, sems, 1 + 2 * b)
    stores = []
    for b, span in enumerate(spans):
        wait_all(loads[:3] if b == 0 else loads[1 + 2 * b : 3 + 2 * b])
        grad = res_ref[span] + mm_nt(pre_ref[span], flat(weight_ref[...]))
        out_ref[span] = (grad * scale_ref[b]).astype(bf16)
        stores += fetch([(out_ref.at[span], out_hbm.at[span])], sems, 1 + 2 * buffers + b)
    wait_all(stores)


def states_gradient(scale, res, pre, weight, buffers):
    tokens, width = res.shape
    return call(
        functools.partial(states_kernel, buffers),
        "states_gradient",
        [((tokens, width), bf16)],
        [SMEM] + [HBM] * 3,
        [HBM],
        (scale, res, pre, weight),
        6 * tokens * width * width,
        8e6,
        [
            pltpu.VMEM(res.shape, f32),
            pltpu.VMEM(pre.shape, bf16),
            pltpu.VMEM(weight.shape, bf16),
            pltpu.VMEM(res.shape, bf16),
            pltpu.SemaphoreType.DMA((1 + 3 * buffers,)),
        ],
        limit=16,
    )[0]


def body(
    slot_states, answer_tags, slot_mask, retrieval, query_emb, qkv_weight, qkv_bias, out_weight,
    out_bias, attn_gain, attn_shift, up_weight, up_bias, down_weight, down_bias, ffn_gain, ffn_shift,
):
    group_count = lax.axis_size(AXES)
    device_index = lax.axis_index(AXES)
    tuned = group_count == BLOCKS
    buffers, length, width = slot_states.shape
    query_count, slot_count = slot_mask.shape
    tokens = buffers * length
    x = slot_states.reshape(tokens, width)

    running = jnp.cumsum(slot_mask.reshape(-1), dtype=jnp.int32)
    slot_ranks = jnp.arange(buffers, dtype=jnp.int32) * group_count + device_index
    places = jnp.sum(
        (running[None, :] <= slot_ranks[:, None]).astype(jnp.int32), axis=1, dtype=jnp.int32
    )
    slot_pick = places[:, None] == jnp.arange(query_count * slot_count, dtype=jnp.int32)[None, :]
    owner = places // slot_count
    owner_mask = owner[:, None] == jnp.arange(query_count, dtype=jnp.int32)[None]
    prior_score = jnp.sum(jnp.where(slot_pick, retrieval.reshape(-1)[None, :], 0.0), axis=1)

    order = Order(tuned)
    if tuned:
        table = position_table(device_index)
        vectors = (out_bias, attn_gain, attn_shift, down_bias, ffn_gain, ffn_shift)
        g1 = Gather(order, pack_first(qkv_weight, vectors, qkv_bias, up_bias, query_emb))
        g2 = Gather(order, jnp.concatenate([out_weight, up_weight], axis=1)[None])
        g3 = Gather(order, down_weight[None])
        g1.start_line()
        g1.join_line()
        g1.start_near()
        g2.start_line(g1.held)
        g1.join_near()
        g1.start_other(g1.near, owner, prior_score)
        g2.join_line()
        g2.start_near()
        g2.start_other()
        g1.join_last()
        g3.start_line(g2.held)
        g1.join_other()
        first = g1.pieces()
        vectors, bias, up_bias_all = unpack_small(table, first, 3 * width, query_count)
        order.mark(vectors)
    else:
        table = jnp.arange(BLOCKS, dtype=jnp.int32)
        everything = lambda part: lax.all_gather(part, AXES, axis=0, tiled=True).astype(f32)
        first = gather_plain(qkv_weight)
        second = gather_plain(jnp.concatenate([out_weight, up_weight], axis=1))
        third = gather_plain(down_weight)
        vectors = jnp.stack(
            [
                everything(part)
                for part in (out_bias, attn_gain, attn_shift, down_bias, ffn_gain, ffn_shift)
            ]
        )
        bias = everything(qkv_bias)
        bias = jnp.concatenate([bias[:width], jnp.zeros((width,), f32), bias[width:]]).reshape(1, -1)
        up_bias_all = everything(up_bias).reshape(1, -1)
        query_table = lax.all_gather(query_emb, AXES, axis=1, tiled=True).astype(f32)
        vectors = jnp.concatenate([vectors, jnp.zeros((VECTORS - SIX, width), f32), query_table])

    qkv, wqkv = qkv_forward(table, order.place(x), bias, first)
    if tuned:
        order.mark(qkv)
        g3.join_line()
        g3.start_near()
        g2.join_near()
    context, lse = attention_forward(order.place(qkv), buffers)
    if tuned:
        order.mark(context)
        g3.start_other(order.last)
        g2.join_other()
        g3.join_near()
        g2.join_last()
        second = g2.pieces()
    hidden, act, slope, normed, inverse, wout, wup = up_forward(
        table, x, context, vectors, up_bias_all, second
    )
    if tuned:
        order.mark(act)
        g3.join_other()
        g3.join_last()
        third = g3.pieces()
    mixed, like, normed_out, sides, wdown, mixed_out = down_forward(
        table, owner, hidden, act, vectors, answer_tags, third, buffers
    )

    scores = like[:, 0] + prior_score
    masked = jnp.where(owner_mask, scores[:, None], neg_fill)
    local_peak = jnp.max(masked, axis=0)
    local_total = jnp.sum(jnp.where(owner_mask, jnp.exp(masked - local_peak[None, :]), 0.0), axis=0)
    merged = (local_peak, local_total)
    if tuned:
        order.mark(local_total)
        merged = merge_join(order, merged, merge_start(merged, (CORE_BIT,)))
        got = merge_start(merged, LINE_MASKS)
    else:
        merged = merge_plain(merged)

    grad_low, grad_up, grad_res, sums = up_backward(
        owner, order.place(mixed), normed_out, sides, slope, vectors, wdown, buffers
    )
    if tuned:
        order.mark(grad_low)
        merged = merge_join(order, merged, got)
        got = merge_start(merged, (X_BIT, Y_BIT, X_BIT | Y_BIT))
    grad_hidden, grad_attn, grad_context, attn_sums = hidden_backward(
        order.place(grad_res), grad_up, normed, inverse, vectors, wup, wout, buffers
    )
    if tuned:
        order.mark(grad_attn)
        merged = merge_join(order, merged, got)
    totals = merged[0] + jnp.log(merged[1])
    scale = jnp.sum(
        jnp.where(owner_mask, jnp.exp(scores[:, None] - totals[None, :]), 0.0), axis=1
    )

    pairs = [(context, grad_attn), (hidden, grad_up)]
    halves2 = weight_gradient("up_gradient", table, scale, pairs, buffers)
    if tuned:
        order.mark(halves2[1])
        s2 = Scatter(order, *halves2)
        s2.start_core()
    pairs = [(order.place(act), grad_low)]
    halves3 = weight_gradient("down_gradient", table, scale, pairs, buffers)
    if tuned:
        order.mark(halves3[1])
        s3 = Scatter(order, *halves3)
        s3.start_core()
        s2.join_core()
        s2.start_other()
    grad_pre, *halves1, pre_sums = attention_gradient(
        table, scale, owner, query_count, qkv, lse, order.place(grad_context), x, sums, attn_sums, buffers
    )
    if tuned:
        order.mark(halves1[1])
        s1 = Scatter(order, *halves1)
        s1.start_core()
        s2.join_last()
        s3.join_core()
    states = states_gradient(scale, grad_hidden, order.place(grad_pre), wqkv, buffers)
    if tuned:
        order.mark(states)
        s3.start_other(order.last)
        s2.join_sides()
        s1.join_core()
        s3.join_last()
        s1.join_last()
        s1.start_other(order.last)
        s3.join_sides()
        second_grad = s2.finish(0, width), s2.finish(width)
        order.mark(second_grad[1])
        s1.join_sides()
        third_grad = s3.finish()
        order.mark(third_grad)
        totals = order.place(totals)
        first_grad, *six, qkv_bias_sum, up_bias_sum, query_sum = split_first(
            s1.own, [order.place(part) for part in s1.line], query_count
        )
    else:
        third_grad = scatter_plain(*halves3)
        cut = lambda halves, start, end: scatter_plain(*(half[:, :, start:end] for half in halves))
        second_grad = cut(halves2, 0, width), cut(halves2, width, width + up_weight.shape[1])
        first_grad = cut(halves1, 0, 3 * width)
    if not tuned:
        weigh = lambda part: jnp.sum(scale[:, None] * part, axis=0)
        mine = lambda part: lax.psum_scatter(weigh(part), AXES, scatter_dimension=0, tiled=True)
        rows_for = lambda part, kind: part[kind * buffers : (kind + 1) * buffers, :width]
        six = [mine(rows_for(attn_sums, kind)) for kind in (OUT_SUM, ATTN_GAIN_SUM, ATTN_SHIFT_SUM)]
        six += [mine(rows_for(sums, kind)) for kind in (DOWN_SUM, GAIN_SUM, SHIFT_SUM)]
        qkv_bias_sum, up_bias_sum = mine(pre_sums), mine(sums[:buffers])
        weighed = jnp.where(owner_mask, scale[:, None], 0.0)
        query_sum = jnp.sum(weighed[:, :, None] * rows_for(sums, QUERY_SUM)[:, None, :], axis=0)
        query_sum = lax.psum_scatter(query_sum, AXES, scatter_dimension=1, tiled=True)
    loss = -jnp.sum(totals)
    return (
        mixed_out.reshape(slot_states.shape),
        loss,
        states.reshape(slot_states.shape),
        query_sum,
        first_grad,
        qkv_bias_sum,
        second_grad[0],
        six[0],
        six[1],
        six[2],
        second_grad[1],
        up_bias_sum,
        third_grad,
        six[3],
        six[4],
        six[5],
    )


def solution(mesh):
    split = P(AXES)
    in_specs = (split, split, P(), P(), P(None, AXES)) + (split,) * 12
    out_specs = (split, P(), split, P(None, AXES)) + (split,) * 12
    return jax.shard_map(body, mesh=mesh, in_specs=in_specs, out_specs=out_specs, check_vma=False)
```
